32 devices in a mesh: rep: 4 (over x, core), ep: 8 (over z, y).
Axes of the slice: x: 2, y: 2, z: 4, core: 2. Of those that a mesh axis runs over, the one named last changes fastest.
Arguments:
- tokens: bfloat16 [8192, 1536], P(('rep', 'ep')), may hold values from -6 to 6
- segments: int32 [32, 256], P(('rep', 'ep')), may hold values from 0 to 7, never falling along the last dimension, each value on 1 to 128 neighbouring positions
- routes: int32 [8192, 4], P(('rep', 'ep')), may hold values from 0 to 7, all different within a row; in each aligned block of 256 rows (0 to 255, 256 to 511, ...) at most 192 rows name the same one
- valid_mask: int32 [32, 256], P(('rep', 'ep')), may hold values from 0 to 1, as said below
- teacher: bfloat16 [8192, 1536], P(('rep', 'ep')), may hold values from -6 to 6
- gain_one: bfloat16 [1536], replicated, may hold values from 0.5 to 1.5
- w_query: bfloat16 [1536, 1536], replicated, may hold values from -0.15625 to 0.15625
- w_key: bfloat16 [1536, 256], replicated, may hold values from -0.15625 to 0.15625
- w_value: bfloat16 [1536, 256], replicated, may hold values from -0.15625 to 0.15625
- w_out: bfloat16 [1536, 1536], replicated, may hold values from -0.4375 to 0.4375
- gain_two: bfloat16 [1536], replicated, may hold values from 0.5 to 1.5
- router: bfloat16 [1536, 8], replicated, may hold values from -0.078125 to 0.078125
- w_gate: bfloat16 [8, 1536, 768], P('ep'), may hold values from -0.15625 to 0.15625
- w_up: bfloat16 [8, 1536, 768], P('ep'), may hold values from -0.15625 to 0.15625
- w_down: bfloat16 [8, 768, 1536], P('ep'), may hold values from -0.4375 to 0.4375
Outputs:
- output: bfloat16 [8192, 1536], P(('rep', 'ep'))
- loss_value: float32 [], replicated
- grad_tokens: float32 [8192, 1536], P(('rep', 'ep'))
- grad_gain_one: float32 [1536], replicated
- grad_w_query: float32 [1536, 1536], P('ep')
- grad_w_key: float32 [1536, 256], P('ep')
- grad_w_value: float32 [1536, 256], P('ep')
- grad_w_out: float32 [1536, 1536], P('ep')
- grad_gain_two: float32 [1536], replicated
- grad_router: float32 [1536, 8], replicated
- grad_w_gate: float32 [8, 1536, 768], P('ep', 'rep')
- grad_w_up: float32 [8, 1536, 768], P('ep', 'rep')
- grad_w_down: float32 [8, 768, 1536], P('ep', 'rep')
The draws below stay inside these ranges and needn't reach their ends.
Inputs may be any that keep to these rules, and one draw needn't show every extreme that they name: `segments`: segment numbers never fall along a sequence. `routes`: among the 256 rows of one device no expert is named more than 192 times; a token names 4 different experts. `valid_mask`: the first token of every sequence is valid.
All inputs are finite; a program needn't handle non-finite values.
Results may differ from the reference program's by a relative error of at most 0.018.
Values may be sent and summed in bfloat16 or wider, within the bound.
No kernel may reach another device: no remote copies, remote signals or barrier semaphores. Data moves between devices by JAX's collectives and lax.ppermute only.
A program may use at most 192 MiB of HBM per device.

```python
import math
import jax
import jax.numpy as jnp
import numpy as np
from jax import lax

D = 1536
H = 12
KVH = 2
HEAD = 128
MOE_FF = 768
TOP = 4
TOK_DEV = 256
DOCS = 8
EXPERTS = 8
CAP = 192
QW = 1536
KVW = 256
SEQS = 32
TOKENS = 8192
N_REP = 4
N_EP = 8


def draw_teacher(key, part):
    device_count = TOKENS // TOK_DEV
    row_device = (jnp.arange(TOKENS, dtype=jnp.int32) // TOK_DEV).astype(jnp.float32)
    device_share = row_device / max(device_count - 1, 1)
    scales = 0.5 + 2.5 * device_share
    values = jax.random.truncated_normal(key, -2.0, 2.0, (TOKENS, D), jnp.float32) * scales[:, None]
    return values.astype(jnp.bfloat16)


def draw_valid_mask(key, part):
    seq_ids = jnp.arange(SEQS, dtype=jnp.int32)[:, None]
    limits = 300 + 600 * seq_ids // max(SEQS - 1, 1)
    dice_rolls = jax.random.randint(key, (SEQS, TOK_DEV), 0, 1000, dtype=jnp.int32)
    first_token = jnp.arange(TOK_DEV, dtype=jnp.int32)[None, :] == 0
    return jnp.where((dice_rolls < limits) | first_token, 1, 0).astype(jnp.int32)


def block_scale(own_key, shape, split, smallest, high):
    level, own = 1.0, jax.random.fold_in(own_key, 6)
    for position, parts in split:
        heights = jnp.exp(jax.random.uniform(jax.random.fold_in(own, position), (parts,), jnp.float32, smallest / len(split), high / len(split)))
        level = level * jnp.repeat(heights, shape[position] // parts).reshape([-1 if axis == position else 1 for axis in range(len(shape))])
    return level


def length_profile(amount, total, limit, slope):
    loads = [(1 << 20) // math.isqrt(grade ** slope) + 1 for grade in range(2, amount + 1)]
    surplus, holding = total - limit - (amount - 1), [1] * (amount - 1)
    while surplus > 0:
        candidates = [i for i in range(amount - 1) if holding[i] < limit]
        whole, budget = sum([loads[i] for i in candidates]), surplus
        for i in candidates:
            addition = min(limit - holding[i], max(1, budget * loads[i] // whole), surplus)
            holding[i] = holding[i] + addition
            surplus = surplus - addition
    return np.array([limit] + holding)


def ragged_sizes(stream_key, amount, total, most, slope):
    if amount == 2:
        one = jax.random.randint(stream_key, (), max(1, total - most), min(most, total - 1) + 1)
        return jnp.stack([one, total - one])
    tallies = jnp.asarray(length_profile(amount, total, most, slope), jnp.int32)
    couples = (amount - 1) // 2
    source_of, sink = tallies[1:1 + 2 * couples:2], tallies[2:2 + 2 * couples:2]
    room = jnp.minimum(source_of - 1, most - sink)
    moved = jax.random.randint(jax.random.fold_in(stream_key, 1), (couples,), 0, 1 << 20) % (room + 1)
    tallies = tallies.at[1:1 + 2 * couples:2].set(source_of - moved).at[2:2 + 2 * couples:2].set(sink + moved)
    return tallies[jax.random.permutation(jax.random.fold_in(stream_key, 2), amount)]


def routed_block(key, own, number, rows, amount, top, limit, lean):
    sequence = jax.random.permutation(key, amount)
    heavy_load, common = portions_of(amount, rows * top, limit, lean, True), portions_of(amount, rows * top, limit, lean, False)
    places = jnp.arange(amount)

    def named(tallies, offset_by):
        used = int((tallies > 0).sum())
        fixed = max(1, used // 4)
        shifted = fixed + (places - fixed + offset_by * (used - fixed)) % max(1, amount - fixed)
        return jnp.zeros((amount,), jnp.int32).at[sequence[jnp.where(places < fixed, places, shifted)]].set(jnp.asarray(tallies, jnp.int32))

    tallies = jnp.where(number % 4 == 0, named(heavy_load, number // 4), named(common, number - number // 4 - 1))
    mixed = jax.random.permutation(jax.random.fold_in(own, 3), amount)
    giver, taker = mixed[0:amount // 2 * 2:2], mixed[1:amount // 2 * 2:2]
    slack = jnp.minimum(tallies[giver] - 1, limit - tallies[taker]) // 2
    slack = jnp.where((giver == sequence[0]) | (taker == sequence[0]) | (tallies[taker] == 0), 0, jnp.maximum(slack, 0))
    shifted = jax.random.randint(jax.random.fold_in(own, 4), (amount // 2,), 0, 1 << 20) % (slack + 1)
    tallies = tallies.at[giver].add(-shifted).at[taker].add(shifted)
    members = jnp.searchsorted(jnp.cumsum(tallies), jnp.arange(rows * top), side="right").astype(jnp.int32)
    grid = members.reshape(top, rows).T
    grid = grid[jax.random.permutation(jax.random.fold_in(own, 1), rows)]
    offset_by = jax.random.randint(jax.random.fold_in(own, 2), (rows, 1), 0, top)
    return jnp.take_along_axis(grid, (jnp.arange(top)[None, :] + offset_by) % top, axis=1)


def portions_of(amount, total, most, slope, full):
    weights = [(1 << 20) // math.isqrt(standing ** slope) + 1 for standing in range(1, amount + 1)]
    largest = most if full else min(most, max(-(-total // amount), total * weights[0] // sum(weights)))
    least = 1 if total - largest >= amount - 1 else 0
    counts, spare = [largest] + [least] * (amount - 1), total - largest - least * (amount - 1)
    while spare > 0:
        movable = [i for i in range(1, amount) if counts[i] < largest] or [i for i in range(1, amount) if counts[i] < most]
        pool, budget = sum([weights[i] for i in movable]), spare
        for i in movable:
            extra = min(most - counts[i], max(1, budget * weights[i] // pool), spare)
            counts[i] = counts[i] + extra
            spare = spare - extra
    return np.array(counts)


def centred(key, dims, scale, reach, split=(), kind=jnp.bfloat16):
    array = scale * jax.random.normal(key, dims, jnp.float32)
    if split:
        array = array * block_scale(key, dims, split, -0.22, 0.18)
    return jnp.clip(array, -reach, reach).astype(kind)


def setup_inputs(seed: int = 0) -> dict:
    keys = jax.random.split(jax.random.key(seed), 16)
    tokens = centred(keys[0], (TOKENS, D), 1.0, 6.0, ((0, 32),))
    segments = jax.vmap(lambda own: jnp.searchsorted(jnp.cumsum(ragged_sizes(own, DOCS, TOK_DEV, TOK_DEV // 2, 2)), jnp.arange(TOK_DEV), side="right"))(jax.random.split(keys[1], SEQS)).reshape((SEQS, TOK_DEV)).astype(jnp.int32)
    routes_keys = jax.random.split(jax.random.fold_in(keys[2], 1), TOKENS // TOK_DEV)
    routes_turns = jax.random.permutation(jax.random.fold_in(keys[2], 3), TOKENS // TOK_DEV)
    routes = jax.vmap(lambda own, number: routed_block(jax.random.fold_in(keys[2], 2), own, number, TOK_DEV, EXPERTS, TOP, CAP, 1))(routes_keys, routes_turns).reshape((TOKENS, TOP))
    valid_mask = draw_valid_mask(jax.random.fold_in(keys[15], 71), 0)
    teacher = draw_teacher(jax.random.fold_in(keys[15], 71), 0)
    gain_one = jnp.clip(1.0 + 0.1 * jax.random.normal(keys[5], (D,), jnp.float32), 0.5, 1.5).astype(jnp.bfloat16)
    w_query = centred(keys[6], (D, QW), D ** -0.5, 0.15625)
    w_key = centred(keys[7], (D, KVW), D ** -0.5, 0.15625)
    w_value = centred(keys[8], (D, KVW), D ** -0.5, 0.15625)
    w_out = centred(keys[9], (QW, D), (QW // 8) ** -0.5, 0.4375)
    gain_two = jnp.clip(1.0 + 0.1 * jax.random.normal(keys[10], (D,), jnp.float32), 0.5, 1.5).astype(jnp.bfloat16)
    router = centred(keys[11], (D, EXPERTS), (4 * D) ** -0.5, 0.078125)
    w_gate = centred(keys[12], (EXPERTS, D, MOE_FF), D ** -0.5, 0.15625, ((0, 8),))
    w_up = centred(keys[13], (EXPERTS, D, MOE_FF), D ** -0.5, 0.15625, ((0, 8),))
    w_down = centred(keys[14], (EXPERTS, MOE_FF, D), (MOE_FF // 4) ** -0.5, 0.4375, ((0, 8),))
    return {"tokens": tokens, "segments": segments, "routes": routes, "valid_mask": valid_mask, "teacher": teacher, "gain_one": gain_one, "w_query": w_query, "w_key": w_key, "w_value": w_value, "w_out": w_out, "gain_two": gain_two, "router": router, "w_gate": w_gate, "w_up": w_up, "w_down": w_down}


EPSILON = 1e-06
ROPE_BASE = 10000.0
NEG_FILL = -1e+30
HIGHEST = lax.Precision.HIGHEST

@jax.custom_vjp
def low(v):
    return lax.optimization_barrier(v.astype(jnp.bfloat16)).astype(jnp.float32)

@jax.custom_vjp
def low_back(v):
    return v

def low_keep(v):
    return (low(v), None)

def low_pass(kept, grad):
    return (grad,)

def back_keep(v):
    return (v, None)

def back_low(kept, grad):
    return (low(grad),)
low.defvjp(low_keep, low_pass)
low_back.defvjp(back_keep, back_low)

def rms_norm(values, gain):
    inverse = lax.rsqrt(lax.optimization_barrier(jnp.mean(values * values, axis=-1, keepdims=True)) + EPSILON)
    return values * inverse * gain

def rotate(values, direction):
    length = values.shape[-3]
    half_dim = values.shape[-1] // 2
    frequency = ROPE_BASE ** (-jnp.arange(half_dim, dtype=jnp.float32) / half_dim)
    angles = jnp.arange(length, dtype=jnp.float32)[:, None] * frequency[None, :] * direction
    cosine = jnp.cos(angles)[:, None, :]
    sinusoid = jnp.sin(angles)[:, None, :]
    first_half = values[..., :half_dim]
    second_half = values[..., half_dim:]
    return jnp.concatenate([first_half * cosine - second_half * sinusoid, second_half * cosine + first_half * sinusoid], axis=-1)

def attention_block(attn_params, x_block, seg_block):
    gain_one, w_query, w_key, w_value, w_out = attn_params
    seq_count = x_block.shape[0]
    length = x_block.shape[1]
    groups = H // KVH
    normed = low(rms_norm(x_block, gain_one))
    queries = low_back(jnp.einsum('bsd,de->bse', normed, w_query, precision=HIGHEST)).reshape(seq_count, length, H, HEAD)
    key_pre = low_back(jnp.einsum('bsd,de->bse', normed, w_key, precision=HIGHEST)).reshape(seq_count, length, KVH, HEAD)
    value_rows = low_back(low(jnp.einsum('bsd,de->bse', normed, w_value, precision=HIGHEST))).reshape(seq_count, length, KVH, HEAD)
    query_rot = low(rotate(queries, 1.0)).reshape(seq_count, length, KVH, groups, HEAD)
    key_rot = low(rotate(key_pre, 1.0))
    raw_scores = jnp.einsum('bqkgc,bpkc->bkgqp', query_rot, key_rot, precision=HIGHEST)
    scores = low_back(raw_scores * HEAD ** (-0.5))
    places = jnp.arange(length)
    allowed = (seg_block[:, :, None] == seg_block[:, None, :]) & (places[:, None] >= places[None, :])[None]
    scores = jnp.where(allowed[:, None, None, :, :], scores, NEG_FILL)
    row_peak = lax.optimization_barrier(jnp.max(scores, axis=-1, keepdims=True))
    exp_terms = jnp.exp(scores - row_peak)
    attn_weights = low(exp_terms / lax.optimization_barrier(jnp.sum(exp_terms, axis=-1, keepdims=True)))
    context = jnp.einsum('bkgqp,bpkc->bqkgc', attn_weights, value_rows, precision=HIGHEST)
    context = low_back(low(context.reshape(seq_count, length, H * HEAD)))
    branch = low_back(jnp.einsum('bse,ed->bsd', context, w_out, precision=HIGHEST))
    return x_block + branch

def expert_apply(expert_inputs, padded_in):
    w_gate_one, w_up_one, w_down_one, slot_token = expert_inputs
    slot_rows = low_back(padded_in[slot_token])
    gate_pre = low_back(jnp.dot(slot_rows, w_gate_one, precision=HIGHEST))
    up_pre = low_back(jnp.dot(slot_rows, w_up_one, precision=HIGHEST))
    hidden = low(jax.nn.gelu(gate_pre, approximate=True) * up_pre)
    return low_back(low(jnp.dot(hidden, w_down_one, precision=HIGHEST)))

def slot_plan(route_group):
    route_rows = route_group.reshape(N_EP, TOK_DEV * TOP)
    onehot = (route_rows[:, :, None] == jnp.arange(EXPERTS, dtype=jnp.int32)[None, None, :]).astype(jnp.int32)
    slot_rank = lax.optimization_barrier(jnp.sum((jnp.cumsum(onehot, axis=1) - 1) * onehot, axis=2))
    source = jnp.arange(N_EP, dtype=jnp.int32)[:, None]
    slot_id = route_rows * (N_EP * CAP) + source * CAP + slot_rank
    token_of = source * TOK_DEV + jnp.arange(TOK_DEV * TOP, dtype=jnp.int32)[None, :] // TOP
    slot_token = jnp.full((EXPERTS * N_EP * CAP,), N_EP * TOK_DEV, jnp.int32).at[slot_id.reshape(-1)].set(token_of.reshape(-1).astype(jnp.int32))
    return (slot_id.reshape(N_EP * TOK_DEV, TOP).astype(jnp.int32), slot_token)

def group_forward(params, x_group, seg_group, route_group, valid_group, teacher_group):
    gain_one, w_query, w_key, w_value, w_out, gain_two, router, w_gate, w_up, w_down = params
    per_block = math.gcd(N_EP, max(1, 4096 // TOK_DEV))
    block_count = N_EP // per_block
    checked_attention = jax.checkpoint(attention_block)
    attn_params = (gain_one, w_query, w_key, w_value, w_out)

    def attention_step(running, inputs):
        return (running, checked_attention(attn_params, inputs[0], inputs[1]))
    block_inputs = (x_group.reshape(block_count, per_block, TOK_DEV, D), seg_group.reshape(block_count, per_block, TOK_DEV))
    _, mixed_blocks = lax.scan(attention_step, jnp.zeros((), jnp.float32), block_inputs)
    mixed_rows = mixed_blocks.reshape(N_EP * TOK_DEV, D)
    moe_in = low(rms_norm(mixed_rows, gain_two))
    logits = low_back(jnp.dot(moe_in, router, precision=HIGHEST))
    chosen = jnp.take_along_axis(logits, route_group, axis=1)
    chosen_peak = lax.optimization_barrier(jnp.max(chosen, axis=1, keepdims=True))
    gate_terms = jnp.exp(chosen - chosen_peak)
    gate_weights = gate_terms / lax.optimization_barrier(jnp.sum(gate_terms, axis=1, keepdims=True))
    slot_id, slot_token = slot_plan(route_group)
    padded_in = jnp.concatenate([moe_in, jnp.zeros((1, D), moe_in.dtype)], axis=0)
    checked_expert = jax.checkpoint(expert_apply)
    stacked = (w_gate, w_up, w_down, slot_token.reshape(EXPERTS, N_EP * CAP))
    expert_rows = lax.map(lambda expert_inputs: checked_expert(expert_inputs, padded_in), stacked)
    picked = expert_rows.reshape(EXPERTS * N_EP * CAP, D)[slot_id]
    output_rows = mixed_rows + lax.optimization_barrier(jnp.sum(gate_weights[:, :, None] * picked, axis=1))
    residual_gap = output_rows - teacher_group
    numerator = jnp.sum(valid_group * lax.optimization_barrier(jnp.sum(residual_gap * residual_gap, axis=-1)))
    return (output_rows, numerator)

def forward(params, token_values, segments, routes, valid_values, teacher_values):
    checked_group = jax.checkpoint(group_forward)
    group_tokens = N_EP * TOK_DEV

    def group_step(running, inputs):
        out_rows, partial_sum = checked_group(params, inputs[0], inputs[1], inputs[2], inputs[3], inputs[4])
        return (running + partial_sum, out_rows)
    group_inputs = (token_values.reshape(N_REP, group_tokens, D), segments.reshape(N_REP, N_EP, TOK_DEV), routes.reshape(N_REP, group_tokens, TOP), valid_values.reshape(N_REP, group_tokens), teacher_values.reshape(N_REP, group_tokens, D))
    total_sum, outputs = lax.scan(group_step, jnp.zeros((), jnp.float32), group_inputs)
    return (outputs.reshape(N_REP * group_tokens, D), total_sum)

def reference(tokens, segments, routes, valid_mask, teacher, gain_one, w_query, w_key, w_value, w_out, gain_two, router, w_gate, w_up, w_down):
    params = tuple((array_in.astype(jnp.float32) for array_in in (gain_one, w_query, w_key, w_value, w_out, gain_two, router, w_gate, w_up, w_down)))
    valid_values = valid_mask.reshape(TOKENS).astype(jnp.float32)
    count_total = jnp.sum(valid_values)
    teacher_values = teacher.astype(jnp.float32)

    def whole(param_set, token_values):
        return forward(param_set, token_values, segments, routes, valid_values, teacher_values)
    (output_rows, numerator), pullback = jax.vjp(whole, params, tokens.astype(jnp.float32))
    param_grads, grad_tokens = pullback((jnp.zeros_like(output_rows), TOKENS / count_total))
    return (output_rows.astype(jnp.bfloat16), numerator / count_total, grad_tokens, param_grads[0], param_grads[1], param_grads[2], param_grads[3], param_grads[4], param_grads[5], param_grads[6], param_grads[7], param_grads[8], param_grads[9])
```

```python
import functools

import jax
import jax.numpy as jnp
from jax import lax
from jax.sharding import Mesh
from jax.sharding import PartitionSpec as P

H = 12
KVH = 2
HEAD = 128

EPSILON = 1e-06
ROPE_BASE = 10000.0
NEG_FILL = -1e30
ALL = ("x", "c", "z", "y")
EP = ("z", "y")
F32 = jnp.float32
BF16 = jnp.bfloat16
RING_LIMIT = 16


def dot(a, b, dims=((1,), (0,))):
    return lax.dot_general(a, b, (dims, ((), ())), preferred_element_type=F32)


def dot_nt(a, b):
    return dot(a, b, ((1,), (1,)))


def dot_tn(a, b):
    return dot(a, b, ((0,), (0,)))


def rms_norm(values, gain):
    inverse = lax.rsqrt(jnp.mean(values * values, axis=-1, keepdims=True) + EPSILON)
    return values * inverse * gain


def rotate(values, direction):
    length = values.shape[-3]
    half_dim = values.shape[-1] // 2
    frequency = ROPE_BASE ** (-jnp.arange(half_dim, dtype=F32) / half_dim)
    angles = jnp.arange(length, dtype=F32)[:, None] * frequency[None, :] * direction
    cosine = jnp.cos(angles)[:, None, :]
    sinusoid = jnp.sin(angles)[:, None, :]
    first_half = values[..., :half_dim]
    second_half = values[..., half_dim:]
    return jnp.concatenate(
        [
            first_half * cosine - second_half * sinusoid,
            second_half * cosine + first_half * sinusoid,
        ],
        axis=-1,
    )


def activate(gate_pre, up_pre):
    return jax.nn.gelu(gate_pre, approximate=True) * up_pre


class Ring:
    def __init__(self, z_size, y_size):
        cycle = [(z, 0) for z in range(z_size)]
        for step, z in enumerate(reversed(range(z_size))):
            rest = list(range(1, y_size))
            cycle += [(z, y) for y in (rest if step % 2 == 0 else rest[::-1])]
        self.order = [z * y_size + y for z, y in cycle]
        self.size = len(self.order)
        self.half = self.size // 2
        n = self.size
        self.forward = [(self.order[i], self.order[(i + 1) % n]) for i in range(n)]
        self.backward = [(b, a) for a, b in self.forward]
        self.place = [self.order.index(e) for e in range(n)]

    def fwd(self, a):
        return lax.ppermute(a, EP, self.forward)

    def bwd(self, a):
        return lax.ppermute(a, EP, self.backward)

    def owners(self):
        mine = jnp.asarray(self.place, jnp.int32)[lax.axis_index(EP)]
        behind = (mine - jnp.arange(self.size, dtype=jnp.int32)) % self.size
        return jnp.asarray(self.order, jnp.int32)[behind]

    def gather(self, a):
        blocks = [None] * self.size
        blocks[0] = a
        ahead = behind = a
        for s in range(1, self.half):
            ahead = self.fwd(ahead)
            behind = self.bwd(behind)
            blocks[s] = ahead
            blocks[self.size - s] = behind
        rows = a.shape[0] // 2
        blocks[self.half] = jnp.concatenate([self.fwd(ahead[:rows]), self.bwd(behind[rows:])], axis=0)
        return blocks

    def scatter_sum(self, terms):
        far = terms(self.half)
        rows = far.shape[0] // 2
        down = self.bwd(far[:rows])
        up = self.fwd(far[rows:])
        first, last = terms(self.half - 1), terms(self.half + 1)

        def add(a, b):
            return (a.astype(F32) + b.astype(F32)).astype(BF16)

        down = jnp.concatenate([add(first[:rows], down), first[rows:]], axis=0)
        up = jnp.concatenate([last[:rows], add(last[rows:], up)], axis=0)
        for s in range(self.half - 2, 0, -1):
            down = add(self.bwd(down), terms(s))
            up = add(self.fwd(up), terms(self.size - s))
        down = self.bwd(down)
        up = self.fwd(up)
        return down.astype(F32) + up.astype(F32) + terms(0).astype(F32)


def butterfly_sum(a, axes):
    for axis in axes:
        size = lax.axis_size(axis)
        step = 1
        while step < size:
            a = a + lax.ppermute(a, axis, [(i, i ^ step) for i in range(size)])
            step *= 2
    return a


def scatter_axis(a, axis, dim):
    size = lax.axis_size(axis)
    if size != 2:
        return lax.psum_scatter(a, axis, scatter_dimension=dim, tiled=True).astype(F32)
    me = lax.axis_index(axis)
    share = a.shape[dim] // 2
    mine = lax.dynamic_slice_in_dim(a, me * share, share, dim)
    other = lax.dynamic_slice_in_dim(a, (1 - me) * share, share, dim)
    got = lax.ppermute(other, axis, [(0, 1), (1, 0)])
    return mine.astype(F32) + got.astype(F32)


def gather_axis(a, axis, dim):
    size = lax.axis_size(axis)
    if size != 2:
        return lax.all_gather(a, axis, axis=dim, tiled=True)
    got = lax.ppermute(a, axis, [(0, 1), (1, 0)])
    first = lax.axis_index(axis) == 0
    return jnp.concatenate([jnp.where(first, a, got), jnp.where(first, got, a)], axis=dim)


class RingExperts:
    def __init__(self, ring, owners, moe_in, route_hot, gate_weights, top, w_gate, w_up, w_down):
        self.ring, self.owners, self.moe_in = ring, owners, moe_in
        self.weights = (w_gate, w_up, w_down)
        gates = lax.all_to_all(gate_weights.T, EP, 0, 0, tiled=True)
        self.gates = jnp.take(gates, owners, axis=0).T
        n = ring.size
        self.by_distance = sorted(range(n), key=lambda j: min(j, n - j))

    def forward(self):
        w_gate, w_up, w_down = self.weights
        self.rows_in = self.ring.gather(self.moe_in)
        self.gate_pre, self.up_pre, self.hidden = {}, {}, {}

        def term(j):
            gate_pre = dot(self.rows_in[j], w_gate)
            up_pre = dot(self.rows_in[j], w_up)
            self.hidden[j] = activate(gate_pre, up_pre).astype(BF16)
            self.gate_pre[j], self.up_pre[j] = gate_pre.astype(BF16), up_pre.astype(BF16)
            return (dot(self.hidden[j], w_down) * self.gates[:, j : j + 1]).astype(BF16)

        terms = {j: term(j) for j in self.by_distance}
        return self.ring.scatter_sum(terms.get)

    def backward(self, grad_out):
        w_gate, w_up, w_down = self.weights
        grads_in = self.ring.gather(grad_out.astype(BF16))
        gate_lows, up_lows, scaled, dots = {}, {}, {}, {}

        def term(j):
            raw = dot_nt(grads_in[j], w_down)
            hidden = self.hidden[j].astype(F32)
            dots[j] = jnp.sum(raw * hidden, axis=1)
            gate = self.gates[:, j : j + 1]
            _, pull = jax.vjp(activate, self.gate_pre[j].astype(F32), self.up_pre[j].astype(F32))
            grad_gate, grad_up = pull(raw * gate)
            gate_lows[j], up_lows[j] = grad_gate.astype(BF16), grad_up.astype(BF16)
            scaled[j] = (hidden * gate).astype(BF16)
            return (dot_nt(gate_lows[j], w_gate) + dot_nt(up_lows[j], w_up)).astype(BF16)

        terms = {j: term(j) for j in self.by_distance}
        stacked = jnp.stack([dots[j] for j in range(self.ring.size)])
        back = jnp.zeros_like(stacked).at[self.owners].set(stacked)
        grad_gates = lax.all_to_all(back, EP, 0, 0, tiled=True).T
        grad_moe_in = self.ring.scatter_sum(terms.get)

        def joined(parts):
            return jnp.concatenate([parts[j] for j in range(self.ring.size)], axis=0)

        rows_all = joined(self.rows_in)
        expert_grads = [
            dot_tn(rows_all, joined(gate_lows)).astype(BF16),
            dot_tn(rows_all, joined(up_lows)).astype(BF16),
            dot_tn(joined(scaled), joined(grads_in)).astype(BF16),
        ]
        return grad_moe_in, grad_gates, expert_grads


class SlotExperts:
    def __init__(self, ring, owners, moe_in, route_hot, gate_weights, top, w_gate, w_up, w_down):
        rows, experts = route_hot.shape
        self.slots = 3 * rows * top // (2 * experts)
        self.group = ring.size
        self.moe_in, self.weights = moe_in, (w_gate, w_up, w_down)
        places = jnp.arange(rows)
        earlier = (places[:, None] > places[None, :]).astype(BF16)
        rank = dot(earlier, route_hot.astype(BF16)).T[:, None, :]
        slot = jnp.arange(self.slots, dtype=F32)[None, :, None]
        picks = ((rank == slot) & route_hot.T[:, None, :]).reshape(experts * self.slots, rows)
        self.picks = picks.astype(BF16)
        self.slot_gate = jnp.where(picks, jnp.repeat(gate_weights.T, self.slots, axis=0), 0.0)

    def swap(self, rows):
        blocks = rows.reshape(self.group, -1, rows.shape[1])
        return lax.all_to_all(blocks, EP, 0, 0, tiled=True).reshape(rows.shape)

    def forward(self):
        w_gate, w_up, w_down = self.weights
        self.arrived = self.swap(dot(self.picks, self.moe_in).astype(BF16))
        self.gate_pre = dot(self.arrived, w_gate)
        self.up_pre = dot(self.arrived, w_up)
        self.hidden = activate(self.gate_pre, self.up_pre).astype(BF16)
        self.returned = self.swap(dot(self.hidden, w_down).astype(BF16))
        return jnp.dot(self.slot_gate.T, self.returned.astype(F32), precision=lax.Precision.HIGHEST)

    def backward(self, grad_out):
        w_gate, w_up, w_down = self.weights
        grad_low = grad_out.astype(BF16)
        rows, experts = grad_out.shape[0], self.picks.shape[0] // self.slots
        products = dot_nt(grad_low, self.returned) * self.picks.T.astype(F32)
        grad_gates = jnp.sum(products.reshape(rows, experts, self.slots), axis=2)
        slot_gate = jnp.sum(self.slot_gate, axis=1, keepdims=True)
        grads_in = self.swap((dot(self.picks, grad_low) * slot_gate).astype(BF16))
        _, pull = jax.vjp(activate, self.gate_pre, self.up_pre)
        grad_gate, grad_up = pull(dot_nt(grads_in, w_down))
        gate_low, up_low = grad_gate.astype(BF16), grad_up.astype(BF16)
        back = self.swap((dot_nt(gate_low, w_gate) + dot_nt(up_low, w_up)).astype(BF16))
        expert_grads = [
            dot_tn(self.arrived, gate_low).astype(BF16),
            dot_tn(self.arrived, up_low).astype(BF16),
            dot_tn(self.hidden, grads_in).astype(BF16),
        ]
        return dot_tn(self.picks, back), grad_gates, expert_grads


def shards(
    ring,
    tokens,
    segments,
    routes,
    valid_mask,
    teacher,
    gain_one,
    w_query,
    w_key,
    w_value,
    w_out,
    gain_two,
    router,
    w_gate,
    w_up,
    w_down,
):
    length = tokens.shape[0]
    width = tokens.shape[1]
    experts_all = router.shape[1]
    tokens_all = length * lax.axis_size(ALL)
    groups = H // KVH
    score_scale = HEAD ** (-0.5)
    w_gate, w_up, w_down = w_gate[0], w_up[0], w_down[0]
    valid_rows = valid_mask.reshape(length).astype(F32)
    count_total = butterfly_sum(jnp.full((8, 128), jnp.sum(valid_rows), F32), ("c", "x", "y", "z"))[0, 0]
    token_values = tokens.astype(F32)
    normed_one, norm_one_pull = jax.vjp(rms_norm, token_values, gain_one.astype(F32))
    normed_low = normed_one.astype(BF16)
    query_pre = dot(normed_low, w_query).reshape(length, H, HEAD)
    key_pre = dot(normed_low, w_key).reshape(length, KVH, HEAD)
    value_low = dot(normed_low, w_value).astype(BF16).reshape(length, KVH, HEAD)
    query_rot = rotate(query_pre, 1.0).astype(BF16).reshape(length, KVH, groups, HEAD)
    key_rot = rotate(key_pre, 1.0).astype(BF16)
    places = jnp.arange(length)
    seg_row = segments.reshape(length)
    allowed = (seg_row[:, None] == seg_row[None, :]) & (places[:, None] >= places[None, :])

    def masked_scores():
        raw_scores = jnp.einsum("qkgc,pkc->kgqp", query_rot, key_rot, preferred_element_type=F32)
        return jnp.where(allowed, raw_scores * score_scale, NEG_FILL)

    scores = masked_scores()
    row_peak = jnp.max(scores, axis=-1, keepdims=True)
    exp_terms = jnp.exp(scores - row_peak)
    row_total = jnp.sum(exp_terms, axis=-1, keepdims=True)
    log_total = row_peak + jnp.log(row_total)
    weights_low = (exp_terms / row_total).astype(BF16)
    context = jnp.einsum("kgqp,pkc->qkgc", weights_low, value_low, preferred_element_type=F32)
    context = context.reshape(length, H * HEAD).astype(BF16)
    mixed_rows = token_values + dot(context, w_out)
    normed_two, norm_two_pull = jax.vjp(rms_norm, mixed_rows, gain_two.astype(F32))
    moe_in = normed_two.astype(BF16)
    logits = dot(moe_in, router)
    expert_ids = jnp.arange(experts_all, dtype=jnp.int32)
    route_hot = jnp.any(routes[:, :, None] == expert_ids[None, None, :], axis=1)
    peak = jnp.max(jnp.where(route_hot, logits, -jnp.inf), axis=1, keepdims=True)
    gate_terms = jnp.where(route_hot, jnp.exp(jnp.where(route_hot, logits - peak, 0.0)), 0.0)
    gate_weights = gate_terms / jnp.sum(gate_terms, axis=1, keepdims=True)

    owners = ring.owners()
    form = RingExperts if ring.size <= RING_LIMIT else SlotExperts
    experts = form(ring, owners, moe_in, route_hot, gate_weights, routes.shape[1], w_gate, w_up, w_down)
    moe_out = experts.forward()
    output_rows = mixed_rows + moe_out
    residual_gap = output_rows - teacher.astype(F32)
    numerator = jnp.sum(valid_rows * jnp.sum(residual_gap * residual_gap, axis=-1))
    grad_out = 2.0 * tokens_all / count_total * valid_rows[:, None] * residual_gap

    grad_moe_in, grad_gates, expert_grads = experts.backward(grad_out)
    x_size, c_size = lax.axis_size("x"), lax.axis_size("c")
    shares = []
    for g in expert_grads:
        part = g.reshape(x_size, c_size, -1, g.shape[1])
        part = scatter_axis(part, "c", 1).astype(BF16)
        shares.append(scatter_axis(part, "x", 0).reshape(1, -1, g.shape[1]))

    grad_chosen = gate_weights * (grad_gates - jnp.sum(gate_weights * grad_gates, axis=1, keepdims=True))
    grad_logits = grad_chosen.astype(BF16)
    grad_router = dot_tn(moe_in, grad_logits)
    grad_moe_in = grad_moe_in + dot_nt(grad_logits, router)
    grad_norm_two, grad_gain_two = norm_two_pull(grad_moe_in)
    grad_mixed = grad_out + grad_norm_two
    grad_branch = grad_mixed.astype(BF16)
    grad_w_out = dot_tn(context, grad_branch)
    grad_context = dot_nt(grad_branch, w_out)
    grad_context = grad_context.astype(BF16).reshape(length, KVH, groups, HEAD)
    attn_weights = jnp.exp(masked_scores() - log_total)
    grad_weights = jnp.einsum("qkgc,pkc->kgqp", grad_context, value_low, preferred_element_type=F32)
    row_term = jnp.sum(attn_weights * grad_weights, axis=-1, keepdims=True)
    grad_scores = (attn_weights * (grad_weights - row_term)).astype(BF16)
    grad_query_rot = jnp.einsum("kgqp,pkc->qkgc", grad_scores, key_rot, preferred_element_type=F32) * score_scale
    grad_key_rot = jnp.einsum("kgqp,qkgc->pkc", grad_scores, query_rot, preferred_element_type=F32) * score_scale
    grad_value = jnp.einsum("kgqp,qkgc->pkc", attn_weights.astype(BF16), grad_context, preferred_element_type=F32)
    grad_value = grad_value.astype(BF16).reshape(length, KVH * HEAD)
    grad_query = rotate(grad_query_rot.reshape(length, H, HEAD), -1.0).astype(BF16).reshape(length, H * HEAD)
    grad_key = rotate(grad_key_rot, -1.0).astype(BF16).reshape(length, KVH * HEAD)
    grad_qkv = jnp.concatenate([grad_query, grad_key, grad_value], axis=1)
    grad_w_qkv = dot_tn(normed_low, grad_qkv)
    grad_normed = dot_nt(grad_query, w_query) + dot_nt(grad_key, w_key) + dot_nt(grad_value, w_value)
    grad_norm_one, grad_gain_one = norm_one_pull(grad_normed)
    grad_tokens = grad_mixed + grad_norm_one

    n = ring.size

    def reduce_rows(g):
        cols = g.shape[1]
        part = g.astype(BF16).reshape(n, c_size, -1, cols)
        part = scatter_axis(part, "c", 1)
        part = part.astype(BF16).reshape(n, x_size, -1, cols)
        part = scatter_axis(part, "x", 1).astype(BF16).reshape(n, -1, cols)
        total = ring.scatter_sum(lambda j: lax.dynamic_index_in_dim(part, owners[j], 0, keepdims=False)).astype(BF16)
        total = gather_axis(gather_axis(total, "x", 0), "c", 0)
        return total.astype(F32)

    out_share = reduce_rows(grad_w_out)
    qkv_share = reduce_rows(grad_w_qkv)
    small = jnp.concatenate([grad_router.reshape(-1), grad_gain_two, jnp.full((128,), numerator)]).reshape(-1, 128)
    small = butterfly_sum(small, ("c", "x", "y", "z"))
    flat = small.reshape(-1)
    router_size = width * experts_all
    gain_one_sum = butterfly_sum(grad_gain_one.reshape(-1, 128), ("c", "x", "y", "z")).reshape(-1)
    return (
        output_rows.astype(BF16),
        flat[router_size + width] / count_total,
        grad_tokens,
        gain_one_sum,
        qkv_share[:, : H * HEAD],
        qkv_share[:, H * HEAD : (H + KVH) * HEAD],
        qkv_share[:, (H + KVH) * HEAD :],
        out_share,
        flat[router_size : router_size + width],
        flat[:router_size].reshape(width, experts_all),
        shares[0],
        shares[1],
        shares[2],
    )


def solution(mesh):
    rep, ep = mesh.shape["rep"], mesh.shape["ep"]
    x_size = rep // 2
    y_size = x_size if ep % x_size == 0 else 1
    grid = Mesh(mesh.devices.reshape(x_size, 2, ep // y_size, y_size), ALL)
    rows = P(ALL, None)
    whole = P()
    expert = P(EP, None, None)
    return jax.shard_map(
        functools.partial(shards, Ring(ep // y_size, y_size)),
        mesh=grid,
        in_specs=(rows,) * 5 + (whole,) * 7 + (expert,) * 3,
        out_specs=(rows, whole, rows, whole)
        + (P(EP, None),) * 4
        + (whole, whole)
        + (P(EP, ("x", "c"), None),) * 3,
        check_vma=False,
    )
```

```python
import functools
import math

import jax
import jax.numpy as jnp
import numpy as np
from jax import lax
from jax.experimental import pallas as pl
from jax.experimental.pallas import tpu as pltpu
from jax.sharding import Mesh
from jax.sharding import PartitionSpec as P

H = 12
KVH = 2
HEAD = 128

EPSILON = 1e-06
ROPE_BASE = 10000.0
NEG_FILL = -1e30
ALL = ("x", "c", "z", "y")
EP = ("z", "y")
F32 = jnp.float32
BF16 = jnp.bfloat16
RING_LIMIT = 16


def dot(a, b, dims=((1,), (0,))):
    return lax.dot_general(a, b, (dims, ((), ())), preferred_element_type=F32)


def dot_nt(a, b):
    return dot(a, b, ((1,), (1,)))


def dot_tn(a, b):
    return dot(a, b, ((0,), (0,)))


def activate(gate_pre, up_pre):
    return jax.nn.gelu(gate_pre, approximate=True) * up_pre


class Ring:
    def __init__(self, z_size, y_size):
        cycle = [(z, 0) for z in range(z_size)]
        for step, z in enumerate(reversed(range(z_size))):
            rest = list(range(1, y_size))
            cycle += [(z, y) for y in (rest if step % 2 == 0 else rest[::-1])]
        self.order = [z * y_size + y for z, y in cycle]
        self.size = len(self.order)
        self.half = self.size // 2
        n = self.size
        self.forward = [(self.order[i], self.order[(i + 1) % n]) for i in range(n)]
        self.backward = [(b, a) for a, b in self.forward]
        self.place = [self.order.index(e) for e in range(n)]

    def fwd(self, a):
        return lax.ppermute(a, EP, self.forward)

    def bwd(self, a):
        return lax.ppermute(a, EP, self.backward)

    def owners(self):
        mine = jnp.asarray(self.place, jnp.int32)[lax.axis_index(EP)]
        behind = (mine - jnp.arange(self.size, dtype=jnp.int32)) % self.size
        return jnp.asarray(self.order, jnp.int32)[behind]

    def pair(self, s):
        return sorted({s, (self.size - s) % self.size})

    def gather(self, a, cut, use, lag, beside=lambda step, sent: ()):
        ahead = behind = a
        ready = {0: a}
        open_steps = [0]
        for s in range(1, self.half + 1):
            sent = (ahead, behind)
            if s < self.half:
                ahead, behind = self.fwd(ahead), self.bwd(behind)
            else:
                ahead, behind = self.fwd(ahead[:cut]), self.bwd(behind[cut:])
            made = [beside(s - 1, sent)]
            while open_steps and open_steps[0] + lag <= s - 1:
                step = open_steps.pop(0)
                made.append(use({j: [after(ready[j], sent) if lag else ready[j]] for j in self.pair(step)}))
            ahead, behind, _ = lax.optimization_barrier((ahead, behind, made))
            if s < self.half:
                ready[s], ready[self.size - s] = ahead, behind
                open_steps.append(s)
        made = use({self.half: [ahead, behind]})
        for step in reversed(open_steps):
            use({j: [after(ready[j], made)] for j in self.pair(step)})

    def scatter_sum(self, terms, cut, beside=lambda step, sent: ()):
        def add(a, b):
            return (a.astype(F32) + b.astype(F32)).astype(BF16)

        far = terms(self.half)
        down, up = far[:cut], far[cut:]
        for s in range(self.half, 0, -1):
            sent = (down, up)
            down, up = self.bwd(down), self.fwd(up)
            down, up, _ = lax.optimization_barrier((down, up, beside(self.half - s, sent)))
            if s == self.half:
                near, away = terms(s - 1), terms(s + 1)
                down = jnp.concatenate([add(near[:cut], down), near[cut:]], axis=0)
                up = jnp.concatenate([away[:cut], add(away[cut:], up)], axis=0)
            elif s > 1:
                down, up = add(down, terms(s - 1)), add(up, terms(self.size - s + 1))
        return down, up, terms(0)


def butterfly_sum(a, axes):
    for axis in axes:
        size = lax.axis_size(axis)
        step = 1
        while step < size:
            a = a + lax.ppermute(a, axis, [(i, i ^ step) for i in range(size)])
            step *= 2
    return a


class Sum:
    def __init__(self, a):
        self.a = a

    @staticmethod
    def send(a, axis, dim):
        size = lax.axis_size(axis)
        if size != 2:
            got = lax.psum_scatter(a, axis, scatter_dimension=dim, tiled=True)
            return jnp.zeros_like(got), got
        me = lax.axis_index(axis)
        mine = lax.dynamic_slice_in_dim(a, me, 1, dim)
        other = lax.dynamic_slice_in_dim(a, 1 - me, 1, dim)
        return mine, lax.ppermute(other, axis, [(0, 1), (1, 0)])

    def over_cores(self, tie):
        self.mine, self.got = self.send(after(self.a, tie), "c", 1)

    def over_x(self, tie):
        mine, got = self.mine, after(self.got, tie)
        both = (mine.astype(F32) + got.astype(F32)).astype(BF16)
        self.mine, self.got = self.send(both, "x", 0)
        return both

    def result(self, tie):
        got = after(self.got, tie)
        return self.mine.astype(F32) + got.astype(F32)


class RingExperts:
    def __init__(self, ring, block, gates, top, w_gate, w_up, w_down):
        self.ring, self.block = ring, block
        self.experts, self.rows = gates.shape
        self.weights = (w_gate, w_up, w_down)
        self.cut = self.rows // 2
        self.expert = lax.axis_index(EP).reshape(1)

    def forward(self, gather_beside, beside):
        self.rows_in, self.saved = {}, {}
        terms, counts = {}, {}

        def use(blocks):
            made = expert_forward(list(blocks.values()), self.experts, self.expert, *self.weights)
            for j, (rows, term, gate_pre, up_pre, hidden, weight, count) in zip(blocks, made):
                self.rows_in[j], terms[j], counts[j] = rows, term, count
                self.saved[j] = (gate_pre, up_pre, hidden, weight)
            return made

        self.ring.gather(self.block, self.cut, use, 1, gather_beside)
        count = sum(counts[j] for j in range(self.ring.size))[0, 0]
        return self.ring.scatter_sum(terms.get, self.cut, beside), count

    def backward(self, grad_out):
        grads_in, gate_lows, up_lows, scaled, terms = {}, {}, {}, {}, {}

        def use(blocks):
            saved = [self.saved[j] for j in blocks]
            made = expert_backward(list(blocks.values()), saved, self.experts, self.expert, *self.weights)
            for j, each in zip(blocks, made):
                grads_in[j], terms[j], gate_lows[j], up_lows[j], scaled[j] = each
            return made

        self.ring.gather(grad_out.astype(BF16), self.cut, use, 0)
        sums = []

        def joined(parts):
            return jnp.concatenate([parts[j] for j in range(self.ring.size)], axis=0)

        def beside(step, sent):
            made = []
            if step == 0:
                self.joined = after(joined(self.rows_in), sent)
                sums.append(expert_sum(self.joined, joined(after(gate_lows, sent))))
                made.append(sums[0].a)
            if step == 1:
                sums[0].over_cores(sent)
                sums.append(expert_sum(self.joined, joined(after(up_lows, sent))))
                made.append(sums[1].a)
            if step == 2:
                made.append(sums[0].over_x(sent))
                sums[1].over_cores(sent)
                sums.append(expert_sum(joined(after(scaled, sent)), joined(after(grads_in, sent))))
                made.append(sums[2].a)
            if step == 3:
                made.append(sums[1].over_x(sent))
                made.append(sums[0].got)
                sums[2].over_cores(sent)
            return made

        return self.ring.scatter_sum(terms.get, self.cut, beside), sums


def expert_sum(a, b):
    product = dot_tn(a, b).astype(BF16)
    return Sum(product.reshape(lax.axis_size("x"), lax.axis_size("c"), -1, product.shape[1]))


class SlotExperts:
    def __init__(self, ring, block, gates, top, w_gate, w_up, w_down):
        experts, rows = gates.shape
        moe_in, route_hot = block[:rows], gates.T > 0
        self.count_here = jnp.full((8, 128), block[rows, -1].astype(F32))
        self.slots = 3 * rows * top // (2 * experts)
        self.group = ring.size
        self.moe_in, self.weights = moe_in, (w_gate, w_up, w_down)
        places = jnp.arange(rows)
        earlier = (places[:, None] > places[None, :]).astype(BF16)
        rank = dot(earlier, route_hot.astype(BF16)).T[:, None, :]
        slot = jnp.arange(self.slots, dtype=F32)[None, :, None]
        picks = ((rank == slot) & route_hot.T[:, None, :]).reshape(experts * self.slots, rows)
        self.picks = picks.astype(BF16)
        self.slot_gate = jnp.where(picks, jnp.repeat(gates, self.slots, axis=0), 0.0)

    def swap(self, rows):
        blocks = rows.reshape(self.group, -1, rows.shape[1])
        return lax.all_to_all(blocks, EP, 0, 0, tiled=True).reshape(rows.shape)

    def forward(self, gather_beside, beside):
        w_gate, w_up, w_down = self.weights
        self.arrived = self.swap(dot(self.picks, self.moe_in).astype(BF16))
        self.gate_pre = dot(self.arrived, w_gate)
        self.up_pre = dot(self.arrived, w_up)
        self.hidden = activate(self.gate_pre, self.up_pre).astype(BF16)
        self.returned = self.swap(dot(self.hidden, w_down).astype(BF16))
        count = butterfly_sum(self.count_here, ("y", "z"))[0, 0]
        return (jnp.dot(self.slot_gate.T, self.returned.astype(F32), precision=lax.Precision.HIGHEST),), count

    def backward(self, grad_out):
        w_gate, w_up, w_down = self.weights
        grad_low = grad_out.astype(BF16)
        rows, experts = grad_out.shape[0], self.picks.shape[0] // self.slots
        products = dot_nt(grad_low, self.returned) * self.picks.T.astype(F32)
        grad_gates = jnp.sum(products.reshape(rows, experts, self.slots), axis=2)
        slot_gate = jnp.sum(self.slot_gate, axis=1, keepdims=True)
        grads_in = self.swap((dot(self.picks, grad_low) * slot_gate).astype(BF16))
        _, pull = jax.vjp(activate, self.gate_pre, self.up_pre)
        grad_gate, grad_up = pull(dot_nt(grads_in, w_down))
        gate_low, up_low = grad_gate.astype(BF16), grad_up.astype(BF16)
        back = self.swap((dot_nt(gate_low, w_gate) + dot_nt(up_low, w_up)).astype(BF16))
        sums = [
            expert_sum(self.arrived, gate_low),
            expert_sum(self.arrived, up_low),
            expert_sum(self.hidden, grads_in),
        ]
        for each in sums:
            each.over_cores(each.a)
        for each in sums[:2]:
            each.over_x(each.a)
        notes = jnp.pad(grad_gates.T, ((0, 0), (0, grad_out.shape[1] - rows)))
        return (jnp.concatenate([dot_tn(self.picks, back), notes], axis=0),), sums


def rope_tables(length):
    half = HEAD // 2
    frequency = ROPE_BASE ** (-np.arange(half, dtype=np.float64) / half)
    angles = np.arange(length, dtype=np.float64)[:, None] * frequency[None, :]
    cosine, sine = np.cos(angles), np.sin(angles)
    pairs = np.concatenate([cosine, cosine], axis=1), np.concatenate([-sine, sine], axis=1)
    return tuple(jnp.asarray(p, F32) for p in pairs)


def turned(values, cosine, sine):
    return values * cosine + pltpu.roll(values, HEAD // 2, 1) * sine


def on_chip(count):
    return [pl.BlockSpec(memory_space=pltpu.VMEM)] * count


def in_place(count):
    return [pl.BlockSpec(memory_space=pltpu.HBM)] * count


def fetch(sources, buffers, semaphores):
    copies = [pltpu.make_async_copy(s, b, semaphores.at[i]) for i, (s, b) in enumerate(zip(sources, buffers))]
    for copy in copies:
        copy.start()
    return copies


def call(body, ins, places, outs, scratch=(), flops=0, moved=0, out_places=None, limit=28):
    return pl.pallas_call(
        body,
        out_shape=[jax.ShapeDtypeStruct(s, d) for s, d in outs],
        in_specs=places,
        out_specs=out_places or on_chip(len(outs)),
        scratch_shapes=list(scratch),
        compiler_params=pltpu.CompilerParams(vmem_limit_bytes=limit << 20),
        cost_estimate=pl.CostEstimate(flops=int(flops), bytes_accessed=int(moved), transcendentals=0),
    )(*ins)


def gelu_parts(values):
    c = math.sqrt(2.0 / math.pi)
    square = values * values
    level = 0.5 + 0.5 * jnp.tanh(c * values * (1.0 + 0.044715 * square))
    slope = level + 2.0 * c * values * level * (1.0 - level) * (1.0 + 3 * 0.044715 * square)
    return level, slope


def note_rows(experts, expert, columns):
    rows = lax.broadcasted_iota(jnp.int32, (experts, columns), 0)
    return (rows == expert).astype(F32)


def expert_forward_body(parts, experts, *refs):
    expert, w_gate, w_up, w_down = refs[0][0], *refs[1:4]
    at = 4
    inputs = []
    for count in parts:
        inputs.append(refs[at : at + count])
        at += count
    mine = note_rows(experts, expert, 128).astype(BF16)
    for pieces in inputs:
        rows_o, term_o, gate_o, up_o, hidden_o, weight_o, count_o = refs[at : at + 7]
        at += 7
        block = jnp.concatenate([p[...] for p in pieces], axis=0)
        rows = block.shape[0] - experts
        notes = block[rows:]
        block = block[:rows]
        rows_o[...] = block
        weight = dot_tn(notes[:, :rows], mine) + dot_tn(notes[:, rows : 2 * rows], mine)
        weight_o[...] = weight
        count_o[...] = notes[:, notes.shape[1] - 128 :].astype(F32)
        step = 256
        for f in range(0, w_gate.shape[1], step):
            gate_pre = dot(block, w_gate[:, f : f + step])
            up_pre = dot(block, w_up[:, f : f + step])
            level, _ = gelu_parts(gate_pre)
            hidden_o[:, f : f + step] = (gate_pre * level * up_pre).astype(BF16)
            gate_o[:, f : f + step] = gate_pre.astype(BF16)
            up_o[:, f : f + step] = up_pre.astype(BF16)
        hidden = hidden_o[...]
        wide = jnp.concatenate([weight] * (step // 128), axis=1)
        for c in range(0, block.shape[1], step):
            term_o[:, c : c + step] = (dot(hidden, w_down[:, c : c + step]) * wide).astype(BF16)


def expert_forward(blocks, experts, expert, w_gate, w_up, w_down):
    parts = [len(pieces) for pieces in blocks]
    flat = [p for pieces in blocks for p in pieces]
    rows = sum(p.shape[0] for p in blocks[0]) - experts
    width, inner = w_gate.shape
    one = [((rows, width), BF16)] * 2 + [((rows, inner), BF16)] * 3 + [((rows, 128), F32), ((experts, 128), F32)]
    made = call(
        functools.partial(expert_forward_body, parts, experts),
        (expert, w_gate, w_up, w_down, *flat),
        [pl.BlockSpec(memory_space=pltpu.SMEM)] + on_chip(3 + len(flat)),
        one * len(blocks),
        flops=len(blocks) * 6 * rows * width * inner,
        limit=24,
    )
    return [made[7 * i : 7 * i + 7] for i in range(len(blocks))]


def expert_backward_body(parts, experts, *refs):
    expert, w_gate, w_up, w_down = refs[0][0], *refs[1:4]
    at = 4
    inputs = []
    for count in parts:
        inputs.append((refs[at : at + count], *refs[at + count : at + count + 4]))
        at += count + 4
    for pieces, gate_ref, up_ref, hidden_ref, weight_ref in inputs:
        grads_o, term_o, gate_o, up_o, scaled_o = refs[at : at + 5]
        at += 5
        grads = jnp.concatenate([p[...] for p in pieces], axis=0)
        grads_o[...] = grads
        rows, width = grads.shape
        step = 256
        ones = jnp.ones((8, step), BF16)
        wide = jnp.concatenate([weight_ref[...]] * (step // 128), axis=1)
        sums = jnp.zeros((8, rows), F32)
        for f in range(0, w_down.shape[0], step):
            raw = dot_nt(grads, w_down[f : f + step, :])
            hidden = hidden_ref[:, f : f + step].astype(F32)
            product = raw * hidden
            high = product.astype(BF16)
            sums = sums + dot_nt(ones, high) + dot_nt(ones, (product - high.astype(F32)).astype(BF16))
            scaled_o[:, f : f + step] = (hidden * wide).astype(BF16)
            gate_pre = gate_ref[:, f : f + step].astype(F32)
            level, slope = gelu_parts(gate_pre)
            grad_hidden = raw * wide
            gate_o[:, f : f + step] = (grad_hidden * up_ref[:, f : f + step].astype(F32) * slope).astype(BF16)
            up_o[:, f : f + step] = (grad_hidden * gate_pre * level).astype(BF16)
        high = sums.astype(BF16).astype(F32)
        notes = jnp.concatenate([high, sums - high, jnp.zeros((8, width - 2 * rows), F32)], axis=1)
        mine = note_rows(experts, expert, width)
        notes = (jnp.broadcast_to(notes[:1], (experts, width)) * mine).astype(BF16)
        gate_low, up_low = gate_o[...], up_o[...]
        terms = [
            (dot_nt(gate_low, w_gate[c : c + step, :]) + dot_nt(up_low, w_up[c : c + step, :])).astype(BF16)
            for c in range(0, width, step)
        ]
        term_o[...] = jnp.concatenate([jnp.concatenate(terms, axis=1), notes], axis=0)


def expert_backward(blocks, saved, experts, expert, w_gate, w_up, w_down):
    parts = [len(pieces) for pieces in blocks]
    flat = [p for pieces, kept in zip(blocks, saved) for p in (*pieces, *kept)]
    rows, inner = saved[0][0].shape
    width = w_gate.shape[0]
    one = [((rows, width), BF16), ((rows + experts, width), BF16)] + [((rows, inner), BF16)] * 3
    made = call(
        functools.partial(expert_backward_body, parts, experts),
        (expert, w_gate, w_up, w_down, *flat),
        [pl.BlockSpec(memory_space=pltpu.SMEM)] + on_chip(3 + len(flat)),
        one * len(blocks),
        flops=len(blocks) * 6 * rows * width * inner,
        limit=24,
    )
    return [made[5 * i : 5 * i + 5] for i in range(len(blocks))]


def attention_forward_body(*refs):
    hbm, outs_hbm, (block_o, gates_o), refs = refs[:13], refs[13:20], refs[20:22], refs[22:]
    bufs, stores, sems, out_sems = refs[:13], refs[13:20], refs[20], refs[21]
    copies = fetch(hbm, bufs, sems)
    tokens, segments, routes, valid, gain_one, gain_two, cosine, sine, router = bufs[:9]
    w_key, w_value, w_query, w_out = bufs[9:]
    normed_o, query_o, key_o, value_o, weights_o, context_o, mixed_o = stores
    leaving = []

    def leave(*which):
        for i in which:
            leaving.append(pltpu.make_async_copy(stores[i], outs_hbm[i], out_sems.at[i]))
            leaving[-1].start()

    for copy in copies[:9]:
        copy.wait()
    copies = copies[9:]
    rows, width = tokens.shape
    groups = H // KVH
    rows_in = tokens[...].astype(F32)
    inverse = lax.rsqrt(jnp.mean(rows_in * rows_in, axis=1, keepdims=True) + EPSILON)
    normed = (rows_in * inverse * gain_one[...].astype(F32)).astype(BF16)
    normed_o[...] = normed
    leave(0)
    cos, sin = cosine[...], sine[...]
    copies[0].wait()
    keys = dot(normed, w_key[...])
    for g in range(KVH):
        at = pl.ds(g * HEAD, HEAD)
        key_o[:, at] = turned(keys[:, g * HEAD : (g + 1) * HEAD], cos, sin).astype(BF16)
    copies[1].wait()
    value_o[...] = dot(normed, w_value[...]).astype(BF16)
    leave(2, 3)
    copies[2].wait()
    half = rows // 2
    lower = lax.broadcasted_iota(jnp.int32, (rows, rows), 0) >= lax.broadcasted_iota(jnp.int32, (rows, rows), 1)
    across = jnp.broadcast_to(segments[...].astype(F32), (rows, rows))
    allowed = (across == across.T) & lower
    for g in range(KVH):
        span = groups * HEAD
        queries = dot(normed, w_query[:, g * span : (g + 1) * span])
        key = key_o[:, g * HEAD : (g + 1) * HEAD]
        value = value_o[:, g * HEAD : (g + 1) * HEAD]
        for i in range(groups):
            h = g * groups + i
            at = pl.ds(h * HEAD, HEAD)
            query = turned(queries[:, i * HEAD : (i + 1) * HEAD], cos, sin).astype(BF16)
            query_o[:, at] = query
            for first, last in ((0, half), (half, rows)):
                scores = dot_nt(query[first:last], key[:last]) * HEAD ** (-0.5)
                scores = jnp.where(allowed[first:last, :last], scores, NEG_FILL)
                peak = jnp.max(scores, axis=1, keepdims=True)
                terms = jnp.exp(scores - peak)
                weights = (terms / jnp.sum(terms, axis=1, keepdims=True)).astype(BF16)
                weights_o[h * rows + first : h * rows + last, :last] = weights
                context_o[first:last, at] = dot(weights, value[:last]).astype(BF16)
            weights_o[h * rows : h * rows + half, half:] = jnp.zeros((half, rows - half), BF16)
    leave(1, 4, 5)
    copies[3].wait()
    step = width // 3
    for c in range(0, width, step):
        mixed_o[:, c : c + step] = tokens[:, c : c + step].astype(F32) + dot(context_o[...], w_out[:, c : c + step])
    leave(6)
    mixed = mixed_o[...]
    inverse = lax.rsqrt(jnp.mean(mixed * mixed, axis=1, keepdims=True) + EPSILON)
    moe_in = (mixed * inverse * gain_two[...].astype(F32)).astype(BF16)
    experts = router.shape[0]
    logits = dot_nt(router[...], moe_in)
    ids = lax.broadcasted_iota(jnp.int32, (experts, rows), 0)
    hot = ids == routes[0:1, :]
    for k in range(1, routes.shape[0]):
        hot = hot | (ids == routes[k : k + 1, :])
    peak = jnp.max(jnp.where(hot, logits, NEG_FILL), axis=0, keepdims=True)
    terms = jnp.where(hot, jnp.exp(jnp.where(hot, logits - peak, 0.0)), 0.0)
    gates = terms / jnp.sum(terms, axis=0, keepdims=True)
    gates_o[...] = gates
    high = gates.astype(BF16).astype(F32)
    low = gates - high
    count = jnp.sum(valid[...].astype(F32), axis=1, keepdims=True)
    counts = jnp.broadcast_to(count, (experts, width - 2 * rows))
    notes = jnp.concatenate([high, low, counts], axis=1).astype(BF16)
    block_o[...] = jnp.concatenate([moe_in, notes], axis=0)
    for copy in leaving:
        copy.wait()


def attention_forward(tokens, segments, routes, valid, gain_one, gain_two, tables, router, weights):
    rows, width = tokens.shape
    experts = router.shape[1]
    w_query, w_key, w_value, w_out = weights
    ins = (tokens, segments, routes.T, valid, gain_one[None], gain_two[None], *tables, router.T)
    ins += (w_key, w_value, w_query, w_out)
    stores = [
        ((rows, width), BF16),
        ((rows, H * HEAD), BF16),
        ((rows, KVH * HEAD), BF16),
        ((rows, KVH * HEAD), BF16),
        ((H * rows, rows), BF16),
        ((rows, H * HEAD), BF16),
        ((rows, width), F32),
    ]
    return call(
        attention_forward_body,
        ins,
        in_place(len(ins)),
        stores + [((rows + experts, width), BF16), ((experts, rows), F32)],
        [pltpu.VMEM(a.shape, a.dtype) for a in ins]
        + [pltpu.VMEM(*store) for store in stores]
        + [pltpu.SemaphoreType.DMA((len(ins),)), pltpu.SemaphoreType.DMA((len(stores),))],
        flops=2 * rows * width * (2 * width + 4 * KVH * HEAD),
        moved=14 << 20,
        out_places=in_place(len(stores)) + on_chip(2),
        limit=60,
    )


def mixed_backward_body(parts, *refs):
    ins, outs = refs[:parts], refs[parts + 6 :]
    grad_out, mixed_ref, moe_in, gates, router, gain_two = refs[parts : parts + 6]
    branch_o, mixed_o, gain_o, router_o = outs
    rows, width = grad_out.shape
    experts = gates.shape[0]
    total = ins[0][...].astype(F32)
    for part in ins[1:]:
        total = total + part[...].astype(F32)
    notes = total[rows : rows + experts]
    grad_gates = notes[:, :rows] + notes[:, rows : 2 * rows]
    weights = gates[...]
    chosen = weights * (grad_gates - jnp.sum(weights * grad_gates, axis=0, keepdims=True))
    logits = chosen.astype(BF16)
    router_o[...] = dot(logits, moe_in[:rows])
    grad_in = total[:rows] + dot_tn(logits, router[...])
    mixed = mixed_ref[...]
    inverse = lax.rsqrt(jnp.mean(mixed * mixed, axis=1, keepdims=True) + EPSILON)
    normal = mixed * inverse
    gain_o[...] = jnp.sum(grad_in * normal, axis=0, keepdims=True)
    scaled = grad_in * gain_two[...].astype(F32)
    inner = jnp.mean(scaled * normal, axis=1, keepdims=True)
    grad_mixed = grad_out[...] + inverse * (scaled - normal * inner)
    mixed_o[...] = grad_mixed
    branch_o[...] = grad_mixed.astype(BF16)


def mixed_backward(parts, grad_out, mixed, block, gates, router, gain_two):
    rows, width = mixed.shape
    experts = router.shape[1]
    ins = (*parts, grad_out, mixed, block, gates, router.T, gain_two[None])
    outs = [((rows, width), BF16), ((rows, width), F32), ((1, width), F32), ((experts, width), F32)]
    return call(functools.partial(mixed_backward_body, len(parts)), ins, on_chip(len(ins)), outs, moved=9 << 20)


def attention_backward_body(branch, weights, query, key, value, cosine, sine, w_hbm, qkv_o, w_out, sems):
    rows = branch.shape[0]
    groups = H // KVH
    span = groups * HEAD
    copies = [
        pltpu.make_async_copy(w_hbm.at[pl.ds(g * span, span)], w_out.at[pl.ds(g * span, span)], sems.at[g])
        for g in range(KVH)
    ]
    for copy in copies:
        copy.start()
    cos, sin = cosine[...], -sine[...]
    half = rows // 2
    scale = HEAD ** (-0.5)
    for g in range(KVH):
        copies[g].wait()
        grad_context = dot_nt(branch[...], w_out[g * span : (g + 1) * span, :]).astype(BF16)
        k = key[:, g * HEAD : (g + 1) * HEAD]
        v = value[:, g * HEAD : (g + 1) * HEAD]
        grad_key = jnp.zeros((rows, HEAD), F32)
        grad_value = jnp.zeros((rows, HEAD), F32)
        for i in range(groups):
            h = g * groups + i
            q = query[:, h * HEAD : (h + 1) * HEAD]
            grad = grad_context[:, i * HEAD : (i + 1) * HEAD]
            low = weights[h * rows : (h + 1) * rows, :]
            grads = dot_nt(grad, v)
            full = low.astype(F32)
            product = full * grads
            scores = (product - full * jnp.sum(product, axis=1, keepdims=True)).astype(BF16)
            grad_query = dot(scores, k) * scale
            qkv_o[:, h * HEAD : (h + 1) * HEAD] = turned(grad_query, cos, sin).astype(BF16)
            grad_key = grad_key + dot_tn(scores, q)
            grad_value = grad_value + dot_tn(low, grad)
        at = (H + g) * HEAD
        qkv_o[:, at : at + HEAD] = turned(grad_key * scale, cos, sin).astype(BF16)
        at += KVH * HEAD
        qkv_o[:, at : at + HEAD] = grad_value.astype(BF16)


def attention_backward(branch, weights, query, key, value, tables, w_out):
    rows = branch.shape[0]
    ins = (branch, weights, query, key, value, *tables)
    outs = [((rows, (H + 2 * KVH) * HEAD), BF16)]
    scratch = [pltpu.VMEM(w_out.shape, BF16), pltpu.SemaphoreType.DMA((KVH,))]
    (made,) = call(
        attention_backward_body,
        ins + (w_out,),
        on_chip(len(ins)) + in_place(1),
        outs,
        scratch,
    )
    return made


def token_backward_body(qkv, tokens, grad_mixed, gain_one, *rest):
    hbm, (tokens_o, gain_o), bufs, sems = rest[:3], rest[3:5], rest[5:8], rest[8]
    copies = fetch(hbm, bufs, sems)
    rows_in = tokens[...].astype(F32)
    inverse = lax.rsqrt(jnp.mean(rows_in * rows_in, axis=1, keepdims=True) + EPSILON)
    normal = rows_in * inverse
    at = H * HEAD
    span = KVH * HEAD
    copies[0].wait()
    grads = dot_nt(qkv[:, at : at + span], bufs[0][...])
    copies[1].wait()
    grads = grads + dot_nt(qkv[:, at + span :], bufs[1][...])
    copies[2].wait()
    grads = grads + dot_nt(qkv[:, :at], bufs[2][...])
    gain_o[...] = jnp.sum(grads * normal, axis=0, keepdims=True)
    scaled = grads * gain_one[...].astype(F32)
    inner = jnp.mean(scaled * normal, axis=1, keepdims=True)
    tokens_o[...] = grad_mixed[...] + inverse * (scaled - normal * inner)


def token_backward(qkv, tokens, grad_mixed, gain_one, weights):
    rows, width = tokens.shape
    w_query, w_key, w_value, _ = weights
    hbm = (w_key, w_value, w_query)
    ins = (qkv, tokens, grad_mixed, gain_one[None])
    outs = [((rows, width), F32), ((1, width), F32)]
    return call(
        token_backward_body,
        ins + hbm,
        on_chip(len(ins)) + in_place(3),
        outs,
        [pltpu.VMEM(w.shape, BF16) for w in hbm] + [pltpu.SemaphoreType.DMA((3,))],
    )


def after(value, first):
    return lax.optimization_barrier((value, first))[0]


def rep_pairs(k):
    size = lax.axis_size(("x", "c"))
    return [(i, i ^ k) for i in range(size)]


def x_gather(a):
    size = lax.axis_size("x")
    return [a] + [lax.ppermute(a, "x", [(i, i ^ k) for i in range(size)]) for k in range(1, size)]


def core_gather(blocks):
    return [b for a in blocks for b in (a, lax.ppermute(a, "c", [(0, 1), (1, 0)]))]


def rep_gather(a):
    return core_gather(x_gather(a))


def rep_spread(a):
    size = lax.axis_size(("x", "c"))
    me = lax.axis_index(("x", "c"))
    share = a.shape[1] // size
    parts = []
    for k in range(size):
        part = lax.dynamic_slice_in_dim(a, (me ^ k) * share, share, 1)
        parts.append(lax.ppermute(part, ("x", "c"), rep_pairs(k)) if k else part)
    return jnp.concatenate(parts, axis=0)


def rep_columns(a):
    size = lax.axis_size(("x", "c"))
    stacked = jnp.stack(rep_gather(a))
    me = lax.axis_index(("x", "c"))
    return jnp.concatenate(
        [lax.dynamic_index_in_dim(stacked, me ^ i, 0, keepdims=False) for i in range(size)], axis=1
    )


def shards(
    ring,
    tokens,
    segments,
    routes,
    valid_mask,
    teacher,
    gain_one,
    w_query,
    w_key,
    w_value,
    w_out,
    gain_two,
    router,
    w_gate,
    w_up,
    w_down,
):
    length, width = tokens.shape
    experts_all = router.shape[1]
    tokens_all = length * lax.axis_size(ALL)
    w_gate, w_up, w_down = w_gate[0], w_up[0], w_down[0]
    valid_rows = valid_mask.reshape(length).astype(F32)
    tables = rope_tables(length)
    attn = (w_query, w_key, w_value, w_out)
    normed_low, query, key, value, weights_low, context, mixed_rows, block, gates = attention_forward(
        tokens, segments, routes, valid_mask, gain_one, gain_two, tables, router, attn
    )
    owners = ring.owners()
    form = RingExperts if ring.size <= RING_LIMIT else SlotExperts
    experts = form(ring, block, gates, routes.shape[1], w_gate, w_up, w_down)
    gathered = {}

    def beside(name, value):
        def work(step, sent):
            if step == 0:
                gathered[name] = x_gather(after(value, sent))
            if step == 2:
                gathered[name] = core_gather(after(gathered[name], sent))
            if step == 1 or step == 3:
                return gathered[name]
            return ()

        return work

    moe_parts, count_group = experts.forward(beside("normed", normed_low), beside("context", context))
    moe_out = sum(part.astype(F32) for part in moe_parts)
    if not gathered:
        gathered = {"normed": rep_gather(normed_low), "context": rep_gather(context)}
    count_total = butterfly_sum(jnp.full((8, 128), count_group), ("c", "x"))[0, 0]
    output_rows = mixed_rows + moe_out
    residual_gap = output_rows - teacher.astype(F32)
    numerator = jnp.sum(valid_rows * jnp.sum(residual_gap * residual_gap, axis=-1))
    grad_out = 2.0 * tokens_all / count_total * valid_rows[:, None] * residual_gap

    grad_out, gathered = lax.optimization_barrier((grad_out, gathered))
    normed_all = jnp.concatenate(gathered["normed"], axis=0)
    context_all = jnp.concatenate(gathered["context"], axis=0)
    back_parts, sums = experts.backward(grad_out)
    grad_branch, grad_mixed, grad_gain_two, grad_router = mixed_backward(
        back_parts, grad_out, mixed_rows, block, gates, router, gain_two
    )
    branch_spread = rep_spread(grad_branch)
    grad_qkv = attention_backward(grad_branch, weights_low, query, key, value, tables, w_out)
    qkv_spread = rep_spread(grad_qkv)
    grad_w_out = dot_tn(context_all, after(branch_spread, grad_qkv)).astype(BF16)
    grad_w_qkv = dot_tn(normed_all, after(qkv_spread, grad_w_out)).astype(BF16)
    grad_tokens, grad_gain_one = token_backward(
        after(grad_qkv, (grad_w_qkv, sums[1].got)), tokens, grad_mixed, gain_one, attn
    )
    sums[2].over_x(grad_w_qkv)

    def reduce_rows(g):
        part = g.astype(BF16).reshape(ring.size, -1, g.shape[1])
        cut = part.shape[1] // 2
        total = ring.scatter_sum(lambda j: lax.dynamic_index_in_dim(part, owners[j], 0, keepdims=False), cut)
        return rep_columns(sum(t.astype(F32) for t in total).astype(BF16)).astype(F32)

    shares = [each.result(grad_tokens)[0] for each in sums]
    out_share = reduce_rows(grad_w_out)
    qkv_share = reduce_rows(grad_w_qkv)
    small = jnp.concatenate(
        [grad_router.reshape(-1), grad_gain_two[0], grad_gain_one[0], jnp.full((128,), numerator)]
    ).reshape(-1, 128)
    flat = butterfly_sum(small, ("c", "x", "y", "z")).reshape(-1)
    at = width * experts_all
    return (
        output_rows.astype(BF16),
        flat[at + 2 * width] / count_total,
        grad_tokens,
        flat[at + width : at + 2 * width],
        qkv_share[:, : H * HEAD],
        qkv_share[:, H * HEAD : (H + KVH) * HEAD],
        qkv_share[:, (H + KVH) * HEAD :],
        out_share,
        flat[at : at + width],
        flat[:at].reshape(experts_all, width).T,
        shares[0],
        shares[1],
        shares[2],
    )


def solution(mesh):
    rep, ep = mesh.shape["rep"], mesh.shape["ep"]
    x_size = rep // 2
    y_size = x_size if ep % x_size == 0 else 1
    grid = Mesh(mesh.devices.reshape(x_size, 2, ep // y_size, y_size), ALL)
    rows = P(ALL, None)
    whole = P()
    expert = P(EP, None, None)
    return jax.shard_map(
        functools.partial(shards, Ring(ep // y_size, y_size)),
        mesh=grid,
        in_specs=(rows,) * 5 + (whole,) * 7 + (expert,) * 3,
        out_specs=(rows, whole, rows, whole)
        + (P(EP, None),) * 4
        + (whole, whole)
        + (P(EP, ("x", "c"), None),) * 3,
        check_vma=False,
    )
```

```python
import functools
import math

import jax
import jax.numpy as jnp
import numpy as np
from jax import lax
from jax.experimental import pallas as pl
from jax.experimental.pallas import tpu as pltpu
from jax.sharding import Mesh
from jax.sharding import PartitionSpec as P

H = 12
KVH = 2
HEAD = 128

EPSILON = 1e-06
ROPE_BASE = 10000.0
NEG_FILL = -1e30
ALL = ("x", "c", "z", "y")
EP = ("z", "y")
F32 = jnp.float32
BF16 = jnp.bfloat16
RING_LIMIT = 16
SPLIT = True
LEAN = 20


def dot(a, b, dims=((1,), (0,))):
    return lax.dot_general(a, b, (dims, ((), ())), preferred_element_type=F32)


def dot_nt(a, b):
    return dot(a, b, ((1,), (1,)))


def dot_tn(a, b):
    return dot(a, b, ((0,), (0,)))


def activate(gate_pre, up_pre):
    return jax.nn.gelu(gate_pre, approximate=True) * up_pre


class Ring:
    def __init__(self, z_size, y_size):
        cycle = [(z, 0) for z in range(z_size)]
        for step, z in enumerate(reversed(range(z_size))):
            rest = list(range(1, y_size))
            cycle += [(z, y) for y in (rest if step % 2 == 0 else rest[::-1])]
        self.order = [z * y_size + y for z, y in cycle]
        self.size = len(self.order)
        self.half = self.size // 2
        n = self.size
        self.forward = [(self.order[i], self.order[(i + 1) % n]) for i in range(n)]
        self.backward = [(b, a) for a, b in self.forward]
        self.place = [self.order.index(e) for e in range(n)]

    def fwd(self, a):
        return lax.ppermute(a, EP, self.forward)

    def bwd(self, a):
        return lax.ppermute(a, EP, self.backward)

    def owner(self, j):
        me = lax.axis_index(EP)
        found = 0
        for e, place in enumerate(self.place):
            found = found + jnp.where(me == e, self.order[(place - j) % self.size], 0)
        return found

    def pair(self, s):
        return sorted({s, (self.size - s) % self.size})

    def gather(self, pieces, use, lag, beside=lambda step, sent: ()):
        ahead = behind = list(pieces) if SPLIT else [jnp.concatenate(pieces, axis=0)]
        cut = pieces[0].shape[0]
        ready = {0: ahead}
        open_steps = [0]
        for s in range(1, self.half + 1):
            sent = (ahead, behind)
            if s == self.half and SPLIT:
                ahead, behind = ahead[:1], behind[1:]
            elif s == self.half:
                ahead, behind = [ahead[0][:cut]], [behind[0][cut:]]
            ahead, behind = [self.fwd(p) for p in ahead], [self.bwd(p) for p in behind]
            made = [beside(s - 1, sent)]
            while open_steps and open_steps[0] + lag <= s - 1:
                step = open_steps.pop(0)
                made.append(use({j: after(ready[j], sent) if lag else ready[j] for j in self.pair(step)}))
            ahead[0], behind[0], _ = lax.optimization_barrier((ahead[0], behind[0], made))
            if s < self.half:
                ready[s], ready[self.size - s] = list(ahead), list(behind)
                open_steps.append(s)
        made = use({self.half: ahead + behind})
        for step in reversed(open_steps):
            use({j: after(ready[j], made) for j in self.pair(step)})

    def scatter_sum(self, terms, beside=lambda step, sent: ()):
        def add(a, b):
            return (a.astype(F32) + b.astype(F32)).astype(BF16)

        far, (near,), (away,) = terms(self.half), terms(self.half - 1), terms(self.half + 1)
        cut = far[0].shape[0]
        down, up = self.bwd(far[0]), self.fwd(far[1])
        down, up, _ = lax.optimization_barrier((down, up, beside(0, far)))
        down = [jnp.concatenate([add(near[:cut], down), near[cut:]], axis=0)]
        up = [jnp.concatenate([away[:cut], add(away[cut:], up)], axis=0)]
        for s in range(self.half - 1, 0, -1):
            sent = (down, up)
            down, up = [self.bwd(p) for p in down], [self.fwd(p) for p in up]
            down[0], up[0], _ = lax.optimization_barrier((down[0], up[0], beside(self.half - s, sent)))
            if s > 1:
                down = [add(a, b) for a, b in zip(down, terms(s - 1))]
                up = [add(a, b) for a, b in zip(up, terms(self.size - s + 1))]
        return down, up, terms(0)


class RingSum:
    def __init__(self, ring, terms):
        self.ring, self.terms, self.left = ring, terms, ring.half
        cut = terms[0].shape[0] // 32 * 16
        self.cut = cut
        far = terms[ring.half]
        self.sent = far
        self.down, self.up = ring.bwd(far[:cut]), ring.fwd(far[cut:])

    def arrive(self, tie):
        self.down, self.up, _ = lax.optimization_barrier((self.down, self.up, tie))

    def step(self, tie):
        ring, cut = self.ring, self.cut
        self.arrive(tie)
        self.left -= 1

        def add(a, b):
            return (a.astype(F32) + b.astype(F32)).astype(BF16)

        near, away = self.terms[self.left], self.terms[ring.size - self.left]
        if self.left == ring.half - 1:
            down = jnp.concatenate([add(near[:cut], self.down), near[cut:]], axis=0)
            up = jnp.concatenate([away[:cut], add(away[cut:], self.up)], axis=0)
        else:
            down, up = add(near, self.down), add(away, self.up)
        self.sent = (down, up)
        self.down, self.up = ring.bwd(down), ring.fwd(up)

    def total(self, tie):
        self.arrive(tie)
        return (self.down.astype(F32) + self.up.astype(F32) + self.terms[0].astype(F32)).astype(BF16)


def butterfly_hops(axes):
    return [(axis, step) for axis in axes for step in (1, 2, 4, 8, 16) if step < lax.axis_size(axis)]


def butterfly_hop(a, hop, tie):
    axis, step = hop
    a, _ = lax.optimization_barrier((a, tie))
    return a, lax.ppermute(a, axis, [(i, i ^ step) for i in range(lax.axis_size(axis))])


def added(lists):
    return sum(jnp.concatenate(pieces, axis=0).astype(F32) for pieces in lists)


def butterfly_sum(a, axes):
    for axis in axes:
        size = lax.axis_size(axis)
        step = 1
        while step < size:
            a = a + lax.ppermute(a, axis, [(i, i ^ step) for i in range(size)])
            step *= 2
    return a


class Sum:
    def __init__(self, a):
        self.a = a

    @staticmethod
    def send(a, axis, dim):
        size = lax.axis_size(axis)
        if size != 2:
            got = lax.psum_scatter(a, axis, scatter_dimension=dim, tiled=True)
            return jnp.zeros_like(got), got
        first = lax.axis_index(axis) == 0
        low, high = lax.slice_in_dim(a, 0, 1, axis=dim), lax.slice_in_dim(a, 1, 2, axis=dim)
        return jnp.where(first, low, high), lax.ppermute(jnp.where(first, high, low), axis, [(0, 1), (1, 0)])

    def over_cores(self, tie):
        self.mine, self.got = self.send(after(self.a, tie), "c", 1)

    def over_x(self, tie):
        mine, got = self.mine, after(self.got, tie)
        both = (mine.astype(F32) + got.astype(F32)).astype(BF16)
        self.mine, self.got = self.send(both, "x", 0)
        return both

    def result(self, tie):
        got = after(self.got, tie)
        return self.mine.astype(F32) + got.astype(F32)


class RingExperts:
    def __init__(self, ring, block, gates, top, w_gate, w_up, w_down):
        self.ring, self.block = ring, list(block)
        self.experts, self.rows = gates.shape
        self.weights = (w_gate, w_up, w_down)
        self.cut = self.rows // 2

    def forward(self, gather_beside, beside):
        self.rows_in, self.saved = {}, {}
        terms, counts = {}, {}

        def use(blocks):
            apart = self.ring.half in blocks
            made = expert_forward(list(blocks.values()), self.experts, apart, *self.weights)
            for j, (rows, top, gate_pre, up_pre, hidden, weight, count, *bottom) in zip(blocks, made):
                self.rows_in[j], terms[j], counts[j] = rows, [top, *bottom], count
                self.saved[j] = (gate_pre, up_pre, hidden, weight)
            return made

        self.ring.gather(self.block, use, 1, gather_beside)
        self.count = sum(counts[j] for j in range(self.ring.size))
        return self.ring.scatter_sum(terms.get, beside)

    def backward(self, grad_out):
        grads_in, gate_lows, up_lows, scaled, terms = {}, {}, {}, {}, {}

        def use(blocks):
            saved = [self.saved[j] for j in blocks]
            apart = self.ring.half in blocks
            made = expert_backward(list(blocks.values()), saved, self.experts, apart, *self.weights)
            for j, (grads, top, gate_low, up_low, part, *bottom) in zip(blocks, made):
                grads_in[j], gate_lows[j], up_lows[j], scaled[j] = grads, gate_low, up_low, part
                terms[j] = [top, *bottom]
            return made

        low = grad_out.astype(BF16)
        self.ring.gather([low[: self.cut], low[self.cut :]], use, 0)
        sums = []

        def joined(parts):
            return jnp.concatenate([parts[j] for j in range(self.ring.size)], axis=0)

        def beside(step, sent):
            made = []
            if step == 0:
                self.joined = after(joined(self.rows_in), sent)
                sums.append(expert_sum(self.joined, joined(after(gate_lows, sent))))
            if step == 1:
                sums.append(expert_sum(self.joined, joined(after(up_lows, sent))))
            if step == 2:
                sums.append(expert_sum(joined(after(scaled, sent)), joined(after(grads_in, sent))))
                made.append(sums[0].got)
            if step == 3:
                made.append(sums[1].got)
            if step > 0:
                made.append(sums[step - 1].over_x(sent))
            if step < 3:
                made.append(sums[step].a)
                sums[step].over_cores(sums[step].a)
            return made

        return self.ring.scatter_sum(terms.get, beside), sums


def expert_sum(a, b):
    product = dot_tn(a, b).astype(BF16)
    return Sum(product.reshape(lax.axis_size("x"), lax.axis_size("c"), -1, product.shape[1]))


class SlotExperts:
    def __init__(self, ring, block, gates, top, w_gate, w_up, w_down):
        experts, rows = gates.shape
        block = jnp.concatenate(block, axis=0)
        moe_in, route_hot = block[:rows], gates.T > 0
        self.count_here = jnp.full((8, 128), block[rows, -1].astype(F32))
        self.slots = 3 * rows * top // (2 * experts)
        self.group = ring.size
        self.moe_in, self.weights = moe_in, (w_gate, w_up, w_down)
        places = jnp.arange(rows)
        earlier = (places[:, None] > places[None, :]).astype(BF16)
        rank = dot(earlier, route_hot.astype(BF16)).T[:, None, :]
        slot = jnp.arange(self.slots, dtype=F32)[None, :, None]
        picks = ((rank == slot) & route_hot.T[:, None, :]).reshape(experts * self.slots, rows)
        self.picks = picks.astype(BF16)
        self.slot_gate = jnp.where(picks, jnp.repeat(gates, self.slots, axis=0), 0.0)

    def swap(self, rows):
        blocks = rows.reshape(self.group, -1, rows.shape[1])
        return lax.all_to_all(blocks, EP, 0, 0, tiled=True).reshape(rows.shape)

    def forward(self, gather_beside, beside):
        w_gate, w_up, w_down = self.weights
        self.arrived = self.swap(dot(self.picks, self.moe_in).astype(BF16))
        self.gate_pre = dot(self.arrived, w_gate)
        self.up_pre = dot(self.arrived, w_up)
        self.hidden = activate(self.gate_pre, self.up_pre).astype(BF16)
        self.returned = self.swap(dot(self.hidden, w_down).astype(BF16))
        self.count = butterfly_sum(self.count_here, ("y", "z"))
        return [[jnp.dot(self.slot_gate.T, self.returned.astype(F32), precision=lax.Precision.HIGHEST)]]

    def backward(self, grad_out):
        w_gate, w_up, w_down = self.weights
        grad_low = grad_out.astype(BF16)
        rows, experts = grad_out.shape[0], self.picks.shape[0] // self.slots
        products = dot_nt(grad_low, self.returned) * self.picks.T.astype(F32)
        grad_gates = jnp.sum(products.reshape(rows, experts, self.slots), axis=2)
        slot_gate = jnp.sum(self.slot_gate, axis=1, keepdims=True)
        grads_in = self.swap((dot(self.picks, grad_low) * slot_gate).astype(BF16))
        _, pull = jax.vjp(activate, self.gate_pre, self.up_pre)
        grad_gate, grad_up = pull(dot_nt(grads_in, w_down))
        gate_low, up_low = grad_gate.astype(BF16), grad_up.astype(BF16)
        back = self.swap((dot_nt(gate_low, w_gate) + dot_nt(up_low, w_up)).astype(BF16))
        sums = [
            expert_sum(self.arrived, gate_low),
            expert_sum(self.arrived, up_low),
            expert_sum(self.hidden, grads_in),
        ]
        for each in sums:
            each.over_cores(each.a)
        for each in sums:
            each.over_x(each.a)
        notes = jnp.pad(grad_gates.T, ((0, 0), (0, grad_out.shape[1] - rows)))
        return [[jnp.concatenate([dot_tn(self.picks, back), notes], axis=0)]], sums


def rope_tables(length):
    half = HEAD // 2
    frequency = ROPE_BASE ** (-np.arange(half, dtype=np.float64) / half)
    angles = np.arange(length, dtype=np.float64)[:, None] * frequency[None, :]
    cosine, sine = np.cos(angles), np.sin(angles)
    pairs = np.concatenate([cosine, cosine], axis=1), np.concatenate([-sine, sine], axis=1)
    return tuple(jnp.asarray(p, F32) for p in pairs)


def turned(values, cosine, sine):
    return values * cosine + pltpu.roll(values, HEAD // 2, 1) * sine


class Stage:
    def __init__(self, slices, outs, first, refs):
        n, m = len(slices), len(outs)
        self.there, self.out_there, refs = refs[:n], refs[n : n + m], refs[n + m :]
        self.here, self.out, in_sems, out_sems = refs[:n], refs[n : n + m], refs[n + m], refs[n + m + 1]
        self.out_sems = out_sems
        self.later = []
        self.coming = {}
        for i, rows in enumerate(slices):
            source = self.there[i] if rows is None else self.there[i].at[pl.ds(*rows)]
            self.coming[i] = pltpu.make_async_copy(source, self.here[i], in_sems.at[i])
            if i < first:
                self.coming[i].start()
            else:
                self.later.append(self.coming[i])
        self.leaving = []

    def get(self, i):
        if i in self.coming:
            self.coming.pop(i).wait()
        for copy in self.later:
            copy.start()
        self.later = []
        return self.here[i]

    def put(self, *which):
        for i in which:
            self.send(self.out[i], i)

    def send(self, source, i):
        self.leaving.append(pltpu.make_async_copy(source, self.out_there[i], self.out_sems.at[i]))
        self.leaving[-1].start()

    def finish(self):
        for copy in self.leaving:
            copy.wait()


def staged(body, ins, outs, scalars=(), flops=0, kept=(), limit=60, first=None, straight=(), room=(), held=()):
    arrays = [a if isinstance(a, jax.Array) else a[0] for a in ins]
    slices = [None if isinstance(a, jax.Array) else a[1:] for a in ins]
    sizes = [a.shape if s is None else (s[1], *a.shape[1:]) for a, s in zip(arrays, slices)]
    start = len(ins) if first is None else first
    tile = ((8, 128), BF16)

    def kernel(*refs):
        count = len(scalars) + len(kept)
        stage = Stage(slices, outs, start, refs[count : len(refs) - len(room)])
        stage.out = [there if i in held else o for i, (there, o) in enumerate(zip(stage.out_there, stage.out))]
        stage.room = refs[len(refs) - len(room) :]
        body(stage, *refs[:count])
        stage.finish()

    any_place = pl.BlockSpec(memory_space=pltpu.HBM)
    vmem = [pltpu.VMEM(*(tile if i in straight or i in held else o)) for i, o in enumerate(outs)]
    out_places = [on_chip(1)[0] if i in held else any_place for i in range(len(outs))]
    return pl.pallas_call(
        kernel,
        out_shape=[jax.ShapeDtypeStruct(s, d) if i in held else pltpu.HBM(s, d) for i, (s, d) in enumerate(outs)],
        in_specs=[pl.BlockSpec(memory_space=pltpu.SMEM)] * len(scalars) + on_chip(len(kept)) + [any_place] * len(ins),
        out_specs=out_places,
        scratch_shapes=[pltpu.VMEM(s, a.dtype) for s, a in zip(sizes, arrays)]
        + vmem
        + [pltpu.SemaphoreType.DMA((max(len(ins), 1),)), pltpu.SemaphoreType.DMA((len(outs),))]
        + [pltpu.VMEM(*r) for r in room],
        compiler_params=pltpu.CompilerParams(vmem_limit_bytes=limit << 20),
        cost_estimate=pl.CostEstimate(flops=int(flops), bytes_accessed=0, transcendentals=0),
    )(*scalars, *kept, *(pltpu.with_memory_space_constraint(a, pltpu.HBM) for a in arrays))


def on_chip(count):
    return [pl.BlockSpec(memory_space=pltpu.VMEM)] * count


def rep_index():
    return lax.axis_index("x") * lax.axis_size("c") + lax.axis_index("c")


def rep_shares(columns):
    size = lax.axis_size(("x", "c"))
    return size if columns % (128 * size) == 0 else 0


def send_shares(stage, source, at):
    count = rep_shares(source.shape[1])
    share = source.shape[1] // max(count, 1)
    me = rep_index()
    for k in range(count):
        start = pl.multiple_of((me ^ k) * share, 128)
        stage.send(source.at[:, pl.ds(start, share)], at + k)


def shares_shape(rows, columns):
    count = rep_shares(columns)
    return [((rows, columns // max(count, 1)), BF16)] * count


def gelu_parts(values):
    c = math.sqrt(2.0 / math.pi)
    square = values * values
    level = 0.5 + 0.5 * jnp.tanh(c * values * (1.0 + 0.044715 * square))
    slope = level + 2.0 * c * values * level * (1.0 - level) * (1.0 + 3 * 0.044715 * square)
    return level, slope


def note_rows(experts, expert, columns):
    rows = lax.broadcasted_iota(jnp.int32, (experts, columns), 0)
    return (rows == expert).astype(F32)


def joined_rows(refs):
    return jnp.concatenate([r[...] for r in refs], axis=0) if len(refs) > 1 else refs[0][...]


def expert_forward(blocks, experts, apart, w_gate, w_up, w_down):
    parts = [len(pieces) for pieces in blocks]
    rows = sum(p.shape[0] for p in blocks[0]) - experts
    width, inner = w_gate.shape
    half = rows // 2 if apart else rows
    size = 8 if apart else 7
    step = 256

    def body(stage, w_g, w_u, w_d):
        mine = note_rows(experts, lax.axis_index(EP), 128).astype(BF16)
        places = iter(range(len(flat)))
        for b, count in enumerate(parts):
            block = joined_rows([stage.get(next(places)) for _ in range(count)])
            first = size * b
            rows_o, top_o, gate_o, up_o, hidden_o, weight_o, count_o, *bottom_o = stage.out[first : first + size]
            notes = block[rows:]
            block = block[:rows]
            rows_o[...] = block
            weight = dot_tn(notes[:, :rows], mine) + dot_tn(notes[:, rows : 2 * rows], mine)
            weight_o[...] = weight
            count_o[...] = notes[:, width - 128 :].astype(F32)
            stage.put(first, first + 5, first + 6)
            for f in range(0, inner, step):
                gate_pre = dot(block, w_g[:, f : f + step])
                up_pre = dot(block, w_u[:, f : f + step])
                level, _ = gelu_parts(gate_pre)
                hidden_o[:, f : f + step] = (gate_pre * level * up_pre).astype(BF16)
                gate_o[:, f : f + step] = gate_pre.astype(BF16)
                up_o[:, f : f + step] = up_pre.astype(BF16)
            stage.put(first + 2, first + 3, first + 4)
            hidden = hidden_o[...]
            wide = jnp.concatenate([weight] * (step // 128), axis=1)
            for c in range(0, width, step):
                term = (dot(hidden, w_d[:, c : c + step]) * wide).astype(BF16)
                top_o[:, c : c + step] = term[:half]
                if apart:
                    bottom_o[0][:, c : c + step] = term[half:]
            stage.put(first + 1, *([first + 7] if apart else ()))

    flat = [p for pieces in blocks for p in pieces]
    one = [((rows, width), BF16), ((half, width), BF16)] + [((rows, inner), BF16)] * 3
    one += [((rows, 128), F32), ((experts, 128), F32)] + [((rows - half, width), BF16)] * apart
    flops = len(blocks) * 6 * rows * width * inner
    made = staged(body, flat, one * len(blocks), flops=flops, kept=(w_gate, w_up, w_down), limit=LEAN)
    return [made[size * i : size * i + size] for i in range(len(blocks))]


def expert_backward(blocks, saved, experts, apart, w_gate, w_up, w_down):
    parts = [len(pieces) for pieces in blocks]
    rows, inner = saved[0][0].shape
    width = w_gate.shape[0]
    half = rows // 2
    size = 6 if apart else 5
    step = 256

    def body(stage, w_g, w_u, w_d, *given):
        mine = note_rows(experts, lax.axis_index(EP), width)
        ones = jnp.ones((8, step), BF16)
        at = 0
        for b, count in enumerate(parts):
            places = list(range(at, at + count + 4))
            at += count + 4
            first = size * b
            grads_o, top_o, gate_o, up_o, scaled_o, *bottom_o = stage.out[first : first + size]
            grads = joined_rows([given[i] for i in places[:count]])
            gate_ref, up_ref, hidden_ref, weight_ref = (given[i] for i in places[count:])
            grads_o[...] = grads
            wide = jnp.concatenate([weight_ref[...]] * (step // 128), axis=1)
            sums = jnp.zeros((8, rows), F32)
            for f in range(0, inner, step):
                raw = dot_nt(grads, w_d[f : f + step, :])
                hidden = hidden_ref[:, f : f + step].astype(F32)
                product = raw * hidden
                high = product.astype(BF16)
                sums = sums + dot_nt(ones, high) + dot_nt(ones, (product - high.astype(F32)).astype(BF16))
                scaled_o[:, f : f + step] = (hidden * wide).astype(BF16)
                gate_pre = gate_ref[:, f : f + step].astype(F32)
                level, slope = gelu_parts(gate_pre)
                grad_hidden = raw * wide
                gate_o[:, f : f + step] = (grad_hidden * up_ref[:, f : f + step].astype(F32) * slope).astype(BF16)
                up_o[:, f : f + step] = (grad_hidden * gate_pre * level).astype(BF16)
            high = sums.astype(BF16).astype(F32)
            notes = jnp.concatenate([high, sums - high, jnp.zeros((8, width - 2 * rows), F32)], axis=1)
            notes = (jnp.broadcast_to(notes[:1], (experts, width)) * mine).astype(BF16)
            gate_low, up_low = gate_o[...], up_o[...]
            terms = [
                (dot_nt(gate_low, w_g[c : c + step, :]) + dot_nt(up_low, w_u[c : c + step, :])).astype(BF16)
                for c in range(0, width, step)
            ]
            term = jnp.concatenate(terms, axis=1)
            if apart:
                top_o[...] = term[:half]
                bottom_o[0][...] = jnp.concatenate([term[half:], notes], axis=0)
            else:
                top_o[...] = jnp.concatenate([term, notes], axis=0)

    flat = [p for pieces, kept in zip(blocks, saved) for p in (*pieces, *kept)]
    one = [((rows, width), BF16), ((half if apart else rows + experts, width), BF16)] + [((rows, inner), BF16)] * 3
    one += [((rows - half + experts, width), BF16)] * apart
    flops = len(blocks) * 6 * rows * width * inner
    every = range(size * len(blocks))
    made = staged(body, (), one * len(blocks), flops=flops, kept=(w_gate, w_up, w_down, *flat), limit=LEAN, held=every)
    return [made[size * i : size * i + size] for i in range(len(blocks))]


def attention_forward(tokens, segments, routes, valid, gain_one, gain_two, tables, router, weights):
    rows, width = tokens.shape
    experts = router.shape[1]
    w_query, w_key, w_value, w_out = weights
    half = rows // 2
    groups = H // KVH
    span = groups * HEAD

    def body(stage):
        normed_o, query_o, key_o, value_o, weights_o, context_o, mixed_o, top_o, bottom_o, gates_o = stage.out
        gains = stage.get(1)
        tokens_ref = stage.get(0)
        rows_in = tokens_ref[...].astype(F32)
        inverse = lax.rsqrt(jnp.mean(rows_in * rows_in, axis=1, keepdims=True) + EPSILON)
        normed = (rows_in * inverse * gains[0:1, :].astype(F32)).astype(BF16)
        normed_o[...] = normed
        stage.put(0)
        cos, sin = stage.get(2)[...], stage.get(3)[...]
        keys = dot(normed, stage.get(4)[...])
        for g in range(KVH):
            at = slice(g * HEAD, (g + 1) * HEAD)
            key_o[:, at] = turned(keys[:, at], cos, sin).astype(BF16)
        value_o[...] = dot(normed, stage.get(5)[...]).astype(BF16)
        stage.put(2, 3)
        lower = lax.broadcasted_iota(jnp.int32, (rows, rows), 0) >= lax.broadcasted_iota(jnp.int32, (rows, rows), 1)
        across = jnp.broadcast_to(stage.get(6)[...].astype(F32), (rows, rows))
        allowed = (across == across.T) & lower
        w_q = stage.get(7)
        for g in range(KVH):
            queries = dot(normed, w_q[:, g * span : (g + 1) * span])
            key = key_o[:, g * HEAD : (g + 1) * HEAD]
            value = value_o[:, g * HEAD : (g + 1) * HEAD]
            for i in range(groups):
                h = g * groups + i
                at = slice(h * HEAD, (h + 1) * HEAD)
                query = turned(queries[:, i * HEAD : (i + 1) * HEAD], cos, sin).astype(BF16)
                query_o[:, at] = query
                for first, last in ((0, half), (half, rows)):
                    scores = dot_nt(query[first:last], key[:last]) * HEAD ** (-0.5)
                    scores = jnp.where(allowed[first:last, :last], scores, NEG_FILL)
                    peak = jnp.max(scores, axis=1, keepdims=True)
                    terms = jnp.exp(scores - peak)
                    low = (terms / jnp.sum(terms, axis=1, keepdims=True)).astype(BF16)
                    weights_o[h * rows + first : h * rows + last, :last] = low
                    context_o[first:last, at] = dot(low, value[:last]).astype(BF16)
                weights_o[h * rows : h * rows + half, half:] = jnp.zeros((half, rows - half), BF16)
        stage.put(1, 4, 5)
        w_o = stage.get(8)
        step = width // 3
        for c in range(0, width, step):
            at = slice(c, c + step)
            mixed_o[:, at] = tokens_ref[:, at].astype(F32) + dot(context_o[...], w_o[:, at])
        stage.put(6)
        mixed = mixed_o[...]
        inverse = lax.rsqrt(jnp.mean(mixed * mixed, axis=1, keepdims=True) + EPSILON)
        moe_in = (mixed * inverse * gains[1:2, :].astype(F32)).astype(BF16)
        routes_ref = stage.get(9)
        logits = dot_nt(stage.get(10)[...], moe_in)
        ids = lax.broadcasted_iota(jnp.int32, (experts, rows), 0)
        hot = ids == routes_ref[0:1, :]
        for k in range(1, routes_ref.shape[0]):
            hot = hot | (ids == routes_ref[k : k + 1, :])
        peak = jnp.max(jnp.where(hot, logits, NEG_FILL), axis=0, keepdims=True)
        terms = jnp.where(hot, jnp.exp(jnp.where(hot, logits - peak, 0.0)), 0.0)
        gates = terms / jnp.sum(terms, axis=0, keepdims=True)
        gates_o[...] = gates
        high = gates.astype(BF16).astype(F32)
        count = jnp.sum(stage.get(11)[...].astype(F32), axis=1, keepdims=True)
        counts = jnp.broadcast_to(count, (experts, width - 2 * rows))
        notes = jnp.concatenate([high, gates - high, counts], axis=1).astype(BF16)
        top_o[...] = moe_in[:half]
        bottom_o[...] = jnp.concatenate([moe_in[half:], notes], axis=0)
        stage.put(7, 8, 9)

    ins = (
        tokens,
        jnp.stack([gain_one, gain_two]),
        *tables,
        w_key,
        w_value,
        segments,
        w_query,
        w_out,
        routes.T,
        router.T,
        valid,
    )
    outs = [
        ((rows, width), BF16),
        ((rows, H * HEAD), BF16),
        ((rows, KVH * HEAD), BF16),
        ((rows, KVH * HEAD), BF16),
        ((H * rows, rows), BF16),
        ((rows, H * HEAD), BF16),
        ((rows, width), F32),
        ((half, width), BF16),
        ((rows - half + experts, width), BF16),
        ((experts, rows), F32),
    ]
    return staged(body, ins, outs, flops=2 * rows * width * (2 * width + 4 * KVH * HEAD), first=7)


def mixed_backward(parts, grad_out, mixed, block, gates, router, gain_two):
    rows, width = mixed.shape
    experts = router.shape[1]
    counts = [len(pieces) for pieces in parts]
    n = sum(counts)

    def body(stage, *refs):
        branch_o, mixed_o, gain_o, router_o = stage.out[:4]
        weights = refs[0][...]
        moe_in = joined_rows([refs[5 + i] for i in range(len(block))])
        mixed_rows = refs[3][...]
        inverse = lax.rsqrt(jnp.mean(mixed_rows * mixed_rows, axis=1, keepdims=True) + EPSILON)
        normal = mixed_rows * inverse
        places = iter(range(5 + len(block), 5 + len(block) + n))
        total = 0.0
        for count in counts:
            total = total + joined_rows([refs[next(places)] for _ in range(count)]).astype(F32)
        notes = total[rows : rows + experts]
        grad_gates = notes[:, :rows] + notes[:, rows : 2 * rows]
        chosen = weights * (grad_gates - jnp.sum(weights * grad_gates, axis=0, keepdims=True))
        logits = chosen.astype(BF16)
        router_o[...] = dot(logits, moe_in[:rows])
        grad_in = total[:rows] + dot_tn(logits, refs[1][...])
        gain_o[...] = jnp.sum(grad_in * normal, axis=0, keepdims=True)
        scaled = grad_in * refs[2][...].astype(F32)
        inner = jnp.mean(scaled * normal, axis=1, keepdims=True)
        grad_mixed = refs[4][...] + inverse * (scaled - normal * inner)
        branch_o[...] = grad_mixed.astype(BF16)
        mixed_o[...] = grad_mixed
        send_shares(stage, branch_o, 4)
        stage.put(0, 1, 2, 3)

    ins = (gates, router.T, gain_two[None], mixed, grad_out, *block, *(p for pieces in parts for p in pieces))
    outs = [((rows, width), BF16), ((rows, width), F32), ((1, width), F32), ((experts, width), F32)]
    outs += shares_shape(rows, width)
    made = staged(body, (), outs, kept=ins, limit=LEAN, straight=range(4, len(outs)))
    return made[:4], made[4:]


def attention_backward(branch, weights, query, key, value, tables, w_out):
    rows = branch.shape[0]
    groups = H // KVH
    span = groups * HEAD
    scale = HEAD ** (-0.5)

    def body(stage):
        qkv_o = stage.out[0]
        grad_branch = stage.get(0)[...]
        for g in range(KVH):
            w_o = stage.get((1, 8)[g])
            grad_context = dot_nt(grad_branch, w_o[...]).astype(BF16)
            key_ref, value_ref = stage.get(2), stage.get(3)
            k = key_ref[:, g * HEAD : (g + 1) * HEAD]
            v = value_ref[:, g * HEAD : (g + 1) * HEAD]
            grad_key = jnp.zeros((rows, HEAD), F32)
            grad_value = jnp.zeros((rows, HEAD), F32)
            query_ref, low_ref = stage.get(4), stage.get((5, 9)[g])
            cos, sin = stage.get(6)[...], -stage.get(7)[...]
            for i in range(groups):
                h = g * groups + i
                q = query_ref[:, h * HEAD : (h + 1) * HEAD]
                grad = grad_context[:, i * HEAD : (i + 1) * HEAD]
                low = low_ref[i * rows : (i + 1) * rows, :]
                grads = dot_nt(grad, v)
                full = low.astype(F32)
                product = full * grads
                scores = (product - full * jnp.sum(product, axis=1, keepdims=True)).astype(BF16)
                grad_query = dot(scores, k) * scale
                qkv_o[:, h * HEAD : (h + 1) * HEAD] = turned(grad_query, cos, sin).astype(BF16)
                grad_key = grad_key + dot_tn(scores, q)
                grad_value = grad_value + dot_tn(low, grad)
            at = (H + g) * HEAD
            qkv_o[:, at : at + HEAD] = turned(grad_key * scale, cos, sin).astype(BF16)
            at += KVH * HEAD
            qkv_o[:, at : at + HEAD] = grad_value.astype(BF16)
        send_shares(stage, qkv_o, 1)
        stage.put(0)

    heads = groups * rows
    ins = (
        branch,
        (w_out, 0, span),
        key,
        value,
        query,
        (weights, 0, heads),
        *tables,
        (w_out, span, span),
        (weights, heads, heads),
    )
    columns = (H + 2 * KVH) * HEAD
    outs = [((rows, columns), BF16)] + shares_shape(rows, columns)
    made = staged(body, ins, outs, first=2, straight=range(1, len(outs)), limit=60)
    return made[0], made[1:]


def weight_grads(ring, early, late):
    columns, width = early[0].shape[1], late[0].shape[1]
    share = columns // ring.size
    step = 256

    def body(stage):
        total = stage.room[0]
        early_refs = [stage.get(i) for i in range(0, 2 * len(late), 2)]
        late_refs = [stage.get(i) for i in range(1, 2 * len(late), 2)]
        for c in range(0, columns, step):
            made = 0.0
            for a, b in zip(early_refs, late_refs):
                made = made + dot_tn(a[:, c : c + step], b[...])
            total[c : c + step, :] = made.astype(BF16)
        for j in range(ring.size):
            start = pl.multiple_of(ring.owner(j) * share, 16)
            stage.send(total.at[pl.ds(start, share)], j)

    ins = [p for pair in zip(early, late) for p in pair]
    outs = [((share, width), BF16)] * ring.size
    every = range(len(outs))
    return staged(body, ins, outs, straight=every, held=every, room=[((columns, width), BF16)], limit=LEAN)


def token_backward(qkv, tokens, grad_mixed, gain_one, weights):
    rows, width = tokens.shape
    w_query, w_key, w_value, _ = weights
    at, span = H * HEAD, KVH * HEAD

    def body(stage):
        tokens_o, gain_o = stage.out
        qkv_ref = stage.get(0)
        rows_in = stage.get(1)[...].astype(F32)
        inverse = lax.rsqrt(jnp.mean(rows_in * rows_in, axis=1, keepdims=True) + EPSILON)
        normal = rows_in * inverse
        grads = dot_nt(qkv_ref[:, at : at + span], stage.get(2)[...])
        grads = grads + dot_nt(qkv_ref[:, at + span :], stage.get(3)[...])
        grads = grads + dot_nt(qkv_ref[:, :at], stage.get(4)[...])
        gain_o[...] = jnp.sum(grads * normal, axis=0, keepdims=True)
        scaled = grads * stage.get(5)[...].astype(F32)
        inner = jnp.mean(scaled * normal, axis=1, keepdims=True)
        tokens_o[...] = stage.get(6)[...] + inverse * (scaled - normal * inner)
        stage.put(0, 1)

    ins = (qkv, tokens, w_key, w_value, w_query, gain_one[None], grad_mixed)
    return staged(body, ins, [((rows, width), F32), ((1, width), F32)], limit=LEAN + 10)


def after(value, first):
    return lax.optimization_barrier((value, first))[0]


def rep_pairs(k):
    size = lax.axis_size(("x", "c"))
    return [(i, i ^ k) for i in range(size)]


def x_gather(a):
    size = lax.axis_size("x")
    return [a] + [lax.ppermute(a, "x", [(i, i ^ k) for i in range(size)]) for k in range(1, size)]


def core_gather(blocks):
    return [b for a in blocks for b in (a, lax.ppermute(a, "c", [(0, 1), (1, 0)]))]


def rep_gather(a):
    return core_gather(x_gather(a))


def rep_spread(parts):
    return [lax.ppermute(p, ("x", "c"), rep_pairs(k)) if k else p for k, p in enumerate(parts)]


def rep_parts(a):
    size = lax.axis_size(("x", "c"))
    share = a.shape[1] // size
    return [lax.dynamic_slice_in_dim(a, (rep_index() ^ k) * share, share, 1) for k in range(size)]


def rep_columns(blocks):
    step = 1
    while step < len(blocks):
        swap = (rep_index() & step) != 0
        blocks = [jnp.where(swap, blocks[i ^ step], blocks[i]) for i in range(len(blocks))]
        step *= 2
    return jnp.concatenate(blocks, axis=1).astype(F32)


def shards(
    ring,
    tokens,
    segments,
    routes,
    valid_mask,
    teacher,
    gain_one,
    w_query,
    w_key,
    w_value,
    w_out,
    gain_two,
    router,
    w_gate,
    w_up,
    w_down,
):
    length, width = tokens.shape
    experts_all = router.shape[1]
    tokens_all = length * lax.axis_size(ALL)
    w_gate, w_up, w_down = w_gate[0], w_up[0], w_down[0]
    valid_rows = valid_mask.reshape(length).astype(F32)
    tables = rope_tables(length)
    attn = (w_query, w_key, w_value, w_out)
    normed_low, query, key, value, weights_low, context, mixed_rows, *block, gates = attention_forward(
        tokens, segments, routes, valid_mask, gain_one, gain_two, tables, router, attn
    )
    form = RingExperts if ring.size <= RING_LIMIT else SlotExperts
    experts = form(ring, block, gates, routes.shape[1], w_gate, w_up, w_down)
    gathered = {}

    def gather_beside(step, sent):
        if step == 0:
            gathered["normed"] = x_gather(after(normed_low, sent))
        if step == 2:
            gathered["normed"] = core_gather(after(gathered["normed"], sent))
        return gathered["normed"] if step % 2 else ()

    def beside(step, sent):
        if step == 0:
            gathered["count"] = butterfly_sum(experts.count, ("c", "x"))
        if step == 1:
            gathered["context"] = x_gather(after(context, (sent, gathered["count"])))
        if step == 3:
            gathered["context"] = core_gather(after(gathered["context"], sent))
        return gathered["count"] if step == 1 else ()

    moe_parts = experts.forward(gather_beside, beside)
    if not gathered:
        gathered = {"normed": rep_gather(normed_low), "context": rep_gather(context)}
        gathered["count"] = butterfly_sum(experts.count, ("c", "x"))
    count_total = gathered["count"][0, 0]
    moe_out = added(moe_parts)
    output_rows = mixed_rows + moe_out
    residual_gap = output_rows - teacher.astype(F32)
    numerator = jnp.sum(valid_rows * jnp.sum(residual_gap * residual_gap, axis=-1))
    grad_out = 2.0 * tokens_all / count_total * valid_rows[:, None] * residual_gap

    grad_out, gathered, numerator = lax.optimization_barrier((grad_out, gathered, numerator))
    back_parts, sums = experts.backward(grad_out)
    (grad_branch, grad_mixed, grad_gain_two, grad_router), branch_parts = mixed_backward(
        after(back_parts, [each.got for each in sums]), grad_out, mixed_rows, block, gates, router, gain_two
    )
    branch_spread = rep_spread(branch_parts or rep_parts(grad_branch))
    grad_qkv, qkv_parts = attention_backward(
        grad_branch, weights_low, query, key, value, tables, w_out
    )
    qkv_spread = rep_spread(qkv_parts or rep_parts(grad_qkv))
    out_sum = RingSum(ring, weight_grads(ring, gathered["context"], after(branch_spread, grad_qkv)))
    grad_w_qkv = weight_grads(ring, gathered["normed"], after(qkv_spread, out_sum.sent))
    out_sum.step(grad_w_qkv[0])
    qkv_sum = RingSum(ring, grad_w_qkv)
    grad_tokens, grad_gain_one = token_backward(
        after(grad_qkv, qkv_sum.sent), tokens, grad_mixed, gain_one, attn
    )
    small = jnp.concatenate(
        [grad_router.reshape(-1), grad_gain_two[0], grad_gain_one[0], jnp.full((128,), numerator)]
    ).reshape(-1, 128)
    hops = butterfly_hops(("c", "x", "y", "z"))
    out_blocks = None
    first = grad_tokens
    while qkv_sum.left > 1:
        if out_sum.left > 1:
            out_sum.step(qkv_sum.sent)
        elif out_blocks is None:
            out_blocks = rep_gather(out_sum.total(qkv_sum.sent))
        got = None
        if len(hops) > 1:
            small, got = butterfly_hop(small, hops.pop(0), qkv_sum.sent)
        qkv_sum.step((out_sum.sent, first))
        first = ()
        if got is not None:
            small = small + after(got, qkv_sum.sent)
    if out_blocks is None:
        while out_sum.left > 1:
            out_sum.step(qkv_sum.sent)
        out_blocks = rep_gather(out_sum.total(qkv_sum.sent))
    small, got = butterfly_hop(small, hops.pop(0), qkv_sum.sent)
    qkv_blocks = rep_gather(qkv_sum.total(()))
    small = small + after(got, qkv_blocks[0])
    shares = [each.result(qkv_blocks[0])[0] for each in sums]
    out_share = rep_columns(after(out_blocks, qkv_blocks[0]))
    for hop in hops:
        small, got = butterfly_hop(small, hop, ())
        small = small + got
    flat = small.reshape(-1)
    at = width * experts_all
    router_share = flat[:at].reshape(experts_all, width).T
    gain_shares = (flat[at + width : at + 2 * width], flat[at : at + width])
    loss_value = flat[at + 2 * width] / count_total
    qkv_share = rep_columns(after(qkv_blocks, (shares, out_share, router_share, gain_shares, loss_value)))
    return (
        output_rows.astype(BF16),
        loss_value,
        grad_tokens,
        gain_shares[0],
        qkv_share[:, : H * HEAD],
        qkv_share[:, H * HEAD : (H + KVH) * HEAD],
        qkv_share[:, (H + KVH) * HEAD :],
        out_share,
        gain_shares[1],
        router_share,
        shares[0],
        shares[1],
        shares[2],
    )


def solution(mesh):
    rep, ep = mesh.shape["rep"], mesh.shape["ep"]
    x_size = rep // 2
    y_size = x_size if ep % x_size == 0 else 1
    grid = Mesh(mesh.devices.reshape(x_size, 2, ep // y_size, y_size), ALL)
    rows = P(ALL, None)
    whole = P()
    expert = P(EP, None, None)
    return jax.shard_map(
        functools.partial(shards, Ring(ep // y_size, y_size)),
        mesh=grid,
        in_specs=(rows,) * 5 + (whole,) * 7 + (expert,) * 3,
        out_specs=(rows, whole, rows, whole)
        + (P(EP, None),) * 4
        + (whole, whole)
        + (P(EP, ("x", "c"), None),) * 3,
        check_vma=False,
    )
```

```python
import functools
import math

import jax
import jax.numpy as jnp
import numpy as np
from jax import lax
from jax.experimental import pallas as pl
from jax.experimental.pallas import tpu as pltpu
from jax.sharding import Mesh
from jax.sharding import PartitionSpec as P

H = 12
KVH = 2
HEAD = 128

EPSILON = 1e-06
ROPE_BASE = 10000.0
NEG_FILL = -1e30
ALL = ("x", "c", "z", "y")
EP = ("z", "y")
F32 = jnp.float32
BF16 = jnp.bfloat16
RING_LIMIT = 16
SPLIT = True
LEAN = 20


def dot(a, b, dims=((1,), (0,))):
    return lax.dot_general(a, b, (dims, ((), ())), preferred_element_type=F32)


def dot_nt(a, b):
    return dot(a, b, ((1,), (1,)))


def dot_tn(a, b):
    return dot(a, b, ((0,), (0,)))


def activate(gate_pre, up_pre):
    return jax.nn.gelu(gate_pre, approximate=True) * up_pre


class Ring:
    def __init__(self, z_size, y_size):
        cycle = [(z, 0) for z in range(z_size)]
        for step, z in enumerate(reversed(range(z_size))):
            rest = list(range(1, y_size))
            cycle += [(z, y) for y in (rest if step % 2 == 0 else rest[::-1])]
        self.order = [z * y_size + y for z, y in cycle]
        self.size = len(self.order)
        self.half = self.size // 2
        n = self.size
        self.forward = [(self.order[i], self.order[(i + 1) % n]) for i in range(n)]
        self.backward = [(b, a) for a, b in self.forward]
        self.place = [self.order.index(e) for e in range(n)]

    def fwd(self, a):
        return lax.ppermute(a, EP, self.forward)

    def bwd(self, a):
        return lax.ppermute(a, EP, self.backward)

    def owner(self, j):
        me = lax.axis_index(EP)
        found = 0
        for e, place in enumerate(self.place):
            found = found + jnp.where(me == e, self.order[(place - j) % self.size], 0)
        return found

    def pair(self, s):
        return sorted({s, (self.size - s) % self.size})

    def gather(self, pieces, use, lag, beside=lambda step, sent: ()):
        ahead = behind = list(pieces) if SPLIT else [jnp.concatenate(pieces, axis=0)]
        cut = pieces[0].shape[0]
        ready = {0: ahead}
        open_steps = [0]
        for s in range(1, self.half + 1):
            sent = (ahead, behind)
            if s == self.half and SPLIT:
                ahead, behind = ahead[:1], behind[1:]
            elif s == self.half:
                ahead, behind = [ahead[0][:cut]], [behind[0][cut:]]
            ahead, behind = [self.fwd(p) for p in ahead], [self.bwd(p) for p in behind]
            made = [beside(s - 1, sent)]
            while open_steps and open_steps[0] + lag <= s - 1:
                step = open_steps.pop(0)
                made.append(use({j: after(ready[j], sent) if lag else ready[j] for j in self.pair(step)}))
            ahead[0], behind[0], _ = lax.optimization_barrier((ahead[0], behind[0], made))
            if s < self.half:
                ready[s], ready[self.size - s] = list(ahead), list(behind)
                open_steps.append(s)
        made = use({self.half: ahead + behind})
        for step in reversed(open_steps):
            use({j: after(ready[j], made) for j in self.pair(step)})

    def scatter_sum(self, terms, beside=lambda step, sent: ()):
        def add(a, b):
            return (a.astype(F32) + b.astype(F32)).astype(BF16)

        far, (near,), (away,) = terms(self.half), terms(self.half - 1), terms(self.half + 1)
        cut = far[0].shape[0]
        down, up = self.bwd(far[0]), self.fwd(far[1])
        down, up, _ = lax.optimization_barrier((down, up, beside(0, far)))
        down = [jnp.concatenate([add(near[:cut], down), near[cut:]], axis=0)]
        up = [jnp.concatenate([away[:cut], add(away[cut:], up)], axis=0)]
        for s in range(self.half - 1, 0, -1):
            sent = (down, up)
            down, up = [self.bwd(p) for p in down], [self.fwd(p) for p in up]
            down[0], up[0], _ = lax.optimization_barrier((down[0], up[0], beside(self.half - s, sent)))
            if s > 1:
                down = [add(a, b) for a, b in zip(down, terms(s - 1))]
                up = [add(a, b) for a, b in zip(up, terms(self.size - s + 1))]
        return down, up, terms(0)


class RingSum:
    def __init__(self, ring, terms):
        self.ring, self.terms, self.left = ring, terms, ring.half
        cut = terms[0].shape[0] // 32 * 16
        self.cut = cut
        far = terms[ring.half]
        self.sent = far
        self.down, self.up = ring.bwd(far[:cut]), ring.fwd(far[cut:])

    def arrive(self, tie):
        self.down, self.up, _ = lax.optimization_barrier((self.down, self.up, tie))

    def step(self, tie):
        ring, cut = self.ring, self.cut
        self.arrive(tie)
        self.left -= 1

        def add(a, b):
            return (a.astype(F32) + b.astype(F32)).astype(BF16)

        near, away = self.terms[self.left], self.terms[ring.size - self.left]
        if self.left == ring.half - 1:
            down = jnp.concatenate([add(near[:cut], self.down), near[cut:]], axis=0)
            up = jnp.concatenate([away[:cut], add(away[cut:], self.up)], axis=0)
        else:
            down, up = add(near, self.down), add(away, self.up)
        self.sent = (down, up)
        self.down, self.up = ring.bwd(down), ring.fwd(up)

    def total(self, tie):
        self.arrive(tie)
        return (self.down.astype(F32) + self.up.astype(F32) + self.terms[0].astype(F32)).astype(BF16)


def butterfly_hops(axes):
    return [(axis, step) for axis in axes for step in (1, 2, 4, 8, 16) if step < lax.axis_size(axis)]


def butterfly_hop(a, hop, tie):
    axis, step = hop
    a, _ = lax.optimization_barrier((a, tie))
    return a, lax.ppermute(a, axis, [(i, i ^ step) for i in range(lax.axis_size(axis))])


def added(lists):
    return sum(jnp.concatenate(pieces, axis=0).astype(F32) for pieces in lists)


def butterfly_sum(a, axes):
    for axis in axes:
        size = lax.axis_size(axis)
        step = 1
        while step < size:
            a = a + lax.ppermute(a, axis, [(i, i ^ step) for i in range(size)])
            step *= 2
    return a


class Sum:
    def __init__(self, a):
        self.a = a

    @staticmethod
    def send(a, axis, dim):
        size = lax.axis_size(axis)
        if size != 2:
            got = lax.psum_scatter(a, axis, scatter_dimension=dim, tiled=True)
            return jnp.zeros_like(got), got
        first = lax.axis_index(axis) == 0
        low, high = lax.slice_in_dim(a, 0, 1, axis=dim), lax.slice_in_dim(a, 1, 2, axis=dim)
        return jnp.where(first, low, high), lax.ppermute(jnp.where(first, high, low), axis, [(0, 1), (1, 0)])

    def over_cores(self, tie):
        self.mine, self.got = self.send(after(self.a, tie), "c", 1)

    def over_x(self, tie):
        mine, got = self.mine, after(self.got, tie)
        both = (mine.astype(F32) + got.astype(F32)).astype(BF16)
        self.mine, self.got = self.send(both, "x", 0)
        return both

    def result(self, tie):
        got = after(self.got, tie)
        return self.mine.astype(F32) + got.astype(F32)


class RingExperts:
    def __init__(self, ring, block, gates, top, w_gate, w_up, w_down):
        self.ring, self.block = ring, list(block)
        self.experts, self.rows = gates.shape
        self.weights = (w_gate, w_up, w_down)
        self.cut = self.rows // 2

    def forward(self, gather_beside, beside):
        self.rows_in, self.saved = {}, {}
        terms, counts = {}, {}

        def use(blocks):
            apart = self.ring.half in blocks
            made = expert_forward(list(blocks.values()), self.experts, apart, *self.weights)
            for j, (rows, top, gate_pre, up_pre, hidden, weight, count, *bottom) in zip(blocks, made):
                self.rows_in[j], terms[j], counts[j] = rows, [top, *bottom], count
                self.saved[j] = (gate_pre, up_pre, hidden, weight)
            return made

        self.ring.gather(self.block, use, 1, gather_beside)
        self.count = sum(counts[j] for j in range(self.ring.size))
        return self.ring.scatter_sum(terms.get, beside)

    def backward(self, low, gather_beside):
        grads_in, gate_lows, up_lows, scaled, terms = {}, {}, {}, {}, {}

        def use(blocks):
            saved = [self.saved[j] for j in blocks]
            apart = self.ring.half in blocks
            made = expert_backward(list(blocks.values()), saved, self.experts, apart, *self.weights)
            for j, (grads, top, gate_low, up_low, part, *bottom) in zip(blocks, made):
                grads_in[j], gate_lows[j], up_lows[j], scaled[j] = grads, gate_low, up_low, part
                terms[j] = [top, *bottom]
            return made

        self.ring.gather([low[: self.cut], low[self.cut :]], use, 0, gather_beside)
        sums = []

        def joined(parts):
            return jnp.concatenate([parts[j] for j in range(self.ring.size)], axis=0)

        def beside(step, sent):
            made = []
            if step == 0:
                self.joined = after(joined(self.rows_in), sent)
                sums.append(expert_sum(self.joined, joined(after(gate_lows, sent))))
            if step == 1:
                sums.append(expert_sum(self.joined, joined(after(up_lows, sent))))
            if step == 2:
                sums.append(expert_sum(joined(after(scaled, sent)), joined(after(grads_in, sent))))
                made.append(sums[0].got)
            if step == 3:
                made.append(sums[1].got)
            if step > 0:
                made.append(sums[step - 1].over_x(sent))
            if step < 3:
                made.append(sums[step].a)
                sums[step].over_cores(sums[step].a)
            return made

        return self.ring.scatter_sum(terms.get, beside), sums


def expert_sum(a, b):
    product = dot_tn(a, b).astype(BF16)
    return Sum(product.reshape(lax.axis_size("x"), lax.axis_size("c"), -1, product.shape[1]))


class SlotExperts:
    def __init__(self, ring, block, gates, top, w_gate, w_up, w_down):
        experts, rows = gates.shape
        block = jnp.concatenate(block, axis=0)
        moe_in, route_hot = block[:rows], gates.T > 0
        self.count_here = jnp.full((8, 128), block[rows, -1].astype(F32))
        self.slots = 3 * rows * top // (2 * experts)
        self.group = ring.size
        self.moe_in, self.weights = moe_in, (w_gate, w_up, w_down)
        places = jnp.arange(rows)
        earlier = (places[:, None] > places[None, :]).astype(BF16)
        rank = dot(earlier, route_hot.astype(BF16)).T[:, None, :]
        slot = jnp.arange(self.slots, dtype=F32)[None, :, None]
        picks = ((rank == slot) & route_hot.T[:, None, :]).reshape(experts * self.slots, rows)
        self.picks = picks.astype(BF16)
        self.slot_gate = jnp.where(picks, jnp.repeat(gates, self.slots, axis=0), 0.0)

    def swap(self, rows):
        blocks = rows.reshape(self.group, -1, rows.shape[1])
        return lax.all_to_all(blocks, EP, 0, 0, tiled=True).reshape(rows.shape)

    def forward(self, gather_beside, beside):
        w_gate, w_up, w_down = self.weights
        self.arrived = self.swap(dot(self.picks, self.moe_in).astype(BF16))
        self.gate_pre = dot(self.arrived, w_gate)
        self.up_pre = dot(self.arrived, w_up)
        self.hidden = activate(self.gate_pre, self.up_pre).astype(BF16)
        self.returned = self.swap(dot(self.hidden, w_down).astype(BF16))
        self.count = butterfly_sum(self.count_here, ("y", "z"))
        return [[jnp.dot(self.slot_gate.T, self.returned.astype(F32), precision=lax.Precision.HIGHEST)]]

    def backward(self, grad_low, gather_beside):
        w_gate, w_up, w_down = self.weights
        rows, experts = grad_low.shape[0], self.picks.shape[0] // self.slots
        products = dot_nt(grad_low, self.returned) * self.picks.T.astype(F32)
        grad_gates = jnp.sum(products.reshape(rows, experts, self.slots), axis=2)
        slot_gate = jnp.sum(self.slot_gate, axis=1, keepdims=True)
        grads_in = self.swap((dot(self.picks, grad_low) * slot_gate).astype(BF16))
        _, pull = jax.vjp(activate, self.gate_pre, self.up_pre)
        grad_gate, grad_up = pull(dot_nt(grads_in, w_down))
        gate_low, up_low = grad_gate.astype(BF16), grad_up.astype(BF16)
        back = self.swap((dot_nt(gate_low, w_gate) + dot_nt(up_low, w_up)).astype(BF16))
        sums = [
            expert_sum(self.arrived, gate_low),
            expert_sum(self.arrived, up_low),
            expert_sum(self.hidden, grads_in),
        ]
        for each in sums:
            each.over_cores(each.a)
        for each in sums:
            each.over_x(each.a)
        notes = jnp.pad(grad_gates.T, ((0, 0), (0, grad_low.shape[1] - rows)))
        return [[jnp.concatenate([dot_tn(self.picks, back), notes], axis=0)]], sums


def rope_tables(length):
    half = HEAD // 2
    frequency = ROPE_BASE ** (-np.arange(half, dtype=np.float64) / half)
    angles = np.arange(length, dtype=np.float64)[:, None] * frequency[None, :]
    cosine, sine = np.cos(angles), np.sin(angles)
    pairs = np.concatenate([cosine, cosine], axis=1), np.concatenate([-sine, sine], axis=1)
    return tuple(jnp.asarray(p, F32) for p in pairs)


def turned(values, cosine, sine):
    return values * cosine + pltpu.roll(values, HEAD // 2, 1) * sine


class Stage:
    def __init__(self, slices, outs, first, refs):
        n, m = len(slices), len(outs)
        self.there, self.out_there, refs = refs[:n], refs[n : n + m], refs[n + m :]
        self.here, self.out, in_sems, out_sems = refs[:n], refs[n : n + m], refs[n + m], refs[n + m + 1]
        self.out_sems = out_sems
        self.later = []
        self.coming = {}
        for i, rows in enumerate(slices):
            source = self.there[i] if rows is None else self.there[i].at[pl.ds(*rows)]
            self.coming[i] = pltpu.make_async_copy(source, self.here[i], in_sems.at[i])
            if i < first:
                self.coming[i].start()
            else:
                self.later.append(self.coming[i])
        self.leaving = []

    def get(self, i):
        if i in self.coming:
            self.coming.pop(i).wait()
        for copy in self.later:
            copy.start()
        self.later = []
        return self.here[i]

    def put(self, *which):
        for i in which:
            self.send(self.out[i], i)

    def send(self, source, i):
        self.leaving.append(pltpu.make_async_copy(source, self.out_there[i], self.out_sems.at[i]))
        self.leaving[-1].start()

    def finish(self):
        for copy in self.leaving:
            copy.wait()


def staged(body, ins, outs, scalars=(), flops=0, kept=(), limit=60, first=None, straight=(), room=(), held=()):
    arrays = [a if isinstance(a, jax.Array) else a[0] for a in ins]
    slices = [None if isinstance(a, jax.Array) else a[1:] for a in ins]
    sizes = [a.shape if s is None else (s[1], *a.shape[1:]) for a, s in zip(arrays, slices)]
    start = len(ins) if first is None else first
    tile = ((8, 128), BF16)

    def kernel(*refs):
        count = len(scalars) + len(kept)
        stage = Stage(slices, outs, start, refs[count : len(refs) - len(room)])
        stage.out = [there if i in held else o for i, (there, o) in enumerate(zip(stage.out_there, stage.out))]
        stage.room = refs[len(refs) - len(room) :]
        body(stage, *refs[:count])
        stage.finish()

    any_place = pl.BlockSpec(memory_space=pltpu.HBM)
    vmem = [pltpu.VMEM(*(tile if i in straight or i in held else o)) for i, o in enumerate(outs)]
    out_places = [on_chip(1)[0] if i in held else any_place for i in range(len(outs))]
    return pl.pallas_call(
        kernel,
        out_shape=[jax.ShapeDtypeStruct(s, d) if i in held else pltpu.HBM(s, d) for i, (s, d) in enumerate(outs)],
        in_specs=[pl.BlockSpec(memory_space=pltpu.SMEM)] * len(scalars) + on_chip(len(kept)) + [any_place] * len(ins),
        out_specs=out_places,
        scratch_shapes=[pltpu.VMEM(s, a.dtype) for s, a in zip(sizes, arrays)]
        + vmem
        + [pltpu.SemaphoreType.DMA((max(len(ins), 1),)), pltpu.SemaphoreType.DMA((len(outs),))]
        + [pltpu.VMEM(*r) for r in room],
        compiler_params=pltpu.CompilerParams(vmem_limit_bytes=limit << 20),
        cost_estimate=pl.CostEstimate(flops=int(flops), bytes_accessed=0, transcendentals=0),
    )(*scalars, *kept, *(pltpu.with_memory_space_constraint(a, pltpu.HBM) for a in arrays))


def on_chip(count):
    return [pl.BlockSpec(memory_space=pltpu.VMEM)] * count


def rep_index():
    return lax.axis_index("x") * lax.axis_size("c") + lax.axis_index("c")


def rep_shares(columns):
    size = lax.axis_size(("x", "c"))
    return size if columns % (128 * size) == 0 else 0


def send_shares(stage, source, at):
    count = rep_shares(source.shape[1])
    share = source.shape[1] // max(count, 1)
    me = rep_index()
    for k in range(count):
        start = pl.multiple_of((me ^ k) * share, 128)
        stage.send(source.at[:, pl.ds(start, share)], at + k)


def shares_shape(rows, columns):
    count = rep_shares(columns)
    return [((rows, columns // max(count, 1)), BF16)] * count


def gelu_parts(values):
    c = math.sqrt(2.0 / math.pi)
    square = values * values
    level = 0.5 + 0.5 * jnp.tanh(c * values * (1.0 + 0.044715 * square))
    slope = level + 2.0 * c * values * level * (1.0 - level) * (1.0 + 3 * 0.044715 * square)
    return level, slope


def note_rows(experts, expert, columns):
    rows = lax.broadcasted_iota(jnp.int32, (experts, columns), 0)
    return (rows == expert).astype(F32)


def joined_rows(refs):
    return jnp.concatenate([r[...] for r in refs], axis=0) if len(refs) > 1 else refs[0][...]


def expert_forward(blocks, experts, apart, w_gate, w_up, w_down):
    parts = [len(pieces) for pieces in blocks]
    rows = sum(p.shape[0] for p in blocks[0]) - experts
    width, inner = w_gate.shape
    half = rows // 2 if apart else rows
    size = 8 if apart else 7
    step = 256

    def body(stage, w_g, w_u, w_d):
        mine = note_rows(experts, lax.axis_index(EP), 128).astype(BF16)
        places = iter(range(len(flat)))
        for b, count in enumerate(parts):
            block = joined_rows([stage.get(next(places)) for _ in range(count)])
            first = size * b
            rows_o, top_o, gate_o, up_o, hidden_o, weight_o, count_o, *bottom_o = stage.out[first : first + size]
            notes = block[rows:]
            block = block[:rows]
            rows_o[...] = block
            weight = dot_tn(notes[:, :rows], mine) + dot_tn(notes[:, rows : 2 * rows], mine)
            weight_o[...] = weight
            count_o[...] = notes[:, width - 128 :].astype(F32)
            stage.put(first, first + 5, first + 6)
            for f in range(0, inner, step):
                gate_pre = dot(block, w_g[:, f : f + step])
                up_pre = dot(block, w_u[:, f : f + step])
                level, _ = gelu_parts(gate_pre)
                hidden_o[:, f : f + step] = (gate_pre * level * up_pre).astype(BF16)
                gate_o[:, f : f + step] = gate_pre.astype(BF16)
                up_o[:, f : f + step] = up_pre.astype(BF16)
            stage.put(first + 2, first + 3, first + 4)
            hidden = hidden_o[...]
            wide = jnp.concatenate([weight] * (step // 128), axis=1)
            for c in range(0, width, step):
                term = (dot(hidden, w_d[:, c : c + step]) * wide).astype(BF16)
                top_o[:, c : c + step] = term[:half]
                if apart:
                    bottom_o[0][:, c : c + step] = term[half:]
            stage.put(first + 1, *([first + 7] if apart else ()))

    flat = [p for pieces in blocks for p in pieces]
    one = [((rows, width), BF16), ((half, width), BF16)] + [((rows, inner), BF16)] * 3
    one += [((rows, 128), F32), ((experts, 128), F32)] + [((rows - half, width), BF16)] * apart
    flops = len(blocks) * 6 * rows * width * inner
    made = staged(body, flat, one * len(blocks), flops=flops, kept=(w_gate, w_up, w_down), limit=LEAN)
    return [made[size * i : size * i + size] for i in range(len(blocks))]


def expert_backward(blocks, saved, experts, apart, w_gate, w_up, w_down):
    parts = [len(pieces) for pieces in blocks]
    rows, inner = saved[0][0].shape
    width = w_gate.shape[0]
    half = rows // 2
    size = 6 if apart else 5
    step = 256

    def body(stage, w_g, w_u, w_d, *given):
        mine = note_rows(experts, lax.axis_index(EP), width)
        ones = jnp.ones((8, step), BF16)
        at = 0
        for b, count in enumerate(parts):
            places = list(range(at, at + count + 4))
            at += count + 4
            first = size * b
            grads_o, top_o, gate_o, up_o, scaled_o, *bottom_o = stage.out[first : first + size]
            grads = joined_rows([given[i] for i in places[:count]])
            gate_ref, up_ref, hidden_ref, weight_ref = (given[i] for i in places[count:])
            grads_o[...] = grads
            wide = jnp.concatenate([weight_ref[...]] * (step // 128), axis=1)
            sums = jnp.zeros((8, rows), F32)
            for f in range(0, inner, step):
                raw = dot_nt(grads, w_d[f : f + step, :])
                hidden = hidden_ref[:, f : f + step].astype(F32)
                product = raw * hidden
                high = product.astype(BF16)
                sums = sums + dot_nt(ones, high) + dot_nt(ones, (product - high.astype(F32)).astype(BF16))
                scaled_o[:, f : f + step] = (hidden * wide).astype(BF16)
                gate_pre = gate_ref[:, f : f + step].astype(F32)
                level, slope = gelu_parts(gate_pre)
                grad_hidden = raw * wide
                gate_o[:, f : f + step] = (grad_hidden * up_ref[:, f : f + step].astype(F32) * slope).astype(BF16)
                up_o[:, f : f + step] = (grad_hidden * gate_pre * level).astype(BF16)
            high = sums.astype(BF16).astype(F32)
            notes = jnp.concatenate([high, sums - high, jnp.zeros((8, width - 2 * rows), F32)], axis=1)
            notes = (jnp.broadcast_to(notes[:1], (experts, width)) * mine).astype(BF16)
            gate_low, up_low = gate_o[...], up_o[...]
            terms = [
                (dot_nt(gate_low, w_g[c : c + step, :]) + dot_nt(up_low, w_u[c : c + step, :])).astype(BF16)
                for c in range(0, width, step)
            ]
            term = jnp.concatenate(terms, axis=1)
            if apart:
                top_o[...] = term[:half]
                bottom_o[0][...] = jnp.concatenate([term[half:], notes], axis=0)
            else:
                top_o[...] = jnp.concatenate([term, notes], axis=0)

    flat = [p for pieces, kept in zip(blocks, saved) for p in (*pieces, *kept)]
    one = [((rows, width), BF16), ((half if apart else rows + experts, width), BF16)] + [((rows, inner), BF16)] * 3
    one += [((rows - half + experts, width), BF16)] * apart
    flops = len(blocks) * 6 * rows * width * inner
    every = range(size * len(blocks))
    made = staged(body, (), one * len(blocks), flops=flops, kept=(w_gate, w_up, w_down, *flat), limit=LEAN, held=every)
    return [made[size * i : size * i + size] for i in range(len(blocks))]


def attention_forward(tokens, segments, routes, valid, gain_one, gain_two, tables, router, weights):
    rows, width = tokens.shape
    experts = router.shape[1]
    w_query, w_key, w_value, w_out = weights
    half = rows // 2
    groups = H // KVH
    span = groups * HEAD

    def body(stage):
        normed_o, query_o, key_o, value_o, weights_o, context_o, mixed_o, top_o, bottom_o, gates_o = stage.out
        gains = stage.get(1)
        tokens_ref = stage.get(0)
        rows_in = tokens_ref[...].astype(F32)
        inverse = lax.rsqrt(jnp.mean(rows_in * rows_in, axis=1, keepdims=True) + EPSILON)
        normed = (rows_in * inverse * gains[0:1, :].astype(F32)).astype(BF16)
        normed_o[...] = normed
        stage.put(0)
        cos, sin = stage.get(2)[...], stage.get(3)[...]
        keys = dot(normed, stage.get(4)[...])
        for g in range(KVH):
            at = slice(g * HEAD, (g + 1) * HEAD)
            key_o[:, at] = turned(keys[:, at], cos, sin).astype(BF16)
        value_o[...] = dot(normed, stage.get(5)[...]).astype(BF16)
        stage.put(2, 3)
        lower = lax.broadcasted_iota(jnp.int32, (rows, rows), 0) >= lax.broadcasted_iota(jnp.int32, (rows, rows), 1)
        across = jnp.broadcast_to(stage.get(6)[...].astype(F32), (rows, rows))
        allowed = (across == across.T) & lower
        w_q = stage.get(7)
        for g in range(KVH):
            queries = dot(normed, w_q[:, g * span : (g + 1) * span])
            key = key_o[:, g * HEAD : (g + 1) * HEAD]
            value = value_o[:, g * HEAD : (g + 1) * HEAD]
            for i in range(groups):
                h = g * groups + i
                at = slice(h * HEAD, (h + 1) * HEAD)
                query = turned(queries[:, i * HEAD : (i + 1) * HEAD], cos, sin).astype(BF16)
                query_o[:, at] = query
                for first, last in ((0, half), (half, rows)):
                    scores = dot_nt(query[first:last], key[:last]) * HEAD ** (-0.5)
                    scores = jnp.where(allowed[first:last, :last], scores, NEG_FILL)
                    peak = jnp.max(scores, axis=1, keepdims=True)
                    terms = jnp.exp(scores - peak)
                    low = (terms / jnp.sum(terms, axis=1, keepdims=True)).astype(BF16)
                    weights_o[h * rows + first : h * rows + last, :last] = low
                    context_o[first:last, at] = dot(low, value[:last]).astype(BF16)
                weights_o[h * rows : h * rows + half, half:] = jnp.zeros((half, rows - half), BF16)
        stage.put(1, 4, 5)
        w_o = stage.get(8)
        step = width // 3
        for c in range(0, width, step):
            at = slice(c, c + step)
            mixed_o[:, at] = tokens_ref[:, at].astype(F32) + dot(context_o[...], w_o[:, at])
        stage.put(6)
        mixed = mixed_o[...]
        inverse = lax.rsqrt(jnp.mean(mixed * mixed, axis=1, keepdims=True) + EPSILON)
        moe_in = (mixed * inverse * gains[1:2, :].astype(F32)).astype(BF16)
        routes_ref = stage.get(9)
        logits = dot_nt(stage.get(10)[...], moe_in)
        ids = lax.broadcasted_iota(jnp.int32, (experts, rows), 0)
        hot = ids == routes_ref[0:1, :]
        for k in range(1, routes_ref.shape[0]):
            hot = hot | (ids == routes_ref[k : k + 1, :])
        peak = jnp.max(jnp.where(hot, logits, NEG_FILL), axis=0, keepdims=True)
        terms = jnp.where(hot, jnp.exp(jnp.where(hot, logits - peak, 0.0)), 0.0)
        gates = terms / jnp.sum(terms, axis=0, keepdims=True)
        gates_o[...] = gates
        high = gates.astype(BF16).astype(F32)
        count = jnp.sum(stage.get(11)[...].astype(F32), axis=1, keepdims=True)
        counts = jnp.broadcast_to(count, (experts, width - 2 * rows))
        notes = jnp.concatenate([high, gates - high, counts], axis=1).astype(BF16)
        top_o[...] = moe_in[:half]
        bottom_o[...] = jnp.concatenate([moe_in[half:], notes], axis=0)
        stage.put(7, 8, 9)

    ins = (
        tokens,
        jnp.stack([gain_one, gain_two]),
        *tables,
        w_key,
        w_value,
        segments,
        w_query,
        w_out,
        routes.T,
        router.T,
        valid,
    )
    outs = [
        ((rows, width), BF16),
        ((rows, H * HEAD), BF16),
        ((rows, KVH * HEAD), BF16),
        ((rows, KVH * HEAD), BF16),
        ((H * rows, rows), BF16),
        ((rows, H * HEAD), BF16),
        ((rows, width), F32),
        ((half, width), BF16),
        ((rows - half + experts, width), BF16),
        ((experts, rows), F32),
    ]
    return staged(body, ins, outs, flops=2 * rows * width * (2 * width + 4 * KVH * HEAD), first=7)


def mixed_backward(parts, grad_out, mixed, block, gates, router, gain_two):
    rows, width = mixed.shape
    experts = router.shape[1]
    counts = [len(pieces) for pieces in parts]
    n = sum(counts)

    def body(stage, *refs):
        branch_o, mixed_o, gain_o, router_o = stage.out[:4]
        weights = refs[0][...]
        moe_in = joined_rows([refs[5 + i] for i in range(len(block))])
        mixed_rows = refs[3][...]
        inverse = lax.rsqrt(jnp.mean(mixed_rows * mixed_rows, axis=1, keepdims=True) + EPSILON)
        normal = mixed_rows * inverse
        places = iter(range(5 + len(block), 5 + len(block) + n))
        total = 0.0
        for count in counts:
            total = total + joined_rows([refs[next(places)] for _ in range(count)]).astype(F32)
        notes = total[rows : rows + experts]
        grad_gates = notes[:, :rows] + notes[:, rows : 2 * rows]
        chosen = weights * (grad_gates - jnp.sum(weights * grad_gates, axis=0, keepdims=True))
        logits = chosen.astype(BF16)
        router_o[...] = dot(logits, moe_in[:rows])
        grad_in = total[:rows] + dot_tn(logits, refs[1][...])
        gain_o[...] = jnp.sum(grad_in * normal, axis=0, keepdims=True)
        scaled = grad_in * refs[2][...].astype(F32)
        inner = jnp.mean(scaled * normal, axis=1, keepdims=True)
        grad_mixed = refs[4][...] + inverse * (scaled - normal * inner)
        branch_o[...] = grad_mixed.astype(BF16)
        mixed_o[...] = grad_mixed
        send_shares(stage, branch_o, 4)
        stage.put(0, 1, 2, 3)

    ins = (gates, router.T, gain_two[None], mixed, grad_out, *block, *(p for pieces in parts for p in pieces))
    outs = [((rows, width), BF16), ((rows, width), F32), ((1, width), F32), ((experts, width), F32)]
    outs += shares_shape(rows, width)
    made = staged(body, (), outs, kept=ins, limit=LEAN, straight=range(4, len(outs)))
    return made[:4], made[4:]


def attention_backward(branch, weights, query, key, value, tables, w_out):
    rows = branch.shape[0]
    groups = H // KVH
    span = groups * HEAD
    scale = HEAD ** (-0.5)

    def body(stage, key_ref, value_ref, query_ref, low_all, cos_ref, sin_ref):
        qkv_o = stage.out[0]
        grad_branch = stage.get(0)[...]
        for g in range(KVH):
            w_o = stage.get(1 + g)
            grad_context = dot_nt(grad_branch, w_o[...]).astype(BF16)
            k = key_ref[:, g * HEAD : (g + 1) * HEAD]
            v = value_ref[:, g * HEAD : (g + 1) * HEAD]
            grad_key = jnp.zeros((rows, HEAD), F32)
            grad_value = jnp.zeros((rows, HEAD), F32)
            cos, sin = cos_ref[...], -sin_ref[...]
            for i in range(groups):
                h = g * groups + i
                q = query_ref[:, h * HEAD : (h + 1) * HEAD]
                grad = grad_context[:, i * HEAD : (i + 1) * HEAD]
                low = low_all[h * rows : (h + 1) * rows, :]
                grads = dot_nt(grad, v)
                full = low.astype(F32)
                product = full * grads
                scores = (product - full * jnp.sum(product, axis=1, keepdims=True)).astype(BF16)
                grad_query = dot(scores, k) * scale
                qkv_o[:, h * HEAD : (h + 1) * HEAD] = turned(grad_query, cos, sin).astype(BF16)
                grad_key = grad_key + dot_tn(scores, q)
                grad_value = grad_value + dot_tn(low, grad)
            at = (H + g) * HEAD
            qkv_o[:, at : at + HEAD] = turned(grad_key * scale, cos, sin).astype(BF16)
            at += KVH * HEAD
            qkv_o[:, at : at + HEAD] = grad_value.astype(BF16)
        send_shares(stage, qkv_o, 1)
        stage.put(0)

    ins = (branch, (w_out, 0, span), (w_out, span, span))
    columns = (H + 2 * KVH) * HEAD
    outs = [((rows, columns), BF16)] + shares_shape(rows, columns)
    made = staged(
        body, ins, outs, first=2, straight=range(1, len(outs)), limit=LEAN + 4,
        kept=(key, value, query, weights, *tables))
    return made[0], made[1:]


def weight_grads(ring, early, late):
    columns, width = early[0].shape[1], late[0].shape[1]
    share = columns // ring.size
    step = 256

    def body(stage):
        total = stage.room[0]
        early_refs = [stage.get(i) for i in range(0, 2 * len(late), 2)]
        late_refs = [stage.get(i) for i in range(1, 2 * len(late), 2)]
        for c in range(0, columns, step):
            made = 0.0
            for a, b in zip(early_refs, late_refs):
                made = made + dot_tn(a[:, c : c + step], b[...])
            total[c : c + step, :] = made.astype(BF16)
        for j in range(ring.size):
            start = pl.multiple_of(ring.owner(j) * share, 16)
            stage.send(total.at[pl.ds(start, share)], j)

    ins = [p for pair in zip(early, late) for p in pair]
    outs = [((share, width), BF16)] * ring.size
    every = range(len(outs))
    return staged(body, ins, outs, straight=every, held=every, room=[((columns, width), BF16)], limit=LEAN)


def token_backward(qkv, tokens, grad_mixed, gain_one, weights):
    rows, width = tokens.shape
    w_query, w_key, w_value, _ = weights
    at, span = H * HEAD, KVH * HEAD

    def body(stage):
        tokens_o, gain_o = stage.out
        qkv_ref = stage.get(0)
        rows_in = stage.get(1)[...].astype(F32)
        inverse = lax.rsqrt(jnp.mean(rows_in * rows_in, axis=1, keepdims=True) + EPSILON)
        normal = rows_in * inverse
        grads = dot_nt(qkv_ref[:, at : at + span], stage.get(2)[...])
        grads = grads + dot_nt(qkv_ref[:, at + span :], stage.get(3)[...])
        grads = grads + dot_nt(qkv_ref[:, :at], stage.get(4)[...])
        gain_o[...] = jnp.sum(grads * normal, axis=0, keepdims=True)
        scaled = grads * stage.get(5)[...].astype(F32)
        inner = jnp.mean(scaled * normal, axis=1, keepdims=True)
        tokens_o[...] = stage.get(6)[...] + inverse * (scaled - normal * inner)
        stage.put(0, 1)

    ins = (qkv, tokens, w_key, w_value, w_query, gain_one[None], grad_mixed)
    return staged(body, ins, [((rows, width), F32), ((1, width), F32)], limit=LEAN + 10)


def after(value, first):
    return lax.optimization_barrier((value, first))[0]


def rep_pairs(k):
    size = lax.axis_size(("x", "c"))
    return [(i, i ^ k) for i in range(size)]


def x_gather(a):
    size = lax.axis_size("x")
    return [a] + [lax.ppermute(a, "x", [(i, i ^ k) for i in range(size)]) for k in range(1, size)]


def core_gather(blocks):
    return [b for a in blocks for b in (a, lax.ppermute(a, "c", [(0, 1), (1, 0)]))]


def rep_gather(a):
    return core_gather(x_gather(a))


def rep_spread(parts):
    return [lax.ppermute(p, ("x", "c"), rep_pairs(k)) if k else p for k, p in enumerate(parts)]


def rep_parts(a):
    size = lax.axis_size(("x", "c"))
    share = a.shape[1] // size
    return [lax.dynamic_slice_in_dim(a, (rep_index() ^ k) * share, share, 1) for k in range(size)]


def rep_columns(blocks):
    step = 1
    while step < len(blocks):
        swap = (rep_index() & step) != 0
        blocks = [jnp.where(swap, blocks[i ^ step], blocks[i]) for i in range(len(blocks))]
        step *= 2
    return blocks


def columns_of(blocks, start, stop):
    share = blocks[0].shape[1]
    parts = []
    for i, block in enumerate(blocks):
        low, high = max(start - i * share, 0), min(stop - i * share, share)
        if low < high:
            parts.append(block[:, low:high])
    return jnp.concatenate(parts, axis=1).astype(F32)


def shards(
    ring,
    tokens,
    segments,
    routes,
    valid_mask,
    teacher,
    gain_one,
    w_query,
    w_key,
    w_value,
    w_out,
    gain_two,
    router,
    w_gate,
    w_up,
    w_down,
):
    length, width = tokens.shape
    experts_all = router.shape[1]
    tokens_all = length * lax.axis_size(ALL)
    w_gate, w_up, w_down = w_gate[0], w_up[0], w_down[0]
    valid_rows = valid_mask.reshape(length).astype(F32)
    tables = rope_tables(length)
    attn = (w_query, w_key, w_value, w_out)
    normed_low, query, key, value, weights_low, context, mixed_rows, *block, gates = attention_forward(
        tokens, segments, routes, valid_mask, gain_one, gain_two, tables, router, attn
    )
    form = RingExperts if ring.size <= RING_LIMIT else SlotExperts
    experts = form(ring, block, gates, routes.shape[1], w_gate, w_up, w_down)
    gathered = {}

    def gather_beside(step, sent):
        if step == 0:
            gathered["normed"] = x_gather(after(normed_low, sent))
        if step == 2:
            gathered["normed"] = core_gather(after(gathered["normed"], sent))
        return gathered["normed"] if step % 2 else ()

    def beside(step, sent):
        if step == 0:
            gathered["count"] = butterfly_sum(experts.count, ("c", "x"))
        if step == 1:
            gathered["context"] = x_gather(after(context, (sent, gathered["count"])))
        if step == 3:
            gathered["context"] = core_gather(after(gathered["context"], sent))
        return gathered["count"] if step == 1 else ()

    moe_parts = experts.forward(gather_beside, beside)
    if not gathered:
        gathered = {"normed": rep_gather(normed_low), "context": rep_gather(context)}
        gathered["count"] = butterfly_sum(experts.count, ("c", "x"))
    count_total = gathered["count"][0, 0]
    scale = 2.0 * tokens_all / count_total * valid_rows[:, None]

    def gap_rows(parts, mixed, aim):
        rows = mixed + added(parts)
        return rows, rows - aim.astype(F32)

    grad_low = (scale * gap_rows(moe_parts, mixed_rows, teacher)[1]).astype(BF16)
    moe_parts, mixed_again, aim, scale = after((moe_parts, mixed_rows, teacher, scale), grad_low)
    output_rows, residual_gap = gap_rows(moe_parts, mixed_again, aim)
    numerator = jnp.sum(valid_rows * jnp.sum(residual_gap * residual_gap, axis=-1))
    grad_out = scale * residual_gap

    def back_beside(step, sent):
        return (gathered, numerator, grad_out) if step == 1 else ()

    back_parts, sums = experts.backward(grad_low, back_beside)
    (grad_branch, grad_mixed, grad_gain_two, grad_router), branch_parts = mixed_backward(
        after(back_parts, [each.got for each in sums]), grad_out, mixed_rows, block, gates, router, gain_two
    )
    branch_spread = rep_spread(branch_parts or rep_parts(grad_branch))
    grad_qkv, qkv_parts = attention_backward(
        grad_branch, weights_low, query, key, value, tables, w_out
    )
    qkv_spread = rep_spread(qkv_parts or rep_parts(grad_qkv))
    out_sum = RingSum(ring, weight_grads(ring, gathered["context"], after(branch_spread, grad_qkv)))
    grad_tokens, grad_gain_one = token_backward(
        after(grad_qkv, out_sum.sent), tokens, grad_mixed, gain_one, attn
    )
    small = jnp.concatenate([grad_router, grad_gain_two, grad_gain_one, jnp.full((1, width), numerator)], axis=0)
    hops = butterfly_hops(("c", "x", "y", "z"))
    small, got = butterfly_hop(small, hops.pop(0), grad_tokens)
    grad_w_qkv = weight_grads(ring, gathered["normed"], after(qkv_spread, small))
    small = small + after(got, grad_w_qkv[0])
    out_sum.step(grad_w_qkv[0])
    qkv_sum = RingSum(ring, grad_w_qkv)
    out_blocks = None
    while qkv_sum.left > 1:
        if out_sum.left > 1:
            out_sum.step(qkv_sum.sent)
        elif out_blocks is None:
            out_blocks = rep_gather(out_sum.total(qkv_sum.sent))
        if hops:
            small, got = butterfly_hop(small, hops.pop(0), qkv_sum.sent)
            small = small + got
        qkv_sum.step((out_sum.sent, small))
    if out_blocks is None:
        while out_sum.left > 1:
            out_sum.step(qkv_sum.sent)
        out_blocks = rep_gather(out_sum.total(qkv_sum.sent))
    for hop in hops:
        small, got = butterfly_hop(small, hop, qkv_sum.sent)
        small = small + got
    qkv_blocks = rep_gather(qkv_sum.total(small))
    shares = [each.result(qkv_blocks[0])[0] for each in sums]
    out_share = columns_of(rep_columns(after(out_blocks, qkv_blocks[0])), 0, width)
    router_share = small[:experts_all].T
    gain_shares = (small[experts_all + 1], small[experts_all])
    loss_value = small[experts_all + 2, 0] / count_total
    qkv_share = rep_columns(after(qkv_blocks, (shares, out_share, router_share, gain_shares, loss_value)))
    return (
        output_rows.astype(BF16),
        loss_value,
        grad_tokens,
        gain_shares[0],
        columns_of(qkv_share, 0, H * HEAD),
        columns_of(qkv_share, H * HEAD, (H + KVH) * HEAD),
        columns_of(qkv_share, (H + KVH) * HEAD, (H + 2 * KVH) * HEAD),
        out_share,
        gain_shares[1],
        router_share,
        shares[0],
        shares[1],
        shares[2],
    )


def solution(mesh):
    rep, ep = mesh.shape["rep"], mesh.shape["ep"]
    x_size = rep // 2
    y_size = x_size if ep % x_size == 0 else 1
    grid = Mesh(mesh.devices.reshape(x_size, 2, ep // y_size, y_size), ALL)
    rows = P(ALL, None)
    whole = P()
    expert = P(EP, None, None)
    return jax.shard_map(
        functools.partial(shards, Ring(ep // y_size, y_size)),
        mesh=grid,
        in_specs=(rows,) * 5 + (whole,) * 7 + (expert,) * 3,
        out_specs=(rows, whole, rows, whole)
        + (P(EP, None),) * 4
        + (whole, whole)
        + (P(EP, ("x", "c"), None),) * 3,
        check_vma=False,
    )
```

```python
import functools
import math

import jax
import jax.numpy as jnp
import numpy as np
from jax import lax
from jax.experimental import pallas as pl
from jax.experimental.pallas import tpu as pltpu
from jax.sharding import Mesh
from jax.sharding import PartitionSpec as P

H = 12
KVH = 2
HEAD = 128

EPSILON = 1e-06
ROPE_BASE = 10000.0
NEG_FILL = -1e30
ALL = ("x", "c", "z", "y")
EP = ("z", "y")
F32 = jnp.float32
BF16 = jnp.bfloat16
RING_LIMIT = 16
SPLIT = True
LEAN = 20


def dot(a, b, dims=((1,), (0,))):
    return lax.dot_general(a, b, (dims, ((), ())), preferred_element_type=F32)


def dot_nt(a, b):
    return dot(a, b, ((1,), (1,)))


def dot_tn(a, b):
    return dot(a, b, ((0,), (0,)))


def activate(gate_pre, up_pre):
    return jax.nn.gelu(gate_pre, approximate=True) * up_pre


class Ring:
    def __init__(self, z_size, y_size):
        cycle = [(z, 0) for z in range(z_size)]
        for step, z in enumerate(reversed(range(z_size))):
            rest = list(range(1, y_size))
            cycle += [(z, y) for y in (rest if step % 2 == 0 else rest[::-1])]
        self.order = [z * y_size + y for z, y in cycle]
        self.size = len(self.order)
        self.half = self.size // 2
        n = self.size
        self.forward = [(self.order[i], self.order[(i + 1) % n]) for i in range(n)]
        self.backward = [(b, a) for a, b in self.forward]
        self.place = [self.order.index(e) for e in range(n)]

    def fwd(self, a):
        return lax.ppermute(a, EP, self.forward)

    def bwd(self, a):
        return lax.ppermute(a, EP, self.backward)

    def owner(self, j):
        me = lax.axis_index(EP)
        found = 0
        for e, place in enumerate(self.place):
            found = found + jnp.where(me == e, self.order[(place - j) % self.size], 0)
        return found

    def pair(self, s):
        return sorted({s, (self.size - s) % self.size})

    def gather(self, pieces, use, lag, beside=lambda step, sent: ()):
        ahead = behind = list(pieces) if SPLIT else [jnp.concatenate(pieces, axis=0)]
        cut = pieces[0].shape[0]
        ready = {0: ahead}
        open_steps = [0]
        for s in range(1, self.half + 1):
            sent = (ahead, behind)
            if s == self.half and SPLIT:
                ahead, behind = ahead[:1], behind[1:]
            elif s == self.half:
                ahead, behind = [ahead[0][:cut]], [behind[0][cut:]]
            ahead, behind = [self.fwd(p) for p in ahead], [self.bwd(p) for p in behind]
            made = [beside(s - 1, sent)]
            while open_steps and open_steps[0] + lag <= s - 1:
                step = open_steps.pop(0)
                made.append(use({j: after(ready[j], sent) if lag else ready[j] for j in self.pair(step)}))
            ahead[0], behind[0], _ = lax.optimization_barrier((ahead[0], behind[0], made))
            if s < self.half:
                ready[s], ready[self.size - s] = list(ahead), list(behind)
                open_steps.append(s)
        made = use({self.half: ahead + behind})
        for step in reversed(open_steps):
            use({j: after(ready[j], made) for j in self.pair(step)})

    def scatter_sum(self, terms, beside=lambda step, sent: ()):
        def add(a, b):
            return (a.astype(F32) + b.astype(F32)).astype(BF16)

        far, (near,), (away,) = terms(self.half), terms(self.half - 1), terms(self.half + 1)
        cut = far[0].shape[0]
        down, up = self.bwd(far[0]), self.fwd(far[1])
        down, up, _ = lax.optimization_barrier((down, up, beside(0, far)))
        down = [jnp.concatenate([add(near[:cut], down), near[cut:]], axis=0)]
        up = [jnp.concatenate([away[:cut], add(away[cut:], up)], axis=0)]
        for s in range(self.half - 1, 0, -1):
            sent = (down, up)
            down, up = [self.bwd(p) for p in down], [self.fwd(p) for p in up]
            down[0], up[0], _ = lax.optimization_barrier((down[0], up[0], beside(self.half - s, sent)))
            if s > 1:
                down = [add(a, b) for a, b in zip(down, terms(s - 1))]
                up = [add(a, b) for a, b in zip(up, terms(self.size - s + 1))]
        return down, up, terms(0)


class RingSum:
    def __init__(self, ring, terms):
        self.ring, self.terms, self.left = ring, terms, ring.half
        cut = terms[0].shape[0] // 32 * 16
        self.cut = cut
        far = terms[ring.half]
        self.sent = far
        self.down, self.up = ring.bwd(far[:cut]), ring.fwd(far[cut:])

    def arrive(self, tie):
        self.down, self.up, _ = lax.optimization_barrier((self.down, self.up, tie))

    def step(self, tie):
        ring, cut = self.ring, self.cut
        self.arrive(tie)
        self.left -= 1

        def add(a, b):
            return (a.astype(F32) + b.astype(F32)).astype(BF16)

        near, away = self.terms[self.left], self.terms[ring.size - self.left]
        if self.left == ring.half - 1:
            down = jnp.concatenate([add(near[:cut], self.down), near[cut:]], axis=0)
            up = jnp.concatenate([away[:cut], add(away[cut:], self.up)], axis=0)
        else:
            down, up = add(near, self.down), add(away, self.up)
        self.sent = (down, up)
        self.down, self.up = ring.bwd(down), ring.fwd(up)

    def total(self, tie):
        self.arrive(tie)
        return (self.down.astype(F32) + self.up.astype(F32) + self.terms[0].astype(F32)).astype(BF16)


def butterfly_hops(axes):
    return [(axis, step) for axis in axes for step in (1, 2, 4, 8, 16) if step < lax.axis_size(axis)]


def butterfly_hop(a, hop, tie):
    axis, step = hop
    a, _ = lax.optimization_barrier((a, tie))
    return a, lax.ppermute(a, axis, [(i, i ^ step) for i in range(lax.axis_size(axis))])


def added(lists):
    return sum(jnp.concatenate(pieces, axis=0).astype(F32) for pieces in lists)


def butterfly_sum(a, axes):
    for axis in axes:
        size = lax.axis_size(axis)
        step = 1
        while step < size:
            a = a + lax.ppermute(a, axis, [(i, i ^ step) for i in range(size)])
            step *= 2
    return a


class Sum:
    def __init__(self, a):
        self.a = a

    @staticmethod
    def send(a, axis, dim):
        size = lax.axis_size(axis)
        if size != 2:
            got = lax.psum_scatter(a, axis, scatter_dimension=dim, tiled=True)
            return jnp.zeros_like(got), got
        first = lax.axis_index(axis) == 0
        low, high = lax.slice_in_dim(a, 0, 1, axis=dim), lax.slice_in_dim(a, 1, 2, axis=dim)
        return jnp.where(first, low, high), lax.ppermute(jnp.where(first, high, low), axis, [(0, 1), (1, 0)])

    def over_cores(self, tie):
        self.mine, self.got = self.send(after(self.a, tie), "c", 1)

    def over_x(self, tie):
        mine, got = self.mine, after(self.got, tie)
        both = (mine.astype(F32) + got.astype(F32)).astype(BF16)
        self.mine, self.got = self.send(both, "x", 0)
        return both

    def result(self, tie):
        got = after(self.got, tie)
        return self.mine.astype(F32) + got.astype(F32)


class RingExperts:
    def __init__(self, ring, block, gates, top, w_gate, w_up, w_down):
        self.ring, self.block = ring, list(block)
        self.experts, self.rows = gates.shape
        self.weights = (w_gate, w_up, w_down)
        self.cut = self.rows // 2

    def forward(self, gather_beside, beside):
        self.rows_in, self.saved = {}, {}
        terms, counts = {}, {}

        def use(blocks):
            apart = self.ring.half in blocks
            made = expert_forward(list(blocks.values()), self.experts, apart, *self.weights)
            for j, (rows, top, gate_pre, up_pre, hidden, weight, count, *bottom) in zip(blocks, made):
                self.rows_in[j], terms[j], counts[j] = rows, [top, *bottom], count
                self.saved[j] = (gate_pre, up_pre, hidden, weight)
            return made

        self.ring.gather(self.block, use, 1, gather_beside)
        self.count = sum(counts[j] for j in range(self.ring.size))
        return self.ring.scatter_sum(terms.get, beside)

    def backward(self, low, gather_beside):
        grads_in, gate_lows, up_lows, scaled, terms = {}, {}, {}, {}, {}

        def use(blocks):
            saved = [self.saved[j] for j in blocks]
            apart = self.ring.half in blocks
            made = expert_backward(list(blocks.values()), saved, self.experts, apart, *self.weights)
            for j, (grads, top, gate_low, up_low, part, *bottom) in zip(blocks, made):
                grads_in[j], gate_lows[j], up_lows[j], scaled[j] = grads, gate_low, up_low, part
                terms[j] = [top, *bottom]
            return made

        self.ring.gather([low[: self.cut], low[self.cut :]], use, 0, gather_beside)
        sums = []

        def joined(parts):
            return jnp.concatenate([parts[j] for j in range(self.ring.size)], axis=0)

        def beside(step, sent):
            made = []
            if step == 0:
                self.joined = after(joined(self.rows_in), sent)
                sums.append(expert_sum(self.joined, joined(after(gate_lows, sent))))
            if step == 1:
                sums.append(expert_sum(self.joined, joined(after(up_lows, sent))))
            if step == 2:
                sums.append(expert_sum(joined(after(scaled, sent)), joined(after(grads_in, sent))))
                made.append(sums[0].got)
            if step == 3:
                made.append(sums[1].got)
            if step > 0:
                made.append(sums[step - 1].over_x(sent))
            if step < 3:
                made.append(sums[step].a)
                sums[step].over_cores(sums[step].a)
            return made

        return self.ring.scatter_sum(terms.get, beside), sums


def expert_sum(a, b):
    product = dot_tn(a, b).astype(BF16)
    return Sum(product.reshape(lax.axis_size("x"), lax.axis_size("c"), -1, product.shape[1]))


class SlotExperts:
    def __init__(self, ring, block, gates, top, w_gate, w_up, w_down):
        experts, rows = gates.shape
        block = jnp.concatenate(block, axis=0)
        moe_in, route_hot = block[:rows], gates.T > 0
        self.count_here = jnp.full((8, 128), block[rows, -1].astype(F32))
        self.slots = 3 * rows * top // (2 * experts)
        self.group = ring.size
        self.moe_in, self.weights = moe_in, (w_gate, w_up, w_down)
        places = jnp.arange(rows)
        earlier = (places[:, None] > places[None, :]).astype(BF16)
        rank = dot(earlier, route_hot.astype(BF16)).T[:, None, :]
        slot = jnp.arange(self.slots, dtype=F32)[None, :, None]
        picks = ((rank == slot) & route_hot.T[:, None, :]).reshape(experts * self.slots, rows)
        self.picks = picks.astype(BF16)
        self.slot_gate = jnp.where(picks, jnp.repeat(gates, self.slots, axis=0), 0.0)

    def swap(self, rows):
        blocks = rows.reshape(self.group, -1, rows.shape[1])
        return lax.all_to_all(blocks, EP, 0, 0, tiled=True).reshape(rows.shape)

    def forward(self, gather_beside, beside):
        w_gate, w_up, w_down = self.weights
        self.arrived = self.swap(dot(self.picks, self.moe_in).astype(BF16))
        self.gate_pre = dot(self.arrived, w_gate)
        self.up_pre = dot(self.arrived, w_up)
        self.hidden = activate(self.gate_pre, self.up_pre).astype(BF16)
        self.returned = self.swap(dot(self.hidden, w_down).astype(BF16))
        self.count = butterfly_sum(self.count_here, ("y", "z"))
        return [[jnp.dot(self.slot_gate.T, self.returned.astype(F32), precision=lax.Precision.HIGHEST)]]

    def backward(self, grad_low, gather_beside):
        w_gate, w_up, w_down = self.weights
        rows, experts = grad_low.shape[0], self.picks.shape[0] // self.slots
        products = dot_nt(grad_low, self.returned) * self.picks.T.astype(F32)
        grad_gates = jnp.sum(products.reshape(rows, experts, self.slots), axis=2)
        slot_gate = jnp.sum(self.slot_gate, axis=1, keepdims=True)
        grads_in = self.swap((dot(self.picks, grad_low) * slot_gate).astype(BF16))
        _, pull = jax.vjp(activate, self.gate_pre, self.up_pre)
        grad_gate, grad_up = pull(dot_nt(grads_in, w_down))
        gate_low, up_low = grad_gate.astype(BF16), grad_up.astype(BF16)
        back = self.swap((dot_nt(gate_low, w_gate) + dot_nt(up_low, w_up)).astype(BF16))
        sums = [
            expert_sum(self.arrived, gate_low),
            expert_sum(self.arrived, up_low),
            expert_sum(self.hidden, grads_in),
        ]
        for each in sums:
            each.over_cores(each.a)
        for each in sums:
            each.over_x(each.a)
        notes = jnp.pad(grad_gates.T, ((0, 0), (0, grad_low.shape[1] - rows)))
        return [[jnp.concatenate([dot_tn(self.picks, back), notes], axis=0)]], sums


def rope_tables(length):
    half = HEAD // 2
    frequency = ROPE_BASE ** (-np.arange(half, dtype=np.float64) / half)
    angles = np.arange(length, dtype=np.float64)[:, None] * frequency[None, :]
    cosine, sine = np.cos(angles), np.sin(angles)
    pairs = np.concatenate([cosine, cosine], axis=1), np.concatenate([-sine, sine], axis=1)
    return tuple(jnp.asarray(p, F32) for p in pairs)


def turned(values, cosine, sine):
    return values * cosine + pltpu.roll(values, HEAD // 2, 1) * sine


class Stage:
    def __init__(self, slices, outs, first, refs):
        n, m = len(slices), len(outs)
        self.there, self.out_there, refs = refs[:n], refs[n : n + m], refs[n + m :]
        self.here, self.out, in_sems, out_sems = refs[:n], refs[n : n + m], refs[n + m], refs[n + m + 1]
        self.out_sems = out_sems
        self.later = []
        self.coming = {}
        for i, rows in enumerate(slices):
            source = self.there[i] if rows is None else self.there[i].at[pl.ds(*rows)]
            self.coming[i] = pltpu.make_async_copy(source, self.here[i], in_sems.at[i])
            if i < first:
                self.coming[i].start()
            else:
                self.later.append(self.coming[i])
        self.leaving = []

    def get(self, i):
        if i in self.coming:
            self.coming.pop(i).wait()
        for copy in self.later:
            copy.start()
        self.later = []
        return self.here[i]

    def put(self, *which):
        for i in which:
            self.send(self.out[i], i)

    def send(self, source, i):
        self.leaving.append(pltpu.make_async_copy(source, self.out_there[i], self.out_sems.at[i]))
        self.leaving[-1].start()

    def finish(self):
        for copy in self.leaving:
            copy.wait()


def staged(body, ins, outs, scalars=(), flops=0, kept=(), limit=60, first=None, straight=(), room=(), held=()):
    arrays = [a if isinstance(a, jax.Array) else a[0] for a in ins]
    slices = [None if isinstance(a, jax.Array) else a[1:] for a in ins]
    sizes = [a.shape if s is None else (s[1], *a.shape[1:]) for a, s in zip(arrays, slices)]
    start = len(ins) if first is None else first
    tile = ((8, 128), BF16)

    def kernel(*refs):
        count = len(scalars) + len(kept)
        stage = Stage(slices, outs, start, refs[count : len(refs) - len(room)])
        stage.out = [there if i in held else o for i, (there, o) in enumerate(zip(stage.out_there, stage.out))]
        stage.room = refs[len(refs) - len(room) :]
        body(stage, *refs[:count])
        stage.finish()

    any_place = pl.BlockSpec(memory_space=pltpu.HBM)
    vmem = [pltpu.VMEM(*(tile if i in straight or i in held else o)) for i, o in enumerate(outs)]
    out_places = [on_chip(1)[0] if i in held else any_place for i in range(len(outs))]
    return pl.pallas_call(
        kernel,
        out_shape=[jax.ShapeDtypeStruct(s, d) if i in held else pltpu.HBM(s, d) for i, (s, d) in enumerate(outs)],
        in_specs=[pl.BlockSpec(memory_space=pltpu.SMEM)] * len(scalars) + on_chip(len(kept)) + [any_place] * len(ins),
        out_specs=out_places,
        scratch_shapes=[pltpu.VMEM(s, a.dtype) for s, a in zip(sizes, arrays)]
        + vmem
        + [pltpu.SemaphoreType.DMA((max(len(ins), 1),)), pltpu.SemaphoreType.DMA((len(outs),))]
        + [pltpu.VMEM(*r) for r in room],
        compiler_params=pltpu.CompilerParams(vmem_limit_bytes=limit << 20),
        cost_estimate=pl.CostEstimate(flops=int(flops), bytes_accessed=0, transcendentals=0),
    )(*scalars, *kept, *(pltpu.with_memory_space_constraint(a, pltpu.HBM) for a in arrays))


def on_chip(count):
    return [pl.BlockSpec(memory_space=pltpu.VMEM)] * count


def rep_index():
    return lax.axis_index("x") * lax.axis_size("c") + lax.axis_index("c")


def rep_shares(columns):
    size = lax.axis_size(("x", "c"))
    return size if columns % (128 * size) == 0 else 0


def send_shares(stage, source, at):
    count = rep_shares(source.shape[1])
    share = source.shape[1] // max(count, 1)
    me = rep_index()
    for k in range(count):
        start = pl.multiple_of((me ^ k) * share, 128)
        stage.send(source.at[:, pl.ds(start, share)], at + k)


def shares_shape(rows, columns):
    count = rep_shares(columns)
    return [((rows, columns // max(count, 1)), BF16)] * count


def gelu_parts(values):
    c = math.sqrt(2.0 / math.pi)
    square = values * values
    level = 0.5 + 0.5 * jnp.tanh(c * values * (1.0 + 0.044715 * square))
    slope = level + 2.0 * c * values * level * (1.0 - level) * (1.0 + 3 * 0.044715 * square)
    return level, slope


def note_rows(experts, expert, columns):
    rows = lax.broadcasted_iota(jnp.int32, (experts, columns), 0)
    return (rows == expert).astype(F32)


def joined_rows(refs):
    return jnp.concatenate([r[...] for r in refs], axis=0) if len(refs) > 1 else refs[0][...]


def expert_forward(blocks, experts, apart, w_gate, w_up, w_down):
    parts = [len(pieces) for pieces in blocks]
    rows = sum(p.shape[0] for p in blocks[0]) - experts
    width, inner = w_gate.shape
    half = rows // 2 if apart else rows
    size = 8 if apart else 7
    step = 256

    def body(stage, w_g, w_u, w_d):
        mine = note_rows(experts, lax.axis_index(EP), 128).astype(BF16)
        places = iter(range(len(flat)))
        for b, count in enumerate(parts):
            block = joined_rows([stage.get(next(places)) for _ in range(count)])
            first = size * b
            rows_o, top_o, gate_o, up_o, hidden_o, weight_o, count_o, *bottom_o = stage.out[first : first + size]
            notes = block[rows:]
            block = block[:rows]
            rows_o[...] = block
            weight = dot_tn(notes[:, :rows], mine) + dot_tn(notes[:, rows : 2 * rows], mine)
            weight_o[...] = weight
            count_o[...] = notes[:, width - 128 :].astype(F32)
            stage.put(first, first + 5, first + 6)
            for f in range(0, inner, step):
                gate_pre = dot(block, w_g[:, f : f + step])
                up_pre = dot(block, w_u[:, f : f + step])
                level, _ = gelu_parts(gate_pre)
                hidden_o[:, f : f + step] = (gate_pre * level * up_pre).astype(BF16)
                gate_o[:, f : f + step] = gate_pre.astype(BF16)
                up_o[:, f : f + step] = up_pre.astype(BF16)
            stage.put(first + 2, first + 3, first + 4)
            hidden = hidden_o[...]
            wide = jnp.concatenate([weight] * (step // 128), axis=1)
            for c in range(0, width, step):
                term = (dot(hidden, w_d[:, c : c + step]) * wide).astype(BF16)
                top_o[:, c : c + step] = term[:half]
                if apart:
                    bottom_o[0][:, c : c + step] = term[half:]
            stage.put(first + 1, *([first + 7] if apart else ()))

    flat = [p for pieces in blocks for p in pieces]
    one = [((rows, width), BF16), ((half, width), BF16)] + [((rows, inner), BF16)] * 3
    one += [((rows, 128), F32), ((experts, 128), F32)] + [((rows - half, width), BF16)] * apart
    flops = len(blocks) * 6 * rows * width * inner
    made = staged(body, flat, one * len(blocks), flops=flops, kept=(w_gate, w_up, w_down), limit=LEAN)
    return [made[size * i : size * i + size] for i in range(len(blocks))]


def expert_backward(blocks, saved, experts, apart, w_gate, w_up, w_down):
    parts = [len(pieces) for pieces in blocks]
    rows, inner = saved[0][0].shape
    width = w_gate.shape[0]
    half = rows // 2
    size = 6 if apart else 5
    step = 256

    def body(stage, w_g, w_u, w_d, *given):
        mine = note_rows(experts, lax.axis_index(EP), width)
        ones = jnp.ones((8, step), BF16)
        at = 0
        for b, count in enumerate(parts):
            places = list(range(at, at + count + 4))
            at += count + 4
            first = size * b
            grads_o, top_o, gate_o, up_o, scaled_o, *bottom_o = stage.out[first : first + size]
            grads = joined_rows([given[i] for i in places[:count]])
            gate_ref, up_ref, hidden_ref, weight_ref = (given[i] for i in places[count:])
            grads_o[...] = grads
            wide = jnp.concatenate([weight_ref[...]] * (step // 128), axis=1)
            sums = jnp.zeros((8, rows), F32)
            for f in range(0, inner, step):
                raw = dot_nt(grads, w_d[f : f + step, :])
                hidden = hidden_ref[:, f : f + step].astype(F32)
                product = raw * hidden
                high = product.astype(BF16)
                sums = sums + dot_nt(ones, high) + dot_nt(ones, (product - high.astype(F32)).astype(BF16))
                scaled_o[:, f : f + step] = (hidden * wide).astype(BF16)
                gate_pre = gate_ref[:, f : f + step].astype(F32)
                level, slope = gelu_parts(gate_pre)
                grad_hidden = raw * wide
                gate_o[:, f : f + step] = (grad_hidden * up_ref[:, f : f + step].astype(F32) * slope).astype(BF16)
                up_o[:, f : f + step] = (grad_hidden * gate_pre * level).astype(BF16)
            high = sums.astype(BF16).astype(F32)
            notes = jnp.concatenate([high, sums - high, jnp.zeros((8, width - 2 * rows), F32)], axis=1)
            notes = (jnp.broadcast_to(notes[:1], (experts, width)) * mine).astype(BF16)
            gate_low, up_low = gate_o[...], up_o[...]
            terms = [
                (dot_nt(gate_low, w_g[c : c + step, :]) + dot_nt(up_low, w_u[c : c + step, :])).astype(BF16)
                for c in range(0, width, step)
            ]
            term = jnp.concatenate(terms, axis=1)
            if apart:
                top_o[...] = term[:half]
                bottom_o[0][...] = jnp.concatenate([term[half:], notes], axis=0)
            else:
                top_o[...] = jnp.concatenate([term, notes], axis=0)

    flat = [p for pieces, kept in zip(blocks, saved) for p in (*pieces, *kept)]
    one = [((rows, width), BF16), ((half if apart else rows + experts, width), BF16)] + [((rows, inner), BF16)] * 3
    one += [((rows - half + experts, width), BF16)] * apart
    flops = len(blocks) * 6 * rows * width * inner
    every = range(size * len(blocks))
    made = staged(body, (), one * len(blocks), flops=flops, kept=(w_gate, w_up, w_down, *flat), limit=LEAN, held=every)
    return [made[size * i : size * i + size] for i in range(len(blocks))]


def attention_forward(tokens, segments, routes, valid, gain_one, gain_two, tables, router, weights):
    rows, width = tokens.shape
    experts = router.shape[1]
    w_query, w_key, w_value, w_out = weights
    half = rows // 2
    groups = H // KVH
    span = groups * HEAD

    def body(stage):
        normed_o, query_o, key_o, value_o, weights_o, context_o, mixed_o, top_o, bottom_o, gates_o = stage.out
        gains = stage.get(1)
        tokens_ref = stage.get(0)
        rows_in = tokens_ref[...].astype(F32)
        inverse = lax.rsqrt(jnp.mean(rows_in * rows_in, axis=1, keepdims=True) + EPSILON)
        normed = (rows_in * inverse * gains[0:1, :].astype(F32)).astype(BF16)
        normed_o[...] = normed
        stage.put(0)
        cos, sin = stage.get(2)[...], stage.get(3)[...]
        keys = dot(normed, stage.get(4)[...])
        for g in range(KVH):
            at = slice(g * HEAD, (g + 1) * HEAD)
            key_o[:, at] = turned(keys[:, at], cos, sin).astype(BF16)
        value_o[...] = dot(normed, stage.get(5)[...]).astype(BF16)
        stage.put(2, 3)
        lower = lax.broadcasted_iota(jnp.int32, (rows, rows), 0) >= lax.broadcasted_iota(jnp.int32, (rows, rows), 1)
        across = jnp.broadcast_to(stage.get(6)[...].astype(F32), (rows, rows))
        allowed = (across == across.T) & lower
        w_q = stage.get(7)
        for g in range(KVH):
            queries = dot(normed, w_q[:, g * span : (g + 1) * span])
            key = key_o[:, g * HEAD : (g + 1) * HEAD]
            value = value_o[:, g * HEAD : (g + 1) * HEAD]
            for i in range(groups):
                h = g * groups + i
                at = slice(h * HEAD, (h + 1) * HEAD)
                query = turned(queries[:, i * HEAD : (i + 1) * HEAD], cos, sin).astype(BF16)
                query_o[:, at] = query
                for first, last in ((0, half), (half, rows)):
                    scores = dot_nt(query[first:last], key[:last]) * HEAD ** (-0.5)
                    scores = jnp.where(allowed[first:last, :last], scores, NEG_FILL)
                    peak = jnp.max(scores, axis=1, keepdims=True)
                    terms = jnp.exp(scores - peak)
                    low = (terms / jnp.sum(terms, axis=1, keepdims=True)).astype(BF16)
                    weights_o[h * rows + first : h * rows + last, :last] = low
                    context_o[first:last, at] = dot(low, value[:last]).astype(BF16)
                weights_o[h * rows : h * rows + half, half:] = jnp.zeros((half, rows - half), BF16)
        stage.put(1, 4, 5)
        w_o = stage.get(8)
        step = width // 3
        for c in range(0, width, step):
            at = slice(c, c + step)
            mixed_o[:, at] = tokens_ref[:, at].astype(F32) + dot(context_o[...], w_o[:, at])
        stage.put(6)
        mixed = mixed_o[...]
        inverse = lax.rsqrt(jnp.mean(mixed * mixed, axis=1, keepdims=True) + EPSILON)
        moe_in = (mixed * inverse * gains[1:2, :].astype(F32)).astype(BF16)
        routes_ref = stage.get(9)
        logits = dot_nt(stage.get(10)[...], moe_in)
        ids = lax.broadcasted_iota(jnp.int32, (experts, rows), 0)
        hot = ids == routes_ref[0:1, :]
        for k in range(1, routes_ref.shape[0]):
            hot = hot | (ids == routes_ref[k : k + 1, :])
        peak = jnp.max(jnp.where(hot, logits, NEG_FILL), axis=0, keepdims=True)
        terms = jnp.where(hot, jnp.exp(jnp.where(hot, logits - peak, 0.0)), 0.0)
        gates = terms / jnp.sum(terms, axis=0, keepdims=True)
        gates_o[...] = gates
        high = gates.astype(BF16).astype(F32)
        count = jnp.sum(stage.get(11)[...].astype(F32), axis=1, keepdims=True)
        counts = jnp.broadcast_to(count, (experts, width - 2 * rows))
        notes = jnp.concatenate([high, gates - high, counts], axis=1).astype(BF16)
        top_o[...] = moe_in[:half]
        bottom_o[...] = jnp.concatenate([moe_in[half:], notes], axis=0)
        stage.put(7, 8, 9)

    ins = (
        tokens,
        jnp.stack([gain_one, gain_two]),
        *tables,
        w_key,
        w_value,
        segments,
        w_query,
        w_out,
        routes.T,
        router.T,
        valid,
    )
    outs = [
        ((rows, width), BF16),
        ((rows, H * HEAD), BF16),
        ((rows, KVH * HEAD), BF16),
        ((rows, KVH * HEAD), BF16),
        ((H * rows, rows), BF16),
        ((rows, H * HEAD), BF16),
        ((rows, width), F32),
        ((half, width), BF16),
        ((rows - half + experts, width), BF16),
        ((experts, rows), F32),
    ]
    return staged(body, ins, outs, flops=2 * rows * width * (2 * width + 4 * KVH * HEAD))


def mixed_backward(parts, grad_out, mixed, block, gates, router, gain_two):
    rows, width = mixed.shape
    experts = router.shape[1]
    counts = [len(pieces) for pieces in parts]
    n = sum(counts)

    def body(stage, *refs):
        branch_o, mixed_o, gain_o, router_o = stage.out[:4]
        weights = refs[0][...]
        moe_in = joined_rows([refs[5 + i] for i in range(len(block))])
        mixed_rows = refs[3][...]
        inverse = lax.rsqrt(jnp.mean(mixed_rows * mixed_rows, axis=1, keepdims=True) + EPSILON)
        normal = mixed_rows * inverse
        places = iter(range(5 + len(block), 5 + len(block) + n))
        total = 0.0
        for count in counts:
            total = total + joined_rows([refs[next(places)] for _ in range(count)]).astype(F32)
        notes = total[rows : rows + experts]
        grad_gates = notes[:, :rows] + notes[:, rows : 2 * rows]
        chosen = weights * (grad_gates - jnp.sum(weights * grad_gates, axis=0, keepdims=True))
        logits = chosen.astype(BF16)
        router_o[...] = dot(logits, moe_in[:rows])
        grad_in = total[:rows] + dot_tn(logits, refs[1][...])
        gain_o[...] = jnp.sum(grad_in * normal, axis=0, keepdims=True)
        scaled = grad_in * refs[2][...].astype(F32)
        inner = jnp.mean(scaled * normal, axis=1, keepdims=True)
        grad_mixed = refs[4][...] + inverse * (scaled - normal * inner)
        branch_o[...] = grad_mixed.astype(BF16)
        mixed_o[...] = grad_mixed
        send_shares(stage, branch_o, 4)
        stage.put(0, 1, 2, 3)

    ins = (gates, router.T, gain_two[None], mixed, grad_out, *block, *(p for pieces in parts for p in pieces))
    outs = [((rows, width), BF16), ((rows, width), F32), ((1, width), F32), ((experts, width), F32)]
    outs += shares_shape(rows, width)
    made = staged(body, (), outs, kept=ins, limit=LEAN, straight=range(4, len(outs)))
    return made[:4], made[4:]


def attention_backward(branch, weights, query, key, value, tables, w_out):
    rows = branch.shape[0]
    groups = H // KVH
    span = groups * HEAD
    scale = HEAD ** (-0.5)

    def body(stage, key_ref, value_ref, query_ref, low_all, cos_ref, sin_ref):
        qkv_o = stage.out[0]
        grad_branch = stage.get(0)[...]
        for g in range(KVH):
            w_o = stage.get(1 + g)
            grad_context = dot_nt(grad_branch, w_o[...]).astype(BF16)
            k = key_ref[:, g * HEAD : (g + 1) * HEAD]
            v = value_ref[:, g * HEAD : (g + 1) * HEAD]
            grad_key = jnp.zeros((rows, HEAD), F32)
            grad_value = jnp.zeros((rows, HEAD), F32)
            cos, sin = cos_ref[...], -sin_ref[...]
            for i in range(groups):
                h = g * groups + i
                q = query_ref[:, h * HEAD : (h + 1) * HEAD]
                grad = grad_context[:, i * HEAD : (i + 1) * HEAD]
                low = low_all[h * rows : (h + 1) * rows, :]
                grads = dot_nt(grad, v)
                full = low.astype(F32)
                product = full * grads
                scores = (product - full * jnp.sum(product, axis=1, keepdims=True)).astype(BF16)
                grad_query = dot(scores, k) * scale
                qkv_o[:, h * HEAD : (h + 1) * HEAD] = turned(grad_query, cos, sin).astype(BF16)
                grad_key = grad_key + dot_tn(scores, q)
                grad_value = grad_value + dot_tn(low, grad)
            at = (H + g) * HEAD
            qkv_o[:, at : at + HEAD] = turned(grad_key * scale, cos, sin).astype(BF16)
            at += KVH * HEAD
            qkv_o[:, at : at + HEAD] = grad_value.astype(BF16)
        send_shares(stage, qkv_o, 1)
        stage.put(0)

    ins = (branch, (w_out, 0, span), (w_out, span, span))
    columns = (H + 2 * KVH) * HEAD
    outs = [((rows, columns), BF16)] + shares_shape(rows, columns)
    made = staged(
        body, ins, outs, first=2, straight=range(1, len(outs)), limit=LEAN + 4,
        kept=(key, value, query, weights, *tables))
    return made[0], made[1:]


def weight_grads(ring, early, late):
    columns, width = early[0].shape[1], late[0].shape[1]
    share = columns // ring.size
    step = 256

    def body(stage):
        total = stage.room[0]
        early_refs = [stage.get(i) for i in range(0, 2 * len(late), 2)]
        late_refs = [stage.get(i) for i in range(1, 2 * len(late), 2)]
        for c in range(0, columns, step):
            made = 0.0
            for a, b in zip(early_refs, late_refs):
                made = made + dot_tn(a[:, c : c + step], b[...])
            total[c : c + step, :] = made.astype(BF16)
        for j in range(ring.size):
            start = pl.multiple_of(ring.owner(j) * share, 16)
            stage.send(total.at[pl.ds(start, share)], j)

    ins = [p for pair in zip(early, late) for p in pair]
    outs = [((share, width), BF16)] * ring.size
    every = range(len(outs))
    return staged(body, ins, outs, straight=every, held=every, room=[((columns, width), BF16)], limit=LEAN)


def token_backward(qkv, tokens, grad_mixed, gain_one, weights):
    rows, width = tokens.shape
    w_query, w_key, w_value, _ = weights
    at, span = H * HEAD, KVH * HEAD

    def body(stage):
        tokens_o, gain_o = stage.out
        qkv_ref = stage.get(0)
        rows_in = stage.get(1)[...].astype(F32)
        inverse = lax.rsqrt(jnp.mean(rows_in * rows_in, axis=1, keepdims=True) + EPSILON)
        normal = rows_in * inverse
        grads = dot_nt(qkv_ref[:, at : at + span], stage.get(2)[...])
        grads = grads + dot_nt(qkv_ref[:, at + span :], stage.get(3)[...])
        grads = grads + dot_nt(qkv_ref[:, :at], stage.get(4)[...])
        gain_o[...] = jnp.sum(grads * normal, axis=0, keepdims=True)
        scaled = grads * stage.get(5)[...].astype(F32)
        inner = jnp.mean(scaled * normal, axis=1, keepdims=True)
        tokens_o[...] = stage.get(6)[...] + inverse * (scaled - normal * inner)
        stage.put(0, 1)

    ins = (qkv, tokens, w_key, w_value, w_query, gain_one[None], grad_mixed)
    return staged(body, ins, [((rows, width), F32), ((1, width), F32)], limit=LEAN + 10)


def after(value, first):
    return lax.optimization_barrier((value, first))[0]


def rep_pairs(k):
    size = lax.axis_size(("x", "c"))
    return [(i, i ^ k) for i in range(size)]


def x_gather(a):
    size = lax.axis_size("x")
    return [a] + [lax.ppermute(a, "x", [(i, i ^ k) for i in range(size)]) for k in range(1, size)]


def core_gather(blocks):
    return [b for a in blocks for b in (a, lax.ppermute(a, "c", [(0, 1), (1, 0)]))]


def rep_gather(a):
    return core_gather(x_gather(a))


def rep_spread(parts):
    return [lax.ppermute(p, ("x", "c"), rep_pairs(k)) if k else p for k, p in enumerate(parts)]


def rep_parts(a):
    size = lax.axis_size(("x", "c"))
    share = a.shape[1] // size
    return [lax.dynamic_slice_in_dim(a, (rep_index() ^ k) * share, share, 1) for k in range(size)]


def rep_columns(blocks):
    step = 1
    while step < len(blocks):
        swap = (rep_index() & step) != 0
        blocks = [jnp.where(swap, blocks[i ^ step], blocks[i]) for i in range(len(blocks))]
        step *= 2
    return blocks


def columns_of(blocks, start, stop):
    share = blocks[0].shape[1]
    parts = []
    for i, block in enumerate(blocks):
        low, high = max(start - i * share, 0), min(stop - i * share, share)
        if low < high:
            parts.append(block[:, low:high])
    return jnp.concatenate(parts, axis=1).astype(F32)


def shards(
    ring,
    tokens,
    segments,
    routes,
    valid_mask,
    teacher,
    gain_one,
    w_query,
    w_key,
    w_value,
    w_out,
    gain_two,
    router,
    w_gate,
    w_up,
    w_down,
):
    length, width = tokens.shape
    experts_all = router.shape[1]
    tokens_all = length * lax.axis_size(ALL)
    w_gate, w_up, w_down = w_gate[0], w_up[0], w_down[0]
    valid_rows = valid_mask.reshape(length).astype(F32)
    tables = rope_tables(length)
    attn = (w_query, w_key, w_value, w_out)
    normed_low, query, key, value, weights_low, context, mixed_rows, *block, gates = attention_forward(
        tokens, segments, routes, valid_mask, gain_one, gain_two, tables, router, attn
    )
    form = RingExperts if ring.size <= RING_LIMIT else SlotExperts
    experts = form(ring, block, gates, routes.shape[1], w_gate, w_up, w_down)
    gathered = {}

    def gather_beside(step, sent):
        if step == 0:
            gathered["normed"] = x_gather(after(normed_low, sent))
        if step == 2:
            gathered["normed"] = core_gather(after(gathered["normed"], sent))
        return gathered["normed"] if step % 2 else ()

    def beside(step, sent):
        if step == 0:
            gathered["count"] = butterfly_sum(experts.count, ("c", "x"))
        if step == 1:
            gathered["context"] = x_gather(after(context, (sent, gathered["count"])))
        if step == 3:
            gathered["context"] = core_gather(after(gathered["context"], sent))
        return gathered["count"] if step == 1 else ()

    moe_parts = experts.forward(gather_beside, beside)
    if not gathered:
        gathered = {"normed": rep_gather(normed_low), "context": rep_gather(context)}
        gathered["count"] = butterfly_sum(experts.count, ("c", "x"))
    count_total = gathered["count"][0, 0]
    scale = 2.0 * tokens_all / count_total * valid_rows[:, None]

    def gap_rows(parts, mixed, aim):
        rows = mixed + added(parts)
        return rows, rows - aim.astype(F32)

    grad_low = (scale * gap_rows(moe_parts, mixed_rows, teacher)[1]).astype(BF16)
    moe_parts, mixed_again, aim, scale = after((moe_parts, mixed_rows, teacher, scale), grad_low)
    output_rows, residual_gap = gap_rows(moe_parts, mixed_again, aim)
    numerator = jnp.sum(valid_rows * jnp.sum(residual_gap * residual_gap, axis=-1))
    grad_out = scale * residual_gap

    def back_beside(step, sent):
        return (gathered, numerator, grad_out) if step == 1 else ()

    back_parts, sums = experts.backward(grad_low, back_beside)
    (grad_branch, grad_mixed, grad_gain_two, grad_router), branch_parts = mixed_backward(
        after(back_parts, [each.got for each in sums]), grad_out, mixed_rows, block, gates, router, gain_two
    )
    branch_spread = rep_spread(branch_parts or rep_parts(grad_branch))
    grad_qkv, qkv_parts = attention_backward(
        grad_branch, weights_low, query, key, value, tables, w_out
    )
    qkv_spread = rep_spread(qkv_parts or rep_parts(grad_qkv))
    out_sum = RingSum(ring, weight_grads(ring, gathered["context"], after(branch_spread, grad_qkv)))
    grad_tokens, grad_gain_one = token_backward(
        after(grad_qkv, out_sum.sent), tokens, grad_mixed, gain_one, attn
    )
    small = jnp.concatenate([grad_router, grad_gain_two, grad_gain_one, jnp.full((1, width), numerator)], axis=0)
    hops = butterfly_hops(("c", "x", "y", "z"))
    small, got = butterfly_hop(small, hops.pop(0), grad_tokens)
    grad_w_qkv = weight_grads(ring, gathered["normed"], after(qkv_spread, small))
    small = small + after(got, grad_w_qkv[0])
    out_sum.step(grad_w_qkv[0])
    qkv_sum = RingSum(ring, grad_w_qkv)
    out_blocks = None
    while qkv_sum.left > 1:
        if out_sum.left > 1:
            out_sum.step(qkv_sum.sent)
        elif out_blocks is None:
            out_blocks = rep_gather(out_sum.total(qkv_sum.sent))
        if hops:
            small, got = butterfly_hop(small, hops.pop(0), qkv_sum.sent)
            small = small + got
        qkv_sum.step((out_sum.sent, small))
    if out_blocks is None:
        while out_sum.left > 1:
            out_sum.step(qkv_sum.sent)
        out_blocks = rep_gather(out_sum.total(qkv_sum.sent))
    for hop in hops:
        small, got = butterfly_hop(small, hop, qkv_sum.sent)
        small = small + got
    qkv_blocks = rep_gather(qkv_sum.total(small))
    shares = [each.result(qkv_blocks[0])[0] for each in sums]
    out_share = columns_of(rep_columns(after(out_blocks, qkv_blocks[0])), 0, width)
    router_share = small[:experts_all].T
    gain_shares = (small[experts_all + 1], small[experts_all])
    loss_value = small[experts_all + 2, 0] / count_total
    qkv_share = rep_columns(after(qkv_blocks, (shares, out_share, router_share, gain_shares, loss_value)))
    return (
        output_rows.astype(BF16),
        loss_value,
        grad_tokens,
        gain_shares[0],
        columns_of(qkv_share, 0, H * HEAD),
        columns_of(qkv_share, H * HEAD, (H + KVH) * HEAD),
        columns_of(qkv_share, (H + KVH) * HEAD, (H + 2 * KVH) * HEAD),
        out_share,
        gain_shares[1],
        router_share,
        shares[0],
        shares[1],
        shares[2],
    )


def solution(mesh):
    rep, ep = mesh.shape["rep"], mesh.shape["ep"]
    x_size = rep // 2
    y_size = x_size if ep % x_size == 0 else 1
    grid = Mesh(mesh.devices.reshape(x_size, 2, ep // y_size, y_size), ALL)
    rows = P(ALL, None)
    whole = P()
    expert = P(EP, None, None)
    return jax.shard_map(
        functools.partial(shards, Ring(ep // y_size, y_size)),
        mesh=grid,
        in_specs=(rows,) * 5 + (whole,) * 7 + (expert,) * 3,
        out_specs=(rows, whole, rows, whole)
        + (P(EP, None),) * 4
        + (whole, whole)
        + (P(EP, ("x", "c"), None),) * 3,
        check_vma=False,
    )
```
